512 devices in a mesh: sample: 8 (over y_lo, core), row: 8 (over y_hi, x), col: 8 (over z).
Axes of the slice: x: 4, y: 8 (y_hi: 2, y_lo: 4; y = y_hi * 4 + y_lo), z: 8, core: 2. Of those that a mesh axis runs over, the one named last changes fastest.
Arguments:
- images: bfloat16 [8, 192, 192, 256], P('sample', 'row', 'col'), may hold values from -6 to 6
- w_expand: bfloat16 [256, 1024], replicated, may hold values from -0.375 to 0.375
- w_depth: bfloat16 [3, 3, 1024], replicated, may hold values from -2 to 2
- w_short: bfloat16 [256, 512], replicated, may hold values from -0.375 to 0.375
- w_proj: bfloat16 [1024, 512], P('sample'), may hold values from -0.1875 to 0.1875
- w_qkv: bfloat16 [512, 768], P('sample'), may hold values from -0.25 to 0.25
- w_out: bfloat16 [256, 512], P('sample'), may hold values from -0.375 to 0.375
- cotangent: bfloat16 [8, 96, 96, 512], P('sample', 'row', 'col'), may hold values from -6 to 6
Outputs:
- grad_image: bfloat16 [8, 192, 192, 256], P('sample', 'row', 'col')
- grad_expand: float32 [256, 1024], replicated
- grad_depth: float32 [3, 3, 1024], replicated
- grad_short: float32 [256, 512], replicated
- grad_proj: float32 [1024, 512], P('sample')
- grad_qkv: float32 [512, 768], P('sample')
- grad_out: float32 [256, 512], P('sample')
The draws below stay inside these ranges and needn't reach their ends.
All inputs are finite; a program needn't handle non-finite values.
Results may differ from the reference program's by a relative error of at most 0.02.
Values may be sent and summed in bfloat16 or wider, within the bound.
No kernel may reach another device: no remote copies, remote signals or barrier semaphores. Data moves between devices by JAX's collectives and lax.ppermute only.
A program may use at most 64 MiB of HBM per device.

```python
import math
import jax
import jax.numpy as jnp
from jax import lax

GRID = 12
CI = 256
HID = 1024
D = 512
HEADS = 8
A = 256
SAMPLES = 8
HO = 96
WO = 96
HI = 192
WI = 192
N_ROW = 8
N_COL = 8


def block_levels(key, shape, cuts, least, high):
    factor_of, own = 1.0, jax.random.fold_in(key, 6)
    for axis_at, blocks in cuts:
        heights = jnp.exp(jax.random.uniform(jax.random.fold_in(own, axis_at), (blocks,), jnp.float32, least / len(cuts), high / len(cuts)))
        factor_of = factor_of * jnp.repeat(heights, shape[axis_at] // blocks).reshape([-1 if axis == axis_at else 1 for axis in range(len(shape))])
    return factor_of


def gaussian(own_key, shape, scale, most, split=(), held_as=jnp.bfloat16):
    entries = scale * jax.random.normal(own_key, shape, jnp.float32)
    if split:
        entries = entries * block_levels(own_key, shape, split, -0.22, 0.18)
    return jnp.clip(entries, -most, most).astype(held_as)


def setup_inputs(seed: int = 0) -> dict:
    streams_of = jax.random.split(jax.random.key(seed), 9)
    return {
        "images": gaussian(streams_of[0], (SAMPLES, HI, WI, CI), 1.0, 6.0, ((0, 8), (1, 8), (2, 8))),
        "w_expand": gaussian(streams_of[1], (CI, HID), CI ** -0.5, 0.375),
        "w_depth": gaussian(streams_of[2], (3, 3, HID), 9 ** -0.5, 2.0),
        "w_short": gaussian(streams_of[3], (CI, D), CI ** -0.5, 0.375),
        "w_proj": gaussian(streams_of[4], (HID, D), HID ** -0.5, 0.1875, ((0, 8),)),
        "w_qkv": gaussian(streams_of[5], (D, 3 * A), D ** -0.5, 0.25, ((0, 8),)),
        "w_out": gaussian(streams_of[6], (A, D), A ** -0.5, 0.375, ((0, 8),)),
        "cotangent": gaussian(streams_of[7], (SAMPLES, HO, WO, D), 1.0, 6.0, ((0, 8), (1, 8), (2, 8))),
    }


norm_epsilon = 1e-05
tanh_coeff = 0.7978845608028654
cubic_coeff = 0.044715

def gelu_tanh(values):
    return 0.5 * values * (1.0 + jnp.tanh(tanh_coeff * (values + cubic_coeff * values * values * values)))

def gelu_slope(values):
    inner = jnp.tanh(tanh_coeff * (values + cubic_coeff * values * values * values))
    return 0.5 * (1.0 + inner) + 0.5 * values * (1.0 - inner * inner) * tanh_coeff * (1.0 + 3.0 * cubic_coeff * values * values)

def apply_matrix(activations, matrix):
    return lax.dot_general(activations, matrix, (((activations.ndim - 1,), (0,)), ((), ())), preferred_element_type=jnp.float32)

def apply_transpose(activations, matrix):
    return lax.dot_general(activations, matrix, (((activations.ndim - 1,), (1,)), ((), ())), preferred_element_type=jnp.float32)

def outer_sum(left_side, right_side):
    left_flat = left_side.reshape(-1, left_side.shape[-1])
    right_flat = right_side.reshape(-1, right_side.shape[-1])
    return lax.dot_general(left_flat, right_flat, (((0,), (0,)), ((), ())), preferred_element_type=jnp.float32)

def batched(form, left_side, right_side):
    return jnp.einsum(form, left_side.astype(jnp.float32), right_side.astype(jnp.float32))

def depthwise(extended, filters, out_rows, out_cols):
    running = jnp.zeros((extended.shape[0], out_rows, out_cols, extended.shape[3]), jnp.float32)
    for row_tap in range(3):
        for col_tap in range(3):
            window = extended[:, row_tap:row_tap + 2 * out_rows - 1:2, col_tap:col_tap + 2 * out_cols - 1:2, :]
            running = running + window.astype(jnp.float32) * filters[row_tap, col_tap].astype(jnp.float32)
    return running

def depthwise_filter_grad(extended, d_conv):
    out_rows = d_conv.shape[1]
    out_cols = d_conv.shape[2]
    tap_rows = []
    for row_tap in range(3):
        taps = []
        for col_tap in range(3):
            window = extended[:, row_tap:row_tap + 2 * out_rows - 1:2, col_tap:col_tap + 2 * out_cols - 1:2, :]
            taps.append(lax.optimization_barrier(jnp.sum(window.astype(jnp.float32) * d_conv.astype(jnp.float32), axis=(0, 1, 2))))
        tap_rows.append(jnp.stack(taps))
    return jnp.stack(tap_rows)

def depthwise_back(d_conv, filters):
    running = None
    for row_tap in range(3):
        for col_tap in range(3):
            term = d_conv.astype(jnp.float32) * filters[row_tap, col_tap].astype(jnp.float32)
            placed = lax.pad(term, jnp.zeros((), term.dtype), ((0, 0, 0), (row_tap, 2 - row_tap, 1), (col_tap, 2 - col_tap, 1), (0, 0, 0)))
            running = placed if running is None else running + placed
    return running

def pool_cells(images):
    shaped = images.astype(jnp.float32).reshape(images.shape[0], images.shape[1] // 2, 2, images.shape[2] // 2, 2, images.shape[3])
    return lax.optimization_barrier(jnp.mean(shaped, axis=(2, 4))).astype(jnp.bfloat16)

def unpool_cells(d_pooled):
    return jnp.repeat(jnp.repeat(d_pooled, 2, axis=1), 2, axis=2) * 0.25

def layer_norm(section_out):
    widened = section_out.astype(jnp.float32)
    centred = widened - lax.optimization_barrier(jnp.mean(widened, axis=-1, keepdims=True))
    inv_std = lax.rsqrt(lax.optimization_barrier(jnp.mean(centred * centred, axis=-1, keepdims=True)) + norm_epsilon)
    return (centred * inv_std, inv_std)

def layer_norm_back(d_normed, normalized, inv_std):
    return inv_std * (d_normed - lax.optimization_barrier(jnp.mean(d_normed, axis=-1, keepdims=True)) - normalized * lax.optimization_barrier(jnp.mean(d_normed * normalized, axis=-1, keepdims=True)))

def split_heads(grouped, head_count):
    batch, slots, width = grouped.shape
    head_size = width // 3 // head_count
    pieces = grouped.reshape(batch, slots, 3, head_count, head_size)
    return (pieces[:, :, 0], pieces[:, :, 1], pieces[:, :, 2], head_size)

def attend(grouped, key_mask, head_count):
    query_part, key_part, value_part, head_size = split_heads(grouped, head_count)
    scores = batched('bqhd,bkhd->bhqk', query_part, key_part) / math.sqrt(head_size)
    raised = jnp.exp(scores) * key_mask
    weights32 = raised / lax.optimization_barrier(jnp.sum(raised, axis=-1, keepdims=True))
    weights = weights32.astype(jnp.bfloat16)
    mixture = batched('bhqk,bkhd->bqhd', weights, value_part).astype(jnp.bfloat16)
    return (mixture.reshape(grouped.shape[0], grouped.shape[1], -1), weights32, weights)

def attend_back(grouped, weights32, weights, d_mixture, head_count):
    query_part, key_part, value_part, head_size = split_heads(grouped, head_count)
    d_heads = d_mixture.reshape(grouped.shape[0], grouped.shape[1], head_count, head_size)
    d_weights = batched('bqhd,bkhd->bhqk', d_heads, value_part)
    d_values = batched('bhqk,bqhd->bkhd', weights, d_heads)
    d_scores = (weights32 * (d_weights - lax.optimization_barrier(jnp.sum(weights32 * d_weights, axis=-1, keepdims=True)))).astype(jnp.bfloat16)
    d_queries = batched('bhqk,bkhd->bqhd', d_scores, key_part) / math.sqrt(head_size)
    d_keys = batched('bhqk,bqhd->bkhd', d_scores, query_part) / math.sqrt(head_size)
    stacked = jnp.stack([d_queries, d_keys, d_values], axis=2).astype(jnp.bfloat16)
    return stacked.reshape(grouped.shape)

def to_groups(tokens):
    width = tokens.shape[-1]
    shaped = tokens.reshape(GRID, N_ROW, GRID, N_COL, width).transpose(1, 3, 0, 2, 4)
    return shaped.reshape(N_ROW * N_COL, GRID * GRID, width)

def from_groups(grouped):
    width = grouped.shape[-1]
    shaped = grouped.reshape(N_ROW, N_COL, GRID, GRID, width).transpose(2, 0, 3, 1, 4)
    return shaped.reshape(1, GRID * N_ROW, GRID * N_COL, width)

def reference(images, w_expand, w_depth, w_short, w_proj, w_qkv, w_out, cotangent):

    def per_sample(pair):
        image_one = pair[0][None]
        cot_one = pair[1][None]
        pre_act = apply_matrix(image_one, w_expand)
        expanded = gelu_tanh(pre_act).astype(jnp.bfloat16)
        extended = jnp.pad(expanded, ((0, 0), (1, 0), (1, 0), (0, 0)))
        conv_out = depthwise(extended, w_depth, HO, WO)
        activated = gelu_tanh(conv_out).astype(jnp.bfloat16)
        pooled = pool_cells(image_one)
        section_out = (apply_matrix(activated, w_proj) + apply_matrix(pooled, w_short)).astype(jnp.bfloat16)
        normalized, inv_std = layer_norm(section_out)
        normed = normalized.astype(jnp.bfloat16)
        packed = apply_matrix(normed, w_qkv).astype(jnp.bfloat16)
        grouped = to_groups(packed[0])
        key_mask = jnp.ones((GRID * GRID,), jnp.float32)
        mixed_groups, weights32, weights = attend(grouped, key_mask, HEADS)
        mixture = from_groups(mixed_groups)
        g_out = outer_sum(mixture, cot_one)
        d_mixture = apply_transpose(cot_one, w_out).astype(jnp.bfloat16)
        d_grouped = attend_back(grouped, weights32, weights, to_groups(d_mixture[0]), HEADS)
        d_packed = from_groups(d_grouped)
        g_qkv = outer_sum(normed, d_packed)
        d_normed = apply_transpose(d_packed, w_qkv)
        d_section = (cot_one.astype(jnp.float32) + layer_norm_back(d_normed, normalized, inv_std)).astype(jnp.bfloat16)
        g_proj = outer_sum(activated, d_section)
        g_short = outer_sum(pooled, d_section)
        d_activated = apply_transpose(d_section, w_proj)
        d_conv = (d_activated * gelu_slope(conv_out)).astype(jnp.bfloat16)
        g_depth = depthwise_filter_grad(extended, d_conv)
        d_extended = depthwise_back(d_conv, w_depth)
        d_expanded = d_extended[:, 1:, 1:]
        d_pre = (d_expanded * gelu_slope(pre_act)).astype(jnp.bfloat16)
        g_expand = outer_sum(image_one, d_pre)
        d_pooled = apply_transpose(d_section, w_short)
        grad_one = (apply_transpose(d_pre, w_expand) + unpool_cells(d_pooled)).astype(jnp.bfloat16)
        return (grad_one[0], g_expand, g_depth, g_short, g_proj, g_qkv, g_out)
    results = lax.map(per_sample, (images, cotangent))
    grad_scale = 1.0 / math.sqrt(SAMPLES * HO * WO)
    summed = [lax.optimization_barrier(jnp.sum(part, axis=0)) * grad_scale for part in results[1:]]
    return (results[0], summed[0], summed[1], summed[2], summed[3], summed[4], summed[5])
```

```python
import math

import jax
import jax.numpy as jnp
from jax import lax
from jax.sharding import Mesh
from jax.sharding import PartitionSpec as P

HEADS = 8
PARTS = 8

SAMPLE = ("ylo", "core")
ROW = ("yhi", "x")
COL = "z"
GRID_AXES = ("yhi", "x", "z")
CHIPS = ("ylo", "yhi", "x", "z")
RING = ("ylo", "yhi")

norm_epsilon = 1e-05
tanh_coeff = 0.7978845608028654
cubic_coeff = 0.044715

bf16 = jnp.bfloat16
f32 = jnp.float32


def gelu_both(values):
    inner = jnp.tanh(tanh_coeff * (values + cubic_coeff * values * values * values))
    value = 0.5 * values * (1.0 + inner)
    slope = 0.5 * (1.0 + inner) + 0.5 * values * (1.0 - inner * inner) * tanh_coeff * (
        1.0 + 3.0 * cubic_coeff * values * values
    )
    return value, slope


def dot(left, right):
    return lax.dot_general(
        left, right, (((left.ndim - 1,), (0,)), ((), ())), preferred_element_type=f32
    )


def dot_t(left, right):
    return lax.dot_general(
        left, right, (((left.ndim - 1,), (1,)), ((), ())), preferred_element_type=f32
    )


def outer_sum(left, right):
    return lax.dot_general(
        left.reshape(-1, left.shape[-1]),
        right.reshape(-1, right.shape[-1]),
        (((0,), (0,)), ((), ())),
        preferred_element_type=f32,
    )


def step_route(count, distance):
    return [(i - distance, i) for i in range(count) if 0 <= i - distance < count]


def diagonal_route(distance):
    return [
        ((r - distance) * PARTS + c - distance, r * PARTS + c)
        for r in range(PARTS)
        for c in range(PARTS)
        if 0 <= r - distance < PARTS and 0 <= c - distance < PARTS
    ]


def rims(edge_row, edge_col, corner, distance):
    return (
        lax.ppermute(edge_row, ROW, step_route(PARTS, distance)),
        lax.ppermute(edge_col, COL, step_route(PARTS, distance)),
        lax.ppermute(corner, GRID_AXES, diagonal_route(distance)),
    )


def around(distance):
    place = [y % 4 * 2 + y // 4 for y in range(8)]
    return [(place[y], place[(y + distance) % 8]) for y in range(8)]


def swap_cores(block):
    return lax.ppermute(block, "core", [(0, 1), (1, 0)])


def exchange(block, axes):
    return lax.all_to_all(block, axes, 0, 0, tiled=True)


def spread(block, axes, count):
    return exchange(jnp.broadcast_to(block[None], (count,) + block.shape), axes)


def gather_weights(w_proj, w_qkv, w_out):
    flat = jnp.concatenate([w.reshape(-1, 128) for w in (w_proj, w_qkv, w_out)], axis=0)
    core = lax.axis_index("core")
    other = swap_cores(flat)
    pair = jnp.where(core == 0, jnp.stack([flat, other]), jnp.stack([other, flat]))
    below = lax.ppermute(pair, RING, around(1))
    above = lax.ppermute(pair, RING, around(7))
    half = pair.shape[1] // 2
    far_a = lax.ppermute(pair[:, :half], RING, around(2))
    far_b = lax.ppermute(pair[:, half:], RING, around(6))
    far = jnp.concatenate([far_a, far_b], axis=1)
    ring = jnp.stack([pair, above, far, below])
    turned = jnp.take(ring, (jnp.arange(4) - lax.axis_index("ylo")) % 4, axis=0)
    shards = turned.reshape((8,) + flat.shape)
    cuts = [w.size // 128 for w in (w_proj, w_qkv, w_out)]
    proj = shards[:, : cuts[0]].reshape(-1, w_proj.shape[1])
    qkv = shards[:, cuts[0] : cuts[0] + cuts[1]].reshape(-1, w_qkv.shape[1])
    out = shards[:, cuts[0] + cuts[1] :].reshape(-1, w_out.shape[1])
    return proj, qkv, out


def to_units(tokens):
    rows = tokens.shape[0]
    moved = tokens.transpose(2, 0, 1, 3)
    padded = jnp.pad(moved, ((0, 0), (0, 0), (0, 4), (0, 0)))
    quads = padded.reshape(HEADS, rows, 2, 2, 4, 128)
    odd = lax.axis_index("z") % 2 == 1
    quads = jnp.where(odd, quads[:, :, :, ::-1], quads)
    pieces = quads.reshape(HEADS, rows, 2, 8, 128).transpose(0, 3, 1, 2, 4)
    got = exchange(pieces.reshape(64, rows * 2, 128), GRID_AXES)
    got = got.reshape(8, 8, rows, 2, 128).transpose(0, 2, 1, 3, 4)
    got = got.reshape(8 * rows, 4, 2, 2, 128)
    high = lax.axis_index("z") >= 4
    second = jnp.where(high, got[:, :, 1, 1], got[:, :, 0, 1])
    first = got[:, :, :, 0].reshape(8 * rows, 8, 128)
    cols = jnp.concatenate([first, second], axis=1)
    return cols.reshape(12, 8, 12, 128).transpose(1, 0, 2, 3).reshape(8, 144, 128)


def from_units(units):
    rows = 12
    cols = units.reshape(8, 12, 12, 128).transpose(1, 0, 2, 3).reshape(8 * rows, 12, 128)
    first = cols[:, :8].reshape(8 * rows, 4, 2, 128)
    second = jnp.broadcast_to(cols[:, 8:, None], (8 * rows, 4, 2, 128))
    sent = jnp.stack([first, second], axis=3).reshape(8, rows, 8, 2, 128)
    sent = sent.transpose(0, 2, 1, 3, 4).reshape(64, rows * 2, 128)
    got = exchange(sent, GRID_AXES).reshape(HEADS, 8, rows, 2, 128)
    got = got.transpose(0, 2, 3, 1, 4).reshape(HEADS, rows, 2, 2, 4, 128)
    odd = lax.axis_index("z") % 2 == 1
    got = jnp.where(odd, got[:, :, :, ::-1], got).reshape(HEADS, rows, 16, 128)
    return got[:, :, :12].transpose(1, 2, 0, 3)


def attention(units):
    query, key, value, d_mix = (units[..., 32 * i : 32 * i + 32] for i in range(4))
    scale = 1.0 / math.sqrt(32)

    def batched(form, left, right):
        return jnp.einsum(form, left, right, preferred_element_type=f32)

    raised = jnp.exp(batched("uqd,ukd->uqk", query, key) * scale)
    weights32 = raised / jnp.sum(raised, axis=-1, keepdims=True)
    weights = weights32.astype(bf16)
    mixture = batched("uqk,ukd->uqd", weights, value)
    d_weights = batched("uqd,ukd->uqk", d_mix, value)
    d_value = batched("uqk,uqd->ukd", weights, d_mix)
    d_scores = (
        weights32 * (d_weights - jnp.sum(weights32 * d_weights, axis=-1, keepdims=True))
    ).astype(bf16)
    d_query = batched("uqk,ukd->uqd", d_scores, key) * scale
    d_key = batched("uqk,uqd->ukd", d_scores, query) * scale
    return jnp.concatenate([d_query, d_key, d_value, mixture], axis=-1).astype(bf16)


def all_sums(part_proj, part_qkv, part_out, part_expand, part_depth, part_short):
    matrix = jnp.concatenate(
        [part.astype(bf16).reshape(8, -1) for part in (part_proj, part_qkv, part_out)], axis=1
    ).reshape(4, 2, 64, 16, 128)
    rest = jnp.concatenate(
        [part.astype(bf16).reshape(-1, 128) for part in (part_expand, part_depth, part_short)]
    )
    rest_rows = rest.shape[0]
    rest = jnp.pad(rest, ((0, 4096 - rest_rows), (0, 0))).reshape(4, 2, 64, 8, 128)
    both = jnp.concatenate([matrix, rest], axis=3)
    core = lax.axis_index("core")
    mine = jnp.where(core == 0, both[:, 0], both[:, 1])
    theirs = jnp.where(core == 0, both[:, 1], both[:, 0])
    pair = (mine.astype(f32) + swap_cores(theirs).astype(f32)).astype(bf16)
    pieces = exchange(pair.reshape(256, 24, 128), CHIPS)
    grad_scale = 1.0 / math.sqrt(8 * 96 * 96)
    total = (jnp.sum(pieces.astype(f32), axis=0) * grad_scale).astype(bf16)
    near = spread(total, GRID_AXES, 64)
    flat = near[:, :16].reshape(-1).astype(f32)
    sizes = [part.size // 8 for part in (part_proj, part_qkv, part_out)]
    grad_proj = flat[: sizes[0]].reshape(-1, part_proj.shape[1])
    grad_qkv = flat[sizes[0] : sizes[0] + sizes[1]].reshape(-1, part_qkv.shape[1])
    grad_out = flat[sizes[0] + sizes[1] :].reshape(-1, part_out.shape[1])
    mine = near[:, 16:].reshape(512, 128)
    other = swap_cores(mine)
    pair = jnp.where(core == 0, jnp.stack([mine, other]), jnp.stack([other, mine]))
    rest = spread(pair, ("ylo",), 4).reshape(4096, 128).astype(f32)
    cut = part_expand.size // 128
    end = cut + part_depth.size // 128
    return (
        rest[:cut].reshape(part_expand.shape),
        rest[cut:end].reshape(part_depth.shape),
        rest[end:rest_rows].reshape(part_short.shape),
        grad_proj,
        grad_qkv,
        grad_out,
    )


def on_device(images, w_expand, w_depth, w_short, w_proj, w_qkv, w_out, cotangent):
    images = images[0]
    cotangent = cotangent[0]
    top, left, corner = rims(images[-1:], images[:, -1:], images[-1:, -1:], 1)
    proj, qkv, out = gather_weights(w_proj, w_qkv, w_out)

    cells = images.reshape(12, 2, 12, 2, 256)
    top_cells = top.reshape(1, 12, 2, 256)
    left_cells = left.reshape(12, 2, 1, 256)
    planes = {
        (0, 0): cells[:, 0, :, 0],
        (0, 1): jnp.concatenate([left_cells[:, 0], cells[:, 0, :, 1]], axis=1),
        (1, 0): jnp.concatenate([top_cells[:, :, 0], cells[:, 1, :, 0]], axis=0),
        (1, 1): jnp.concatenate(
            [
                jnp.concatenate([corner, top_cells[:, :, 1]], axis=1),
                jnp.concatenate([left_cells[:, 1], cells[:, 1, :, 1]], axis=1),
            ],
            axis=0,
        ),
    }
    expanded, slopes = {}, {}
    for place, plane in planes.items():
        value, slope = gelu_both(dot(plane, w_expand))
        expanded[place] = value.astype(bf16)
        slopes[place] = slope[place[0] :, place[1] :]
    taps = w_depth.astype(f32)

    def window(row_tap, col_tap):
        plane = expanded[(row_tap + 1) % 2, (col_tap + 1) % 2]
        row, col = row_tap // 2, col_tap // 2
        return plane[row : row + 12, col : col + 12].astype(f32)

    conv_out = sum(window(a, b) * taps[a, b] for a in range(3) for b in range(3))
    value, conv_slope = gelu_both(conv_out)
    activated = value.astype(bf16)
    wide = cells.astype(f32)
    pooled = (
        (wide[:, 0, :, 0] + wide[:, 0, :, 1] + wide[:, 1, :, 0] + wide[:, 1, :, 1]) * 0.25
    ).astype(bf16)

    section_out = (dot(activated, proj) + dot(pooled, w_short)).astype(bf16).astype(f32)
    centred = section_out - jnp.mean(section_out, axis=-1, keepdims=True)
    inv_std = lax.rsqrt(jnp.mean(centred * centred, axis=-1, keepdims=True) + norm_epsilon)
    normalized = centred * inv_std
    normed = normalized.astype(bf16)
    packed = dot(normed, qkv).astype(bf16).reshape(12, 12, 3, HEADS, 32)
    d_mixture = dot_t(cotangent, out).astype(bf16).reshape(12, 12, 1, HEADS, 32)
    tokens = jnp.concatenate([packed, d_mixture], axis=2).transpose(0, 1, 3, 2, 4)
    results = from_units(attention(to_units(tokens.reshape(12, 12, HEADS, 128))))
    results = results.reshape(12, 12, HEADS, 4, 32).transpose(0, 1, 3, 2, 4)
    d_packed = results[:, :, :3].reshape(12, 12, 768)
    mixture = results[:, :, 3].reshape(12, 12, 256)

    part_out = outer_sum(mixture, cotangent)
    part_qkv = outer_sum(normed, d_packed)
    d_normed = dot_t(d_packed, qkv)
    d_section = (
        cotangent.astype(f32)
        + inv_std
        * (
            d_normed
            - jnp.mean(d_normed, axis=-1, keepdims=True)
            - normalized * jnp.mean(d_normed * normalized, axis=-1, keepdims=True)
        )
    ).astype(bf16)
    part_proj = outer_sum(activated, d_section)
    part_short = outer_sum(pooled, d_section)
    d_conv = (dot_t(d_section, proj) * conv_slope).astype(bf16)
    below, right, beyond = rims(d_conv[:1], d_conv[:, :1], d_conv[:1, :1], -1)
    d_wide = jnp.concatenate(
        [
            jnp.concatenate([d_conv, right], axis=1),
            jnp.concatenate([below, beyond], axis=1),
        ],
        axis=0,
    ).astype(f32)
    here = d_conv.astype(f32)
    part_depth = jnp.stack(
        [
            jnp.stack([jnp.sum(window(a, b) * here, axis=(0, 1)) for b in range(3)])
            for a in range(3)
        ]
    )
    d_pooled = dot_t(d_section, w_short) * 0.25
    row_terms = {0: ((1, 0),), 1: ((2, 0), (0, 1))}
    part_expand = 0.0
    grads = []
    for row in range(2):
        in_row = []
        for col in range(2):
            d_cells = sum(
                d_wide[i : i + 12, j : j + 12] * taps[a, b]
                for a, i in row_terms[row]
                for b, j in row_terms[col]
            )
            d_pre = (d_cells * slopes[row, col]).astype(bf16)
            part_expand = part_expand + outer_sum(cells[:, row, :, col], d_pre)
            in_row.append((dot_t(d_pre, w_expand) + d_pooled).astype(bf16))
        grads.append(jnp.stack(in_row, axis=2))
    grad_image = jnp.stack(grads, axis=1).reshape(1, 24, 24, 256)
    return (grad_image,) + all_sums(
        part_proj, part_qkv, part_out, part_expand, part_depth, part_short
    )


def solution(mesh):
    fine = Mesh(mesh.devices.reshape(4, 2, 2, 4, 8), ("ylo", "core", "yhi", "x", "z"))
    cells = P(SAMPLE, ROW, COL, None)
    rows = P(SAMPLE, None)
    return jax.shard_map(
        on_device,
        mesh=fine,
        in_specs=(cells, P(), P(), P(), rows, rows, rows, cells),
        out_specs=(cells, P(), P(), P(), rows, rows, rows),
        check_vma=False,
    )
```

```python
import math

import jax
import jax.numpy as jnp
import numpy as np
from jax import lax
from jax.experimental import pallas as pl
from jax.experimental.pallas import tpu as pltpu
from jax.sharding import Mesh
from jax.sharding import PartitionSpec as P

HEADS = 8
PARTS = 8

SAMPLE = ("ylo", "core")
ROW = ("yhi", "x")
COL = "z"
GRID_AXES = ("yhi", "x", "z")
CHIPS = ("ylo", "yhi", "x", "z")
RING = ("ylo", "yhi")

norm_epsilon = 1e-05
tanh_coeff = 0.7978845608028654
cubic_coeff = 0.044715

bf16 = jnp.bfloat16
f32 = jnp.float32


def gelu_both(values):
    inner = jnp.tanh(tanh_coeff * (values + cubic_coeff * values * values * values))
    value = 0.5 * values * (1.0 + inner)
    slope = 0.5 * (1.0 + inner) + 0.5 * values * (1.0 - inner * inner) * tanh_coeff * (
        1.0 + 3.0 * cubic_coeff * values * values
    )
    return value, slope


def dot(left, right):
    return lax.dot_general(
        left, right, (((left.ndim - 1,), (0,)), ((), ())), preferred_element_type=f32
    )


def dot_t(left, right):
    return lax.dot_general(
        left, right, (((left.ndim - 1,), (1,)), ((), ())), preferred_element_type=f32
    )


def dot_tt(left, right):
    return lax.dot_general(left, right, (((0,), (0,)), ((), ())), preferred_element_type=f32)


def outer_sum(left, right):
    return lax.dot_general(
        left.reshape(-1, left.shape[-1]),
        right.reshape(-1, right.shape[-1]),
        (((0,), (0,)), ((), ())),
        preferred_element_type=f32,
    )


def step_route(count, distance):
    return [(i - distance, i) for i in range(count) if 0 <= i - distance < count]


def diagonal_route(distance):
    return [
        ((r - distance) * PARTS + c - distance, r * PARTS + c)
        for r in range(PARTS)
        for c in range(PARTS)
        if 0 <= r - distance < PARTS and 0 <= c - distance < PARTS
    ]


def rims(edge_row, edge_col, corner, distance):
    return (
        lax.ppermute(edge_row, ROW, step_route(PARTS, distance)),
        lax.ppermute(edge_col, COL, step_route(PARTS, distance)),
        lax.ppermute(corner, GRID_AXES, diagonal_route(distance)),
    )


def around(distance):
    place = [y % 4 * 2 + y // 4 for y in range(8)]
    return [(place[y], place[(y + distance) % 8]) for y in range(8)]


def swap_cores(block):
    return lax.ppermute(block, "core", [(0, 1), (1, 0)])


def exchange(block, axes):
    return lax.all_to_all(block, axes, 0, 0, tiled=True)


def spread(block, axes, count):
    return exchange(jnp.broadcast_to(block[None], (count,) + block.shape), axes)


def gather_weights(w_proj, w_qkv, w_out):
    tail = w_qkv[:, 512:]
    own = jnp.concatenate(
        [w_proj, w_qkv[:, :512], w_out, jnp.concatenate([tail[:32], tail[32:]], axis=1)], axis=0
    )
    below = lax.ppermute(own, RING, around(1))
    above = lax.ppermute(own, RING, around(7))
    far = jnp.concatenate(
        [lax.ppermute(own[:128], RING, around(2)), lax.ppermute(own[128:], RING, around(6))]
    )
    ring = jnp.stack([own, above, far, below])
    both = jnp.concatenate([ring, swap_cores(ring)])
    shard = jnp.arange(8)
    side = (shard % 2 + lax.axis_index("core")) % 2
    place = side * 4 + (shard // 2 - lax.axis_index("ylo")) % 4
    shards = jnp.take(both, place, axis=0)
    proj = shards[:, :128].reshape(1024, 512)
    lower = shards[:, 224:]
    tails = jnp.concatenate([lower[:, :, :256], lower[:, :, 256:]], axis=1)
    qkv = jnp.concatenate([shards[:, 128:192], tails], axis=2).reshape(512, 768)
    return proj, qkv, shards[:, 192:224].reshape(256, 512)


def head_order():
    target = np.arange(1024)
    wanted = target // 32 % 4 * 256 + target // 128 * 32 + target % 32
    return jnp.asarray(target[:, None] == wanted[None, :], bf16)


def slot_order():
    target = np.arange(192)
    both = []
    for odd in range(2):
        group = (target // 24 + odd * 4) % 8
        wanted = target // 2 % 12 * 16 + target % 2 * 8 + group
        both.append(target[None, :] == wanted[:, None])
    both = jnp.asarray(np.stack(both), bf16)
    return lax.dynamic_index_in_dim(both, lax.axis_index("z") % 2, 0, keepdims=False)


def row_order():
    target = np.arange(192)
    wanted = target // 2 % 8 * 24 + target // 16 * 2 + target % 2
    return jnp.asarray(target[None, :] == wanted[:, None], bf16)


def dot_kt(left, right):
    return lax.dot_general(left, right, (((1,), (1,)), ((), ())), preferred_element_type=f32)


def attention_kernel(slots_ref, order_ref, valid_ref, out_ref, sorted_ref, result_ref):
    scale = 1.0 / math.sqrt(32)
    order = order_ref[...]
    valid = valid_ref[...] > 0.0
    for part in range(8):
        sorted_ref[part * 192 : part * 192 + 192] = dot(order, slots_ref[part]).astype(bf16)
    for group in range(8):
        blocks = [row * 16 for row in range(96) if row % 8 == group]
        unit = jnp.concatenate([sorted_ref[at : at + 16] for at in blocks], axis=0)
        query, key, value, d_mix = (unit[:, 32 * i : 32 * i + 32] for i in range(4))
        raised = jnp.where(valid, jnp.exp(dot_kt(query, key) * scale), 0.0)
        weights32 = raised / jnp.sum(raised, axis=-1, keepdims=True)
        weights = weights32.astype(bf16)
        mixture = dot(weights, value)
        d_weights = dot_kt(d_mix, value)
        d_value = dot_tt(weights, d_mix)
        d_scores = (
            weights32 * (d_weights - jnp.sum(weights32 * d_weights, axis=-1, keepdims=True))
        ).astype(bf16)
        d_query = dot(d_scores, key) * scale
        d_key = dot_tt(d_scores, query) * scale
        result = jnp.concatenate([d_query, d_key, d_value, mixture], axis=-1).astype(bf16)
        for index, at in enumerate(blocks):
            result_ref[at : at + 16] = result[index * 16 : index * 16 + 16]
    for part in range(8):
        out_ref[part] = dot_tt(order, result_ref[part * 192 : part * 192 + 192]).astype(bf16)


def attention(slots):
    slot = lax.broadcasted_iota(jnp.int32, (1, 192), 1)
    high = (lax.axis_index("z") >= 4).astype(jnp.int32)
    valid = ((slot % 2 == 0) | (slot // 2 % 2 == high)).astype(f32)
    return pl.pallas_call(
        attention_kernel,
        out_shape=jax.ShapeDtypeStruct((8, 192, 128), bf16),
        scratch_shapes=[pltpu.VMEM((1536, 128), bf16), pltpu.VMEM((1536, 128), bf16)],
        cost_estimate=pl.CostEstimate(
            flops=500_000_000, bytes_accessed=1_000_000, transcendentals=300_000
        ),
        name="attention",
    )(slots, row_order(), valid)


def mix_tokens(tokens, heads, slots):
    sorted_tokens = dot(slots, dot(tokens, heads).astype(bf16)).astype(bf16)
    pieces = sorted_tokens.reshape(192, HEADS, 128).transpose(1, 0, 2)
    got = exchange(pieces.reshape(64, 24, 128), GRID_AXES)
    results = attention(got.reshape(8, 192, 128))
    got = exchange(results.reshape(64, 24, 128), GRID_AXES).reshape(HEADS, 192, 128)
    got = got.transpose(1, 0, 2).reshape(192, 1024)
    return dot_t(dot_tt(slots, got).astype(bf16), heads).astype(bf16)


def tiles(part, shards, height):
    rows, columns = part.shape
    cut = part.astype(bf16).reshape(shards, rows // shards // height, height, columns // 128, 128)
    return cut.transpose(0, 1, 3, 2, 4).reshape(shards, -1, height, 128)


def untiled(pieces, rows, columns):
    height = pieces.shape[1]
    cut = pieces.reshape(rows // height, columns // 128, height, 128)
    return cut.transpose(0, 2, 1, 3).reshape(rows, columns).astype(f32)


def add_cores(halves, axis):
    core = lax.axis_index("core")
    mine = lax.dynamic_index_in_dim(halves, core, axis, keepdims=False)
    theirs = lax.dynamic_index_in_dim(halves, 1 - core, axis, keepdims=False)
    return mine, theirs


def paired_sum(mine, theirs):
    pair = (mine.astype(f32) + swap_cores(theirs).astype(f32)).astype(bf16)
    pieces = exchange(pair, CHIPS)
    grad_scale = 1.0 / math.sqrt(8 * 96 * 96)
    return (jnp.sum(pieces.astype(f32), axis=0) * grad_scale).astype(bf16)


def all_sums(part_proj, part_qkv, part_out, part_expand, part_depth, part_short):
    matrix = jnp.concatenate(
        [tiles(part, 8, 16) for part in (part_proj, part_qkv, part_out)], axis=1
    ).reshape(4, 2, 64, 16, 128)
    rest = jnp.concatenate(
        [
            tiles(part_expand, 1, 8)[0],
            tiles(part_short, 1, 8)[0],
            part_depth.astype(bf16).reshape(9, 8, 128),
        ]
    )
    rest = jnp.pad(rest, ((0, 512 - rest.shape[0]), (0, 0), (0, 0))).reshape(2, 256, 8, 128)
    matrix_mine, matrix_theirs = add_cores(matrix, 1)
    rest_mine, rest_theirs = add_cores(rest, 0)
    mine = jnp.concatenate([matrix_mine.reshape(256, 16, 128), rest_mine], axis=1)
    theirs = jnp.concatenate([matrix_theirs.reshape(256, 16, 128), rest_theirs], axis=1)
    near = spread(paired_sum(mine, theirs), GRID_AXES, 64)
    grad_proj = untiled(near[:32, :16], 128, 512)
    grad_qkv = untiled(near[32:56, :16], 64, 768)
    grad_out = untiled(near[56:, :16], 32, 512)
    own = near[:, 16:]
    ring = jnp.stack(
        [own] + [lax.ppermute(own, RING, around(step)) for step in (7, 2, 1)]
    )
    both = jnp.concatenate([ring, swap_cores(ring)])
    shard = jnp.arange(8)
    side = (shard // 4 + lax.axis_index("core")) % 2
    place = side * 4 + (shard % 4 - lax.axis_index("ylo")) % 4
    both = jnp.take(both, place, axis=0).reshape(512, 8, 128)
    grad_expand = untiled(both[:256], 256, 1024)
    grad_short = untiled(both[256:384], 256, 512)
    grad_depth = both[384:393].reshape(3, 3, 1024).astype(f32)
    return grad_expand, grad_depth, grad_short, grad_proj, grad_qkv, grad_out


def slots16(cells, last=None):
    rows, _, width = cells.shape
    if last is None:
        return jnp.pad(cells, ((0, 0), (0, 4), (0, 0)))
    return jnp.concatenate([cells, jnp.zeros((rows, 3, width), cells.dtype), last], axis=1)


def on_device(images, w_expand, w_depth, w_short, w_proj, w_qkv, w_out, cotangent):
    images = images[0]
    cotangent = slots16(cotangent[0])
    proj, qkv, out = gather_weights(w_proj, w_qkv, w_out)
    top, left, corner = rims(images[-1:], images[:, -1:], images[-1:, -1:], 1)
    heads, slots = head_order(), slot_order()
    used = lax.broadcasted_iota(jnp.int32, (1, 16, 1), 1) < 12

    cells = images.reshape(12, 2, 12, 2, 256)
    top_cells = top.reshape(1, 12, 2, 256)
    left_cells = left.reshape(12, 2, 1, 256)
    planes = {
        (0, 0): slots16(cells[:, 0, :, 0]),
        (0, 1): slots16(cells[:, 0, :, 1], left_cells[:, 0]),
        (1, 0): jnp.concatenate([slots16(top_cells[:, :, 0]), slots16(cells[:, 1, :, 0])]),
        (1, 1): jnp.concatenate(
            [
                slots16(top_cells[:, :, 1], corner),
                slots16(cells[:, 1, :, 1], left_cells[:, 1]),
            ]
        ),
    }
    expanded, slopes = {}, {}
    for place, plane in planes.items():
        value, slope = gelu_both(dot(plane, w_expand))
        expanded[place] = value.astype(bf16)
        slopes[place] = slope[place[0] :].astype(bf16)
    taps = w_depth.astype(f32)

    def window(row_tap, odd_col):
        plane = expanded[(row_tap + 1) % 2, odd_col]
        return plane[row_tap // 2 : row_tap // 2 + 12].astype(f32)

    straight = sum(
        window(a, 0) * taps[a, 1] + window(a, 1) * taps[a, 2] for a in range(3)
    )
    moved = sum(window(a, 1) * taps[a, 0] for a in range(3))
    value, conv_slope = gelu_both(straight + jnp.roll(moved, 1, axis=1))
    activated = value.astype(bf16)
    conv_slope = conv_slope.astype(bf16)
    wide = cells.astype(f32)
    pooled = slots16(
        ((wide[:, 0, :, 0] + wide[:, 0, :, 1] + wide[:, 1, :, 0] + wide[:, 1, :, 1]) * 0.25).astype(bf16)
    )

    section_out = (dot(activated, proj) + dot(pooled, w_short)).astype(bf16).astype(f32)
    centred = section_out - jnp.mean(section_out, axis=-1, keepdims=True)
    inv_std = lax.rsqrt(jnp.mean(centred * centred, axis=-1, keepdims=True) + norm_epsilon)
    normalized = centred * inv_std
    normed = jnp.where(used, normalized.astype(bf16), jnp.zeros((), bf16))
    packed = dot(normed, qkv).astype(bf16)
    d_mixture = dot_t(cotangent, out).astype(bf16)
    tokens = jnp.concatenate([packed, d_mixture], axis=-1).reshape(192, 1024)
    results = mix_tokens(tokens, heads, slots)
    results = jnp.where(used, results.reshape(12, 16, 1024), jnp.zeros((), bf16))
    d_packed = results[:, :, :768]
    mixture = results[:, :, 768:]

    part_out = outer_sum(mixture, cotangent)
    part_qkv = outer_sum(normed, d_packed)
    d_normed = dot_t(d_packed, qkv)
    d_section = (
        cotangent.astype(f32)
        + inv_std
        * (
            d_normed
            - jnp.mean(d_normed, axis=-1, keepdims=True)
            - normalized * jnp.mean(d_normed * normalized, axis=-1, keepdims=True)
        )
    ).astype(bf16)
    d_section = jnp.where(used, d_section, jnp.zeros((), bf16))
    d_conv = (dot_t(d_section, proj) * conv_slope.astype(f32)).astype(bf16)
    below, right, beyond = rims(d_conv[:1, :12], d_conv[:, :1], d_conv[:1, :1], -1)
    part_proj = outer_sum(activated, d_section)
    part_short = outer_sum(pooled, d_section)
    here = d_conv.astype(f32)
    back = jnp.roll(here, -1, axis=1)
    part_depth = jnp.stack(
        [
            jnp.stack(
                [
                    jnp.sum(window(a, 1) * back, axis=(0, 1)),
                    jnp.sum(window(a, 0) * here, axis=(0, 1)),
                    jnp.sum(window(a, 1) * here, axis=(0, 1)),
                ]
            )
            for a in range(3)
        ]
    )
    rows = jnp.concatenate([d_conv, slots16(below)], axis=0)
    column = jnp.concatenate([right, beyond], axis=0)
    slot = lax.broadcasted_iota(jnp.int32, (1, 16, 1), 1)
    after = jnp.where(slot == 11, column, jnp.roll(rows, -1, axis=1)).astype(f32)
    rows = rows.astype(f32)
    d_pooled = dot_t(d_section, w_short) * 0.25
    row_terms = {0: ((1, 0),), 1: ((2, 0), (0, 1))}
    col_terms = {0: ((1, rows),), 1: ((2, rows), (0, after))}
    part_expand = 0.0
    grads = []
    for row in range(2):
        in_row = []
        for col in range(2):
            d_cells = sum(
                source[i : i + 12] * taps[a, b]
                for a, i in row_terms[row]
                for b, source in col_terms[col]
            )
            d_pre = (d_cells * slopes[row, col].astype(f32)).astype(bf16)
            d_pre = jnp.where(used, d_pre, jnp.zeros((), bf16))
            part_expand = part_expand + outer_sum(planes[row, col][row:], d_pre)
            in_row.append((dot_t(d_pre, w_expand) + d_pooled).astype(bf16)[:, :12])
        grads.append(jnp.stack(in_row, axis=2))
    grad_image = jnp.stack(grads, axis=1).reshape(1, 24, 24, 256)
    return (grad_image,) + all_sums(
        part_proj, part_qkv, part_out, part_expand, part_depth, part_short
    )


def solution(mesh):
    fine = Mesh(mesh.devices.reshape(4, 2, 2, 4, 8), ("ylo", "core", "yhi", "x", "z"))
    cells = P(SAMPLE, ROW, COL, None)
    rows = P(SAMPLE, None)
    return jax.shard_map(
        on_device,
        mesh=fine,
        in_specs=(cells, P(), P(), P(), rows, rows, rows, cells),
        out_specs=(cells, P(), P(), P(), rows, rows, rows),
        check_vma=False,
    )
```

```python
import math

import jax
import jax.numpy as jnp
import numpy as np
from jax import lax
from jax.experimental import pallas as pl
from jax.experimental.pallas import tpu as pltpu
from jax.sharding import Mesh
from jax.sharding import PartitionSpec as P

HEADS = 8
PARTS = 8

SAMPLE = ("ylo", "core")
ROW = ("yhi", "x")
COL = "z"
GRID_AXES = ("yhi", "x", "z")
CHIPS = ("ylo", "yhi", "x", "z")
RING = ("ylo", "yhi")

norm_epsilon = 1e-05
tanh_coeff = 0.7978845608028654
cubic_coeff = 0.044715

bf16 = jnp.bfloat16
f32 = jnp.float32


def gelu_both(values):
    inner = jnp.tanh(tanh_coeff * (values + cubic_coeff * values * values * values))
    value = 0.5 * values * (1.0 + inner)
    slope = 0.5 * (1.0 + inner) + 0.5 * values * (1.0 - inner * inner) * tanh_coeff * (
        1.0 + 3.0 * cubic_coeff * values * values
    )
    return value, slope


def dot(left, right):
    return lax.dot_general(
        left, right, (((left.ndim - 1,), (0,)), ((), ())), preferred_element_type=f32
    )


def dot_t(left, right):
    return lax.dot_general(
        left, right, (((left.ndim - 1,), (1,)), ((), ())), preferred_element_type=f32
    )


def dot_tt(left, right):
    return lax.dot_general(left, right, (((0,), (0,)), ((), ())), preferred_element_type=f32)


def outer_sum(left, right):
    return lax.dot_general(
        left.reshape(-1, left.shape[-1]),
        right.reshape(-1, right.shape[-1]),
        (((0,), (0,)), ((), ())),
        preferred_element_type=f32,
    )


def step_route(count, distance):
    return [(i - distance, i) for i in range(count) if 0 <= i - distance < count]


def row_rim(edge, distance):
    return lax.ppermute(edge, ROW, step_route(PARTS, distance))


def col_rim(edge, distance):
    return lax.ppermute(edge, COL, step_route(PARTS, distance))


def around(distance):
    place = [y % 4 * 2 + y // 4 for y in range(8)]
    return [(place[y], place[(y + distance) % 8]) for y in range(8)]


def swap_cores(block):
    return lax.ppermute(block, "core", [(0, 1), (1, 0)])


def exchange(block, axes):
    return lax.all_to_all(block, axes, 0, 0, tiled=True)


def spread(block, axes, count):
    return exchange(jnp.broadcast_to(block[None], (count,) + block.shape), axes)


def gather_weights(w_proj, w_qkv, w_out):
    tail = w_qkv[:, 512:]
    own = jnp.concatenate(
        [w_proj, w_qkv[:, :512], w_out, jnp.concatenate([tail[:32], tail[32:]], axis=1)], axis=0
    )
    below = lax.ppermute(own, RING, around(1))
    above = lax.ppermute(own, RING, around(7))
    far = lax.ppermute(own, RING, around(2))
    ring = jnp.stack([own, above, far, below])
    return ring, swap_cores(ring)


def head_order():
    target = np.arange(1024)
    wanted = target // 32 % 4 * 256 + target // 128 * 32 + target % 32
    return jnp.asarray(target[:, None] == wanted[None, :], bf16)


def slot_order():
    target = np.arange(192)
    both = []
    for odd in range(2):
        group = (target // 24 + odd * 4) % 8
        wanted = target // 2 % 12 * 16 + target % 2 * 8 + group
        both.append(target[None, :] == wanted[:, None])
    both = jnp.asarray(np.stack(both), bf16)
    return lax.dynamic_index_in_dim(both, lax.axis_index("z") % 2, 0, keepdims=False)


def row_order():
    target = np.arange(192)
    wanted = target // 2 % 8 * 24 + target // 16 * 2 + target % 2
    return jnp.asarray(target[None, :] == wanted[:, None], bf16)


def dot_kt(left, right):
    return lax.dot_general(left, right, (((1,), (1,)), ((), ())), preferred_element_type=f32)


def attention_kernel(slots_ref, order_ref, valid_ref, out_ref, sorted_ref, result_ref):
    scale = 1.0 / math.sqrt(32)
    order = order_ref[...]
    valid = valid_ref[...] > 0.0
    for part in range(8):
        sorted_ref[part * 192 : part * 192 + 192] = dot(order, slots_ref[part]).astype(bf16)
    for group in range(8):
        blocks = [row * 16 for row in range(96) if row % 8 == group]
        unit = jnp.concatenate([sorted_ref[at : at + 16] for at in blocks], axis=0)
        query, key, value, d_mix = (unit[:, 32 * i : 32 * i + 32] for i in range(4))
        raised = jnp.where(valid, jnp.exp(dot_kt(query, key) * scale), 0.0)
        weights32 = raised / jnp.sum(raised, axis=-1, keepdims=True)
        weights = weights32.astype(bf16)
        mixture = dot(weights, value)
        d_weights = dot_kt(d_mix, value)
        d_value = dot_tt(weights, d_mix)
        d_scores = (
            weights32 * (d_weights - jnp.sum(weights32 * d_weights, axis=-1, keepdims=True))
        ).astype(bf16)
        d_query = dot(d_scores, key) * scale
        d_key = dot_tt(d_scores, query) * scale
        result = jnp.concatenate([d_query, d_key, d_value, mixture], axis=-1).astype(bf16)
        for index, at in enumerate(blocks):
            result_ref[at : at + 16] = result[index * 16 : index * 16 + 16]
    for part in range(8):
        out_ref[part] = dot_tt(order, result_ref[part * 192 : part * 192 + 192]).astype(bf16)


def attention(slots):
    slot = lax.broadcasted_iota(jnp.int32, (1, 192), 1)
    high = (lax.axis_index("z") >= 4).astype(jnp.int32)
    valid = ((slot % 2 == 0) | (slot // 2 % 2 == high)).astype(f32)
    return pl.pallas_call(
        attention_kernel,
        out_shape=jax.ShapeDtypeStruct((8, 192, 128), bf16),
        scratch_shapes=[pltpu.VMEM((1536, 128), bf16), pltpu.VMEM((1536, 128), bf16)],
        cost_estimate=pl.CostEstimate(
            flops=500_000_000, bytes_accessed=1_000_000, transcendentals=300_000
        ),
        name="attention",
    )(slots, row_order(), valid)


def token_mask():
    return lax.broadcasted_iota(jnp.int32, (192, 1), 0) % 16 < 12


def normalize(section):
    wide = section.astype(f32)
    centred = wide - jnp.mean(wide, axis=-1, keepdims=True)
    inv_std = lax.rsqrt(jnp.mean(centred * centred, axis=-1, keepdims=True) + norm_epsilon)
    return centred * inv_std, inv_std


def call(body, name, out_shape, flops, scratch=(), **rest):
    return pl.pallas_call(
        body,
        out_shape=out_shape,
        scratch_shapes=scratch,
        compiler_params=pltpu.CompilerParams(vmem_limit_bytes=40 * 1024 * 1024),
        cost_estimate=pl.CostEstimate(flops=flops, bytes_accessed=8_000_000, transcendentals=0),
        name=name,
        **rest,
    )


def section_kernel(
    spot_ref, ring_ref, other_ref, activated_ref, pooled_ref, short_ref, cotangent_ref, heads_ref,
    slots_ref, pieces_ref, section_ref, normed_ref, proj_ref, qkv_ref, out_ref,
):
    core, y_lo = spot_ref[0], spot_ref[1]

    def place(shard, source, at):
        proj_ref[shard * 128 : shard * 128 + 128] = source[at, 0:128]
        qkv_ref[shard * 64 : shard * 64 + 64, 0:512] = source[at, 128:192]
        out_ref[shard * 32 : shard * 32 + 32] = source[at, 192:224]
        qkv_ref[shard * 64 : shard * 64 + 32, 512:768] = source[at, 224:256, 0:256]
        qkv_ref[shard * 64 + 32 : shard * 64 + 64, 512:768] = source[at, 224:256, 256:512]

    for shard in range(8):
        at = lax.rem(shard // 2 - y_lo + 4, 4)
        pl.when(core == shard % 2)(lambda: place(shard, ring_ref, at))
        pl.when(core != shard % 2)(lambda: place(shard, other_ref, at))
    section = (
        dot(activated_ref[...], proj_ref[...]) + dot(pooled_ref[...], short_ref[...])
    ).astype(bf16)
    section_ref[...] = section
    normed = jnp.where(token_mask(), normalize(section)[0], 0.0).astype(bf16)
    normed_ref[...] = normed
    packed = dot(normed, qkv_ref[...]).astype(bf16)
    d_mixture = dot_kt(cotangent_ref[...], out_ref[...]).astype(bf16)
    tokens = jnp.concatenate([packed, d_mixture], axis=1)
    tokens = dot(slots_ref[...], dot(tokens, heads_ref[...]).astype(bf16)).astype(bf16)
    for head in range(HEADS):
        pieces_ref[head] = tokens[:, head * 128 : head * 128 + 128]


def section_step(spot, ring, other, activated, pooled, w_short, cotangent, heads, slots):
    shapes = [(8, 192, 128), (192, 512), (192, 512), (1024, 512), (512, 768), (256, 512)]
    return call(
        section_kernel,
        "section",
        [jax.ShapeDtypeStruct(shape, bf16) for shape in shapes],
        1_500_000_000,
        in_specs=[pl.BlockSpec(memory_space=pltpu.SMEM)]
        + [pl.BlockSpec(memory_space=pltpu.VMEM)] * 8,
    )(spot, ring, other, activated, pooled, w_short, cotangent, heads, slots)[:5]


def back_kernel(
    got_ref, heads_ref, slots_ref, section_ref, cotangent_ref, proj_ref, qkv_ref, slope_ref,
    results_ref, d_section_ref, d_conv_ref,
):
    used = token_mask()
    got = jnp.concatenate([got_ref[head] for head in range(HEADS)], axis=1)
    results = dot_kt(dot_tt(slots_ref[...], got).astype(bf16), heads_ref[...])
    results = jnp.where(used, results, 0.0).astype(bf16)
    results_ref[...] = results
    normalized, inv_std = normalize(section_ref[...])
    d_normed = dot_kt(results[:, :768], qkv_ref[...])
    d_section = cotangent_ref[...].astype(f32) + inv_std * (
        d_normed
        - jnp.mean(d_normed, axis=-1, keepdims=True)
        - normalized * jnp.mean(d_normed * normalized, axis=-1, keepdims=True)
    )
    d_section = jnp.where(used, d_section, 0.0).astype(bf16)
    d_section_ref[...] = d_section
    d_activated = dot_kt(d_section, proj_ref[...])
    d_conv_ref[...] = (d_activated * slope_ref[...].astype(f32)).astype(bf16)


def back_step(*inputs):
    shapes = [(192, 1024), (192, 512), (192, 1024)]
    return call(
        back_kernel,
        "back",
        [jax.ShapeDtypeStruct(shape, bf16) for shape in shapes],
        1_200_000_000,
    )(*inputs)


def parts_kernel(
    results_ref, d_section_ref, normed_ref, cotangent_ref, activated_ref, pooled_ref, short_ref,
    matrix_ref, rest_ref, d_pooled_ref,
):
    results = results_ref[...]
    d_section = d_section_ref[...]

    def store(part, first, rows):
        lanes = part.shape[1] // 128
        for shard in range(8):
            for piece in range(rows // 16 * lanes):
                row = shard * rows + piece // lanes * 16
                lane = piece % lanes * 128
                index = first + piece
                at = shard // 2 * 32 + index % 2 * 16
                matrix_ref[shard % 2, index // 2, at : at + 16, :] = part[
                    row : row + 16, lane : lane + 128
                ]

    store(dot_tt(activated_ref[...], d_section).astype(bf16), 0, 128)
    store(dot_tt(normed_ref[...], results[:, :768]).astype(bf16), 32, 64)
    store(dot_tt(results[:, 768:], cotangent_ref[...]).astype(bf16), 56, 32)
    short = dot_tt(pooled_ref[...], d_section)
    rows = [short[:, lane * 128 : lane * 128 + 128].reshape(16, 2, 8, 128) for lane in range(4)]
    rest_ref[...] = jnp.concatenate(
        [rows[index % 4][:, index // 4] for index in range(8)], axis=1
    ).astype(bf16)
    d_pooled_ref[...] = dot_kt(d_section, short_ref[...]) * 0.25


def parts_step(*inputs):
    return call(
        parts_kernel,
        "parts",
        [
            jax.ShapeDtypeStruct((2, 32, 128, 128), bf16),
            jax.ShapeDtypeStruct((16, 64, 128), bf16),
            jax.ShapeDtypeStruct((192, 256), f32),
        ],
        600_000_000,
    )(*inputs)


def pixel_kernel(
    d_conv_ref, below_ref, right_ref, even_ref, odd_ref, slopes_ref, cells_ref, w_expand_ref,
    taps_ref, d_pooled_ref, image_ref, expand_ref, depth_ref, total_ref,
):
    step = pl.program_id(0)
    slot = lax.broadcasted_iota(jnp.int32, (1, 16, 1), 1)
    here = d_conv_ref[...].astype(f32).reshape(12, 16, 256)
    rows = jnp.concatenate([here, below_ref[...].astype(f32)], axis=0)
    turned = pltpu.roll(rows, 15, 1)
    after = jnp.where(slot == 11, right_ref[...].astype(f32), turned)
    back = turned[:12]
    taps = [[taps_ref[3 * a + b : 3 * a + b + 1, :].astype(f32) for b in range(3)] for a in range(3)]

    def window(row_tap, odd_col):
        source = even_ref if row_tap == 1 else odd_ref
        first = 16 * (row_tap // 2) if row_tap != 1 else 0
        return source[odd_col, first : first + 192, :].astype(f32).reshape(12, 16, 256)

    for a in range(3):
        odd = window(a, 1)
        even = window(a, 0)
        for b, product in ((0, odd * back), (1, even * here), (2, odd * here)):
            total = jnp.sum(jnp.sum(product, axis=0), axis=0, keepdims=True)
            depth_ref[3 * a + b : 3 * a + b + 1, :] = total
    row_terms = {0: ((1, 0),), 1: ((2, 0), (0, 1))}
    col_terms = {0: ((1, rows),), 1: ((2, rows), (0, after))}
    part_expand = 0.0
    for row in range(2):
        for col in range(2):
            d_cells = sum(
                source[i : i + 12] * taps[a][b]
                for a, i in row_terms[row]
                for b, source in col_terms[col]
            )
            d_cells = jnp.where(slot < 12, d_cells, 0.0).reshape(192, 256)
            plane = row * 2 + col
            d_pre = (d_cells * slopes_ref[plane].astype(f32)).astype(bf16)
            part_expand = part_expand + dot_tt(cells_ref[plane], d_pre)
            back_image = dot_kt(d_pre, w_expand_ref[...])

            @pl.when(step == 0)
            def _():
                total_ref[plane] = back_image + d_pooled_ref[...]

            @pl.when(step > 0)
            def _():
                total_ref[plane] += back_image

    expand_ref[...] = jnp.concatenate(
        [part_expand[:, :128].reshape(32, 8, 128), part_expand[:, 128:].reshape(32, 8, 128)],
        axis=1,
    ).astype(bf16)

    @pl.when(step == pl.num_programs(0) - 1)
    def _():
        image_ref[...] = total_ref[...].astype(bf16)


def pixel_step(*inputs):
    def chunk(*lead):
        return pl.BlockSpec(lead + (256,), lambda step: (0,) * len(lead) + (step,))

    def whole(*shape):
        return pl.BlockSpec(shape, lambda step: (0,) * len(shape))

    return call(
        pixel_kernel,
        "pixel",
        [
            jax.ShapeDtypeStruct((4, 192, 256), bf16),
            jax.ShapeDtypeStruct((32, 64, 128), bf16),
            jax.ShapeDtypeStruct((16, 1024), f32),
        ],
        1_200_000_000,
        scratch=[pltpu.VMEM((4, 192, 256), f32)],
        grid=(4,),
        in_specs=[
            chunk(192), chunk(1, 16), chunk(13, 1), chunk(2, 192), chunk(2, 208), chunk(4, 192),
            whole(4, 192, 256), chunk(256), chunk(16), whole(192, 256),
        ],
        out_specs=[
            whole(4, 192, 256),
            pl.BlockSpec((32, 16, 128), lambda step: (0, step, 0)),
            chunk(16),
        ],
    )(*inputs)


def untiled(pieces, rows, columns):
    height = pieces.shape[1]
    cut = pieces.reshape(rows // height, columns // 128, height, 128)
    return cut.transpose(0, 2, 1, 3).reshape(rows, columns).astype(f32)


def add_cores(halves, axis):
    core = lax.axis_index("core")
    mine = lax.dynamic_index_in_dim(halves, core, axis, keepdims=False)
    theirs = lax.dynamic_index_in_dim(halves, 1 - core, axis, keepdims=False)
    return mine, theirs


def all_sums(matrix, short, expand, depth):
    depth = depth[:9].astype(bf16).reshape(9, 8, 128)
    depth = jnp.pad(depth, ((0, 119), (0, 0), (0, 0))).reshape(16, 64, 128)
    short = jnp.concatenate([short, depth], axis=0)
    first = lax.axis_index("core") == 0
    mine, theirs = add_cores(matrix, 0)
    mine = jnp.concatenate([mine, jnp.where(first, expand, short)], axis=1)
    theirs = jnp.concatenate([theirs, jnp.where(first, short, expand)], axis=1)
    pair = (mine.astype(f32) + swap_cores(theirs).astype(f32)).astype(bf16)
    line = jnp.sum(exchange(pair, "x").reshape(4, 8, 192, 128).astype(f32), axis=0).astype(bf16)
    sheet = jnp.sum(exchange(line, "z").astype(f32), axis=0).astype(bf16)
    column = jnp.concatenate(
        [sheet[:128].reshape(4, 32, 128), jnp.broadcast_to(sheet[None, 128:], (4, 64, 128))], axis=1
    )
    column = jnp.broadcast_to(column[:, None], (4, 2, 96, 128)).reshape(8, 96, 128)
    grad_scale = 1.0 / math.sqrt(8 * 96 * 96)
    total = jnp.sum(exchange(column, RING).astype(f32), axis=0) * grad_scale
    near = spread(total.astype(bf16), ("x", "z"), 32)
    own = near[:, 32:].reshape(256, 8, 128)
    other = swap_cores(own)
    matrix = near[:, :32].reshape(64, 16, 128)
    grad_proj = untiled(matrix[:32], 128, 512)
    grad_qkv = untiled(matrix[32:56], 64, 768)
    grad_out = untiled(matrix[56:], 32, 512)
    low = jnp.where(first, own, other)
    high = jnp.where(first, other, own)
    grad_expand = untiled(low, 256, 1024)
    grad_short = untiled(high[:128], 256, 512)
    grad_depth = high[128:137].reshape(3, 3, 1024).astype(f32)
    return grad_expand, grad_depth, grad_short, grad_proj, grad_qkv, grad_out


def slots16(cells, last=None):
    rows, _, width = cells.shape
    if last is None:
        return jnp.pad(cells, ((0, 0), (0, 4), (0, 0)))
    return jnp.concatenate([cells, jnp.zeros((rows, 3, width), cells.dtype), last], axis=1)


def on_device(images, w_expand, w_depth, w_short, w_proj, w_qkv, w_out, cotangent):
    images = images[0]
    cotangent = slots16(cotangent[0])
    ring, other = gather_weights(w_proj, w_qkv, w_out)
    top = row_rim(images[-1:], 1)
    left = col_rim(jnp.concatenate([top[:, -1:], images[:, -1:]], axis=0), 1)
    heads, slots = head_order(), slot_order()
    used = lax.broadcasted_iota(jnp.int32, (1, 16, 1), 1) < 12

    cells = images.reshape(12, 2, 12, 2, 256)
    top_cells = top.reshape(1, 12, 2, 256)
    corner = left[:1]
    left_cells = left[1:].reshape(12, 2, 1, 256)
    planes = {
        (0, 0): slots16(cells[:, 0, :, 0]),
        (0, 1): slots16(cells[:, 0, :, 1], left_cells[:, 0]),
        (1, 0): jnp.concatenate([slots16(top_cells[:, :, 0]), slots16(cells[:, 1, :, 0])]),
        (1, 1): jnp.concatenate(
            [
                slots16(top_cells[:, :, 1], corner),
                slots16(cells[:, 1, :, 1], left_cells[:, 1]),
            ]
        ),
    }
    expanded, slopes = {}, {}
    for place, plane in planes.items():
        value, slope = gelu_both(dot(plane, w_expand))
        expanded[place] = value.astype(bf16)
        slopes[place] = slope[place[0] :].astype(bf16)
    taps = w_depth.astype(f32)

    def window(row_tap, odd_col):
        plane = expanded[(row_tap + 1) % 2, odd_col]
        return plane[row_tap // 2 : row_tap // 2 + 12].astype(f32)

    straight = sum(
        window(a, 0) * taps[a, 1] + window(a, 1) * taps[a, 2] for a in range(3)
    )
    moved = sum(window(a, 1) * taps[a, 0] for a in range(3))
    value, conv_slope = gelu_both(straight + jnp.roll(moved, 1, axis=1))
    activated = value.astype(bf16)
    conv_slope = conv_slope.astype(bf16)
    wide = cells.astype(f32)
    pooled = slots16(
        ((wide[:, 0, :, 0] + wide[:, 0, :, 1] + wide[:, 1, :, 0] + wide[:, 1, :, 1]) * 0.25).astype(bf16)
    )

    cotangent = cotangent.reshape(192, 512)
    activated = activated.reshape(192, 1024)
    pooled = pooled.reshape(192, 256)
    spot = jnp.stack([lax.axis_index("core"), lax.axis_index("ylo")]).astype(jnp.int32)
    pieces, section_out, normed, proj, qkv = section_step(
        spot, ring, other, activated, pooled, w_short, cotangent, heads, slots
    )
    got = exchange(pieces.reshape(64, 24, 128), GRID_AXES)
    mixed = attention(got.reshape(8, 192, 128))
    got = exchange(mixed.reshape(64, 24, 128), GRID_AXES).reshape(HEADS, 192, 128)
    results, d_section, d_conv = back_step(
        got, heads, slots, section_out, cotangent, proj, qkv, conv_slope.reshape(192, 1024)
    )
    below = row_rim(d_conv[:12].reshape(1, 12, 1024), -1)
    edge = d_conv.reshape(12, 16, 1024)[:, :1]
    right = col_rim(jnp.concatenate([edge, below[:, :1]], axis=0), -1)
    matrix, short, d_pooled = parts_step(
        results, d_section, normed, cotangent, activated, pooled, w_short
    )
    even = jnp.stack([expanded[0, 0], expanded[0, 1]]).reshape(2, 192, 1024)
    odd = jnp.stack([expanded[1, 0], expanded[1, 1]]).reshape(2, 208, 1024)
    order = [(row, col) for row in range(2) for col in range(2)]
    slope_planes = jnp.stack([slopes[place] for place in order]).reshape(4, 192, 1024)
    cell_planes = jnp.stack([planes[place][place[0] :] for place in order]).reshape(4, 192, 256)
    taps16 = jnp.pad(w_depth.reshape(9, 1024), ((0, 7), (0, 0)))
    image, expand, depth = pixel_step(
        d_conv, slots16(below), right, even, odd, slope_planes, cell_planes, w_expand, taps16,
        d_pooled,
    )
    image = image.reshape(2, 2, 12, 16, 256)[:, :, :, :12]
    grad_image = image.transpose(2, 0, 3, 1, 4).reshape(1, 24, 24, 256)
    return (grad_image,) + all_sums(matrix, short, expand, depth)


def solution(mesh):
    fine = Mesh(mesh.devices.reshape(4, 2, 2, 4, 8), ("ylo", "core", "yhi", "x", "z"))
    cells = P(SAMPLE, ROW, COL, None)
    rows = P(SAMPLE, None)
    return jax.shard_map(
        on_device,
        mesh=fine,
        in_specs=(cells, P(), P(), P(), rows, rows, rows, cells),
        out_specs=(cells, P(), P(), P(), rows, rows, rows),
        check_vma=False,
    )
```

```python
import math

import jax
import jax.numpy as jnp
import numpy as np
from jax import lax
from jax.experimental import pallas as pl
from jax.experimental.pallas import tpu as pltpu
from jax.sharding import Mesh
from jax.sharding import PartitionSpec as P

HEADS = 8
PARTS = 8

SAMPLE = ("ylo", "core")
ROW = ("yhi", "x")
COL = "z"
GRID_AXES = ("yhi", "x", "z")
CHIPS = ("ylo", "yhi", "x", "z")
RING = ("ylo", "yhi")

norm_epsilon = 1e-05
tanh_coeff = 0.7978845608028654
cubic_coeff = 0.044715

bf16 = jnp.bfloat16
f32 = jnp.float32


def gelu_both(values):
    inner = jnp.tanh(tanh_coeff * (values + cubic_coeff * values * values * values))
    value = 0.5 * values * (1.0 + inner)
    slope = 0.5 * (1.0 + inner) + 0.5 * values * (1.0 - inner * inner) * tanh_coeff * (
        1.0 + 3.0 * cubic_coeff * values * values
    )
    return value, slope


def dot(left, right):
    return lax.dot_general(
        left, right, (((left.ndim - 1,), (0,)), ((), ())), preferred_element_type=f32
    )


def dot_t(left, right):
    return lax.dot_general(
        left, right, (((left.ndim - 1,), (1,)), ((), ())), preferred_element_type=f32
    )


def dot_tt(left, right):
    return lax.dot_general(left, right, (((0,), (0,)), ((), ())), preferred_element_type=f32)


def outer_sum(left, right):
    return lax.dot_general(
        left.reshape(-1, left.shape[-1]),
        right.reshape(-1, right.shape[-1]),
        (((0,), (0,)), ((), ())),
        preferred_element_type=f32,
    )


def step_route(count, distance):
    return [(i - distance, i) for i in range(count) if 0 <= i - distance < count]


def row_rim(edge, distance):
    return lax.ppermute(edge, ROW, step_route(PARTS, distance))


def col_rim(edge, distance):
    return lax.ppermute(edge, COL, step_route(PARTS, distance))


def diagonal_rim(edge, distance):
    route = [
        ((r - distance) * PARTS + c - distance, r * PARTS + c)
        for r in range(PARTS)
        for c in range(PARTS)
        if 0 <= r - distance < PARTS and 0 <= c - distance < PARTS
    ]
    return lax.ppermute(edge, GRID_AXES, route)


def around(distance):
    place = [y % 4 * 2 + y // 4 for y in range(8)]
    return [(place[y], place[(y + distance) % 8]) for y in range(8)]


def swap_cores(block):
    return lax.ppermute(block, "core", [(0, 1), (1, 0)])


def exchange(block, axes):
    return lax.all_to_all(block, axes, 0, 0, tiled=True)


def spread(block, axes, count):
    return exchange(jnp.broadcast_to(block[None], (count,) + block.shape), axes)


def first_transfers(images, w_proj, w_qkv, w_out):
    tail = w_qkv[:, 512:]
    own = jnp.concatenate(
        [w_proj, w_qkv[:, :512], w_out, jnp.concatenate([tail[:32], tail[32:]], axis=1)], axis=0
    )
    top = row_rim(images[-1:], 1)
    below = lax.ppermute(own, RING, around(1))
    above = lax.ppermute(own, RING, around(7))
    own, top = lax.optimization_barrier((own, top))
    left = col_rim(jnp.concatenate([top[:, -1:], images[:, -1:]], axis=0), 1)
    far = jnp.concatenate(
        [lax.ppermute(own[:128], RING, around(2)), lax.ppermute(own[128:], RING, around(6))]
    )
    ring = jnp.stack([own, above, far, below])
    ring, left = lax.optimization_barrier((ring, left))
    return top, left, ring, swap_cores(ring)


def slot_order():
    target = np.arange(192)
    both = []
    for odd in range(2):
        group = (target // 24 + odd * 4) % 8
        wanted = target // 2 % 12 * 16 + target % 2 * 8 + group
        both.append(target[None, :] == wanted[:, None])
    both = jnp.asarray(np.stack(both), bf16)
    return lax.dynamic_index_in_dim(both, lax.axis_index("z") % 2, 0, keepdims=False)


def row_order():
    target = np.arange(192)
    wanted = target // 2 % 8 * 24 + target // 16 * 2 + target % 2
    return jnp.asarray(target[None, :] == wanted[:, None], bf16)


def dot_kt(left, right):
    return lax.dot_general(left, right, (((1,), (1,)), ((), ())), preferred_element_type=f32)


def attention_kernel(slots_ref, order_ref, valid_ref, out_ref, sorted_ref, result_ref):
    scale = 1.0 / math.sqrt(32)
    order = order_ref[...]
    valid = valid_ref[...] > 0.0
    for part in range(8):
        sorted_ref[part * 192 : part * 192 + 192] = dot(order, slots_ref[part]).astype(bf16)
    for group in range(8):
        blocks = [row * 16 for row in range(96) if row % 8 == group]
        unit = jnp.concatenate([sorted_ref[at : at + 16] for at in blocks], axis=0)
        query, key, value, d_mix = (unit[:, 32 * i : 32 * i + 32] for i in range(4))
        raised = jnp.where(valid, jnp.exp(dot_kt(query, key) * scale), 0.0)
        weights32 = raised / jnp.sum(raised, axis=-1, keepdims=True)
        weights = weights32.astype(bf16)
        mixture = dot(weights, value)
        d_weights = dot_kt(d_mix, value)
        d_value = dot_tt(weights, d_mix)
        d_scores = (
            weights32 * (d_weights - jnp.sum(weights32 * d_weights, axis=-1, keepdims=True))
        ).astype(bf16)
        d_query = dot(d_scores, key) * scale
        d_key = dot_tt(d_scores, query) * scale
        result = jnp.concatenate([d_query, d_key, d_value, mixture], axis=-1).astype(bf16)
        for index, at in enumerate(blocks):
            result_ref[at : at + 16] = result[index * 16 : index * 16 + 16]
    for part in range(8):
        out_ref[part] = dot_tt(order, result_ref[part * 192 : part * 192 + 192]).astype(bf16)


def attention(slots):
    slot = lax.broadcasted_iota(jnp.int32, (1, 192), 1)
    high = (lax.axis_index("z") >= 4).astype(jnp.int32)
    valid = ((slot % 2 == 0) | (slot // 2 % 2 == high)).astype(f32)
    return pl.pallas_call(
        attention_kernel,
        out_shape=jax.ShapeDtypeStruct((8, 192, 128), bf16),
        scratch_shapes=[pltpu.VMEM((1536, 128), bf16), pltpu.VMEM((1536, 128), bf16)],
        cost_estimate=pl.CostEstimate(
            flops=7_000_000_000, bytes_accessed=1_000_000, transcendentals=300_000
        ),
        name="attention",
    )(slots, row_order(), valid)


def token_mask():
    return lax.broadcasted_iota(jnp.int32, (192, 1), 0) % 16 < 12


def normalize(section):
    wide = section.astype(f32)
    centred = wide - jnp.mean(wide, axis=-1, keepdims=True)
    inv_std = lax.rsqrt(jnp.mean(centred * centred, axis=-1, keepdims=True) + norm_epsilon)
    return centred * inv_std, inv_std


def call(body, name, out_shape, flops, scratch=(), **rest):
    return pl.pallas_call(
        body,
        out_shape=out_shape,
        scratch_shapes=scratch,
        compiler_params=pltpu.CompilerParams(vmem_limit_bytes=24 * 1024 * 1024),
        cost_estimate=pl.CostEstimate(flops=flops, bytes_accessed=8_000_000, transcendentals=0),
        name=name,
        **rest,
    )


def held(shape, dtype=bf16):
    return pltpu.HBM(shape, dtype)


def expand_kernel(
    images_ref, top_ref, left_ref, w_expand_ref, taps_ref,
    even_ref, odd_ref, slopes_ref, activated_ref, conv_slope_ref, cells_ref, pooled_ref,
    wide_ref, top_wide_ref, left_wide_ref, plane_ref, rows_ref,
):
    @pl.when(pl.program_id(0) == 0)
    def _():
        slot = lax.broadcasted_iota(jnp.int32, (1, 16, 1), 1)
        for half in range(2):
            lanes = slice(128 * half, 128 * half + 128)
            wide_ref[half] = images_ref[:, :, lanes].astype(f32)
            top_wide_ref[half] = top_ref[:, :, lanes].astype(f32)
        left_wide_ref[...] = left_ref[...].astype(f32)
        pooled = 0.0
        for row in range(2):
            for col in range(2):
                plane = 2 * row + col
                plane_ref[...] = jnp.zeros((13, 16, 256), f32)
                for half in range(2):
                    lanes = slice(128 * half, 128 * half + 128)
                    plane_ref[row : row + 12, 0:12, lanes] = wide_ref[
                        half, pl.ds(row, 12, stride=2), pl.ds(col, 12, stride=2), :
                    ]
                    if row:
                        plane_ref[0:1, 0:12, lanes] = top_wide_ref[
                            half, :, pl.ds(col, 12, stride=2), :
                        ]
                if col:
                    plane_ref[row : row + 12, 15:16, :] = left_wide_ref[1:25].reshape(
                        12, 2, 1, 256
                    )[:, row]
                if row and col:
                    plane_ref[0:1, 15:16, :] = left_wide_ref[0:1]
                cells = plane_ref[...]
                rows_ref[plane] = cells.astype(bf16).reshape(208, 256)
                cells = cells[row : row + 12]
                cells_ref[plane] = cells.astype(bf16).reshape(192, 256)
                pooled = pooled + cells
        pooled = jnp.where(slot < 12, pooled * 0.25, 0.0)
        pooled_ref[...] = pooled.astype(bf16).reshape(192, 256)

    taps = [[taps_ref[3 * a + b : 3 * a + b + 1, :].astype(f32) for b in range(3)] for a in range(3)]
    expanded = {}
    for row in range(2):
        for col in range(2):
            count = 192 + 16 * row
            value, slope = gelu_both(dot(rows_ref[2 * row + col, 0:count], w_expand_ref[...]))
            value = value.astype(bf16)
            (odd_ref if row else even_ref)[col] = value
            slopes_ref[2 * row + col] = slope[16 * row :].astype(bf16)
            expanded[row, col] = value.astype(f32).reshape(12 + row, 16, 256)

    def window(row_tap, odd_col):
        plane = expanded[(row_tap + 1) % 2, odd_col]
        return plane[row_tap // 2 : row_tap // 2 + 12]

    straight = sum(
        window(a, 0) * taps[a][1] + window(a, 1) * taps[a][2] for a in range(3)
    )
    moved = sum(window(a, 1) * taps[a][0] for a in range(3))
    value, slope = gelu_both(straight + pltpu.roll(moved, 1, 1))
    activated_ref[...] = value.astype(bf16).reshape(192, 256)
    conv_slope_ref[...] = slope.astype(bf16).reshape(192, 256)


def expand_step(*inputs):
    def chunk(*lead):
        return pl.BlockSpec(lead + (256,), lambda step: (0,) * len(lead) + (step,))

    def whole(*shape):
        return pl.BlockSpec(shape, lambda step: (0,) * len(shape))

    shapes = [
        (2, 192, 1024), (2, 208, 1024), (4, 192, 1024), (192, 1024), (192, 1024), (4, 192, 256),
        (192, 256),
    ]
    return call(
        expand_kernel,
        "expand",
        [held(shape) for shape in shapes],
        6_000_000_000,
        scratch=[
            pltpu.VMEM((2, 24, 24, 128), f32),
            pltpu.VMEM((2, 1, 24, 128), f32),
            pltpu.VMEM((25, 1, 256), f32),
            pltpu.VMEM((13, 16, 256), f32),
            pltpu.VMEM((4, 208, 256), bf16),
        ],
        grid=(4,),
        in_specs=[whole(24, 24, 256), whole(1, 24, 256), whole(25, 1, 256), chunk(256), chunk(16)],
        out_specs=[
            chunk(2, 192), chunk(2, 208), chunk(4, 192), chunk(192), chunk(192),
            whole(4, 192, 256), whole(192, 256),
        ],
    )(*inputs)


def row_buffers():
    return [
        pltpu.VMEM((192, 1024), bf16),
        pltpu.VMEM((192, 256), bf16),
        pltpu.VMEM((192, 512), bf16),
        pltpu.SemaphoreType.DMA((3,)),
    ]


def section_kernel(
    spot_ref, ring_ref, other_ref, activated_in, pooled_in, short_ref, cotangent_in, slots_ref,
    pieces_ref, section_ref, normed_ref, proj_ref, qkv_ref, out_ref,
    activated_ref, pooled_ref, cotangent_ref, sems,
):
    core, y_lo = spot_ref[0], spot_ref[1]
    copies = [
        pltpu.make_async_copy(activated_in, activated_ref, sems.at[0]),
        pltpu.make_async_copy(pooled_in, pooled_ref, sems.at[1]),
        pltpu.make_async_copy(cotangent_in, cotangent_ref, sems.at[2]),
    ]
    for copy in copies:
        copy.start()

    def place(shard, source, at):
        proj_ref[shard * 128 : shard * 128 + 128] = source[at, 0:128]
        qkv_ref[shard * 64 : shard * 64 + 64, 0:512] = source[at, 128:192]
        out_ref[shard * 32 : shard * 32 + 32] = source[at, 192:224]
        qkv_ref[shard * 64 : shard * 64 + 32, 512:768] = source[at, 224:256, 0:256]
        qkv_ref[shard * 64 + 32 : shard * 64 + 64, 512:768] = source[at, 224:256, 256:512]

    for shard in range(8):
        at = lax.rem(shard // 2 - y_lo + 4, 4)
        pl.when(core == shard % 2)(lambda: place(shard, ring_ref, at))
        pl.when(core != shard % 2)(lambda: place(shard, other_ref, at))
    for copy in copies:
        copy.wait()
    section = (
        dot(activated_ref[...], proj_ref[...]) + dot(pooled_ref[...], short_ref[...])
    ).astype(bf16)
    section_ref[...] = section
    normed = jnp.where(token_mask(), normalize(section)[0], 0.0).astype(bf16)
    normed_ref[...] = normed
    packed = dot(normed, qkv_ref[...]).astype(bf16)
    d_mixture = dot_kt(cotangent_ref[...], out_ref[...]).astype(bf16)
    tokens = jnp.concatenate([packed, d_mixture], axis=1)
    tokens = dot(slots_ref[...], tokens).astype(bf16)
    for head in range(HEADS):
        at = [part * 256 + head * 32 for part in range(4)]
        pieces_ref[head] = jnp.concatenate([tokens[:, i : i + 32] for i in at], axis=1)


def in_place(array):
    return pltpu.with_memory_space_constraint(array, pltpu.HBM)


def section_step(spot, ring, other, activated, pooled, w_short, cotangent, slots):
    inputs = (spot, ring, other, in_place(activated), in_place(pooled), w_short, in_place(cotangent), slots)
    shapes = [(8, 192, 128), (192, 512), (192, 512), (1024, 512), (512, 768), (256, 512)]
    return call(
        section_kernel,
        "section",
        [held(shape) for shape in shapes],
        4_000_000_000,
        scratch=row_buffers(),
        in_specs=[
            pl.BlockSpec(memory_space=space)
            for space in (
                pltpu.SMEM, pltpu.VMEM, pltpu.VMEM, pltpu.HBM, pltpu.HBM, pltpu.VMEM, pltpu.HBM,
                pltpu.VMEM,
            )
        ],
    )(*inputs)[:5]


def back_kernel(
    got_ref, slots_ref, section_ref, cotangent_ref, proj_in, qkv_in, slope_in,
    results_ref, d_section_ref, d_conv_ref, proj_ref, qkv_ref, slope_ref, sems,
):
    copies = [
        pltpu.make_async_copy(qkv_in, qkv_ref, sems.at[0]),
        pltpu.make_async_copy(proj_in, proj_ref, sems.at[1]),
        pltpu.make_async_copy(slope_in, slope_ref, sems.at[2]),
    ]
    for copy in copies:
        copy.start()
    used = token_mask()
    got = [got_ref[head] for head in range(HEADS)]
    got = jnp.concatenate(
        [got[head][:, 32 * part : 32 * part + 32] for part in range(4) for head in range(HEADS)],
        axis=1,
    )
    results = dot_tt(slots_ref[...], got)
    results = jnp.where(used, results, 0.0).astype(bf16)
    results_ref[...] = results
    normalized, inv_std = normalize(section_ref[...])
    copies[0].wait()
    d_normed = dot_kt(results[:, :768], qkv_ref[...])
    d_section = cotangent_ref[...].astype(f32) + inv_std * (
        d_normed
        - jnp.mean(d_normed, axis=-1, keepdims=True)
        - normalized * jnp.mean(d_normed * normalized, axis=-1, keepdims=True)
    )
    d_section = jnp.where(used, d_section, 0.0).astype(bf16)
    d_section_ref[...] = d_section
    copies[1].wait()
    copies[2].wait()
    d_activated = dot_kt(d_section, proj_ref[...])
    d_conv_ref[...] = (d_activated * slope_ref[...].astype(f32)).astype(bf16)


def back_step(got, slots, section, cotangent, proj, qkv, slope):
    shapes = [(192, 1024), (192, 512), (192, 1024)]
    return call(
        back_kernel,
        "back",
        [jax.ShapeDtypeStruct(shape, bf16) for shape in shapes],
        1_500_000_000,
        scratch=[
            pltpu.VMEM((1024, 512), bf16),
            pltpu.VMEM((512, 768), bf16),
            pltpu.VMEM((192, 1024), bf16),
            pltpu.SemaphoreType.DMA((3,)),
        ],
        in_specs=[pl.BlockSpec(memory_space=pltpu.VMEM)] * 4
        + [pl.BlockSpec(memory_space=pltpu.HBM)] * 3,
    )(got, slots, section, cotangent, in_place(proj), in_place(qkv), in_place(slope))


def parts_kernel(
    results_ref, d_section_ref, normed_ref, cotangent_in, activated_in, pooled_in, short_ref,
    early_ref, d_pooled_ref, activated_ref, pooled_ref, cotangent_ref, sems,
):
    copies = [
        pltpu.make_async_copy(activated_in, activated_ref, sems.at[0]),
        pltpu.make_async_copy(pooled_in, pooled_ref, sems.at[1]),
        pltpu.make_async_copy(cotangent_in, cotangent_ref, sems.at[2]),
    ]
    for copy in copies:
        copy.start()
    results = results_ref[...]
    d_section = d_section_ref[...]

    def store(part, first, rows):
        lanes = part.shape[1] // 128
        for shard in range(8):
            for piece in range(rows // 16 * lanes):
                row = shard * rows + piece // lanes * 16
                lane = piece % lanes * 128
                index = first + piece
                at = shard // 2 * 32 + index % 2 * 16
                early_ref[shard % 2, index // 2, at : at + 16, :] = part[
                    row : row + 16, lane : lane + 128
                ]

    store(dot_tt(normed_ref[...], results[:, :768]).astype(bf16), 32, 64)
    for copy in copies:
        copy.wait()
    store(dot_tt(activated_ref[...], d_section).astype(bf16), 0, 128)
    store(dot_tt(results[:, 768:], cotangent_ref[...]).astype(bf16), 56, 32)
    short = dot_tt(pooled_ref[...], d_section)
    rows = [short[:, lane * 128 : lane * 128 + 128].reshape(32, 8, 128) for lane in range(4)]
    for core in range(2):
        early_ref[core, :, 128:144, :] = jnp.concatenate(
            [rows[2 * core], rows[2 * core + 1]], axis=1
        ).astype(bf16)
    d_pooled_ref[...] = dot_kt(d_section, short_ref[...]) * 0.25


def parts_step(results, d_section, normed, cotangent, activated, pooled, w_short):
    inputs = (results, d_section, normed, in_place(cotangent), in_place(activated), in_place(pooled), w_short)
    return call(
        parts_kernel,
        "parts",
        [
            jax.ShapeDtypeStruct((2, 32, 144, 128), bf16),
            jax.ShapeDtypeStruct((192, 256), f32),
        ],
        1_000_000_000,
        scratch=row_buffers(),
        in_specs=[
            pl.BlockSpec(memory_space=space)
            for space in (
                pltpu.VMEM, pltpu.VMEM, pltpu.VMEM, pltpu.HBM, pltpu.HBM, pltpu.HBM, pltpu.VMEM,
            )
        ],
    )(*inputs)


def pixel_kernel(
    d_conv_ref, below_ref, right_ref, even_ref, odd_ref, slopes_ref, cells_ref, w_expand_ref,
    taps_ref, d_pooled_ref, image_ref, expand_ref, depth_ref, total_ref,
):
    step = pl.program_id(0)
    slot = lax.broadcasted_iota(jnp.int32, (1, 16, 1), 1)
    here = d_conv_ref[...].astype(f32).reshape(12, 16, 256)
    rows = jnp.concatenate([here, below_ref[...].astype(f32)], axis=0)
    turned = pltpu.roll(rows, 15, 1)
    after = jnp.where(slot == 11, right_ref[...].astype(f32), turned)
    back = turned[:12]
    taps = [[taps_ref[3 * a + b : 3 * a + b + 1, :].astype(f32) for b in range(3)] for a in range(3)]

    def window(row_tap, odd_col):
        source = even_ref if row_tap == 1 else odd_ref
        first = 16 * (row_tap // 2) if row_tap != 1 else 0
        return source[odd_col, first : first + 192, :].astype(f32).reshape(12, 16, 256)

    for a in range(3):
        odd = window(a, 1)
        even = window(a, 0)
        for b, product in ((0, odd * back), (1, even * here), (2, odd * here)):
            total = jnp.sum(jnp.sum(product, axis=0), axis=0, keepdims=True)
            depth_ref[3 * a + b : 3 * a + b + 1, :] = total
    row_terms = {0: ((1, 0),), 1: ((2, 0), (0, 1))}
    col_terms = {0: ((1, rows),), 1: ((2, rows), (0, after))}
    part_expand = 0.0
    for row in range(2):
        for col in range(2):
            d_cells = sum(
                source[i : i + 12] * taps[a][b]
                for a, i in row_terms[row]
                for b, source in col_terms[col]
            )
            d_cells = jnp.where(slot < 12, d_cells, 0.0).reshape(192, 256)
            plane = row * 2 + col
            d_pre = (d_cells * slopes_ref[plane].astype(f32)).astype(bf16)
            part_expand = part_expand + dot_tt(cells_ref[plane], d_pre)
            back_image = dot_kt(d_pre, w_expand_ref[...])

            @pl.when(step == 0)
            def _():
                total_ref[plane] = back_image + d_pooled_ref[...]

            @pl.when(step > 0)
            def _():
                total_ref[plane] += back_image

    expand_ref[0] = jnp.concatenate(
        [part_expand[:, :128].reshape(32, 8, 128), part_expand[:, 128:].reshape(32, 8, 128)],
        axis=1,
    ).astype(bf16)

    @pl.when(step == pl.num_programs(0) - 1)
    def _():
        image_ref[...] = total_ref[...].astype(bf16)


def pixel_step(*inputs):
    def chunk(*lead):
        return pl.BlockSpec(lead + (256,), lambda step: (0,) * len(lead) + (step,))

    def whole(*shape):
        return pl.BlockSpec(shape, lambda step: (0,) * len(shape))

    return call(
        pixel_kernel,
        "pixel",
        [
            jax.ShapeDtypeStruct((4, 192, 256), bf16),
            jax.ShapeDtypeStruct((2, 32, 32, 128), bf16),
            jax.ShapeDtypeStruct((16, 1024), f32),
        ],
        6_000_000_000,
        scratch=[pltpu.VMEM((4, 192, 256), f32)],
        grid=(4,),
        in_specs=[
            chunk(192), chunk(1, 16), chunk(13, 1), chunk(2, 192), chunk(2, 208), chunk(4, 192),
            whole(4, 192, 256), chunk(256), chunk(16), whole(192, 256),
        ],
        out_specs=[
            whole(4, 192, 256),
            pl.BlockSpec((1, 32, 16, 128), lambda step: (step // 2, 0, step % 2, 0)),
            chunk(16),
        ],
    )(*inputs)


def untiled(pieces, rows, columns):
    height = pieces.shape[1]
    cut = pieces.reshape(rows // height, columns // 128, height, 128)
    return cut.transpose(0, 2, 1, 3).reshape(rows, columns).astype(f32)


def pair_sum(halves):
    core = lax.axis_index("core")
    mine = lax.dynamic_index_in_dim(halves, core, 0, keepdims=False)
    theirs = lax.dynamic_index_in_dim(halves, 1 - core, 0, keepdims=False)
    return (mine.astype(f32) + swap_cores(theirs).astype(f32)).astype(bf16)


def all_sums(early, expand, depth):
    depth = jnp.pad(depth[:9].astype(bf16).reshape(9, 8, 128), ((0, 23), (0, 0), (0, 0)))
    core = lax.axis_index("core")

    def share(of):
        own = lax.dynamic_index_in_dim(expand, of, 0, keepdims=False)
        return jnp.concatenate([own, jnp.where(of == 0, depth, jnp.zeros((), bf16))], axis=1)

    late = (share(core).astype(f32) + swap_cores(share(1 - core)).astype(f32)).astype(bf16)
    pair = jnp.concatenate([early, late], axis=1)
    line = jnp.sum(exchange(pair, "x").reshape(4, 8, 184, 128).astype(f32), axis=0).astype(bf16)
    sheet = jnp.sum(exchange(line, "z").astype(f32), axis=0).astype(bf16)
    column = jnp.concatenate(
        [sheet[:128].reshape(4, 32, 128), jnp.broadcast_to(sheet[None, 128:], (4, 56, 128))], axis=1
    )
    column = jnp.broadcast_to(column[:, None], (4, 2, 88, 128)).reshape(8, 88, 128)
    grad_scale = 1.0 / math.sqrt(8 * 96 * 96)
    total = jnp.sum(exchange(column, RING).astype(f32), axis=0) * grad_scale
    near = spread(total.astype(bf16), ("x", "z"), 32)
    own = near[:, 32:]
    other = swap_cores(own)
    matrix = near[:, :32].reshape(64, 16, 128)
    grad_proj = untiled(matrix[:32], 128, 512)
    grad_qkv = untiled(matrix[32:56], 64, 768)
    grad_out = untiled(matrix[56:], 32, 512)
    first = lax.axis_index("core") == 0
    both = jnp.where(first, jnp.stack([own, other]), jnp.stack([other, own]))

    def joined(start, count):
        part = both[:, :, start : start + 8 * count].reshape(2, 32, count, 8, 128)
        return part.transpose(1, 3, 0, 2, 4).reshape(256, 256 * count).astype(f32)

    grad_short = joined(0, 2)
    grad_expand = joined(16, 4)
    grad_depth = both[0, :9, 48:].reshape(3, 3, 1024).astype(f32)
    return grad_expand, grad_depth, grad_short, grad_proj, grad_qkv, grad_out


def slots16(cells):
    return jnp.pad(cells, ((0, 0), (0, 4), (0, 0)))


def on_device(images, w_expand, w_depth, w_short, w_proj, w_qkv, w_out, cotangent):
    images = images[0]
    cotangent = slots16(cotangent[0])
    top, left, ring, other = first_transfers(images, w_proj, w_qkv, w_out)
    slots = slot_order()
    taps16 = jnp.pad(w_depth.reshape(9, 1024), ((0, 7), (0, 0)))
    even, odd, slopes, activated, conv_slope, cells, pooled = expand_step(
        images, top, left, w_expand, taps16
    )
    cotangent = cotangent.reshape(192, 512)
    spot = jnp.stack([lax.axis_index("core"), lax.axis_index("ylo")]).astype(jnp.int32)
    pieces, section_out, normed, proj, qkv = section_step(
        spot, ring, other, activated, pooled, w_short, cotangent, slots
    )
    got = exchange(pieces.reshape(64, 24, 128), GRID_AXES)
    mixed = attention(got.reshape(8, 192, 128))
    got = exchange(mixed.reshape(64, 24, 128), GRID_AXES).reshape(HEADS, 192, 128)
    results, d_section, d_conv = back_step(
        got, slots, section_out, cotangent, proj, qkv, conv_slope
    )
    below = row_rim(d_conv[:12].reshape(1, 12, 1024), -1)
    edge = d_conv.reshape(12, 16, 1024)[:, :1]
    right = jnp.concatenate([col_rim(edge, -1), diagonal_rim(edge[:1], -1)], axis=0)
    early, d_pooled = parts_step(
        results, d_section, normed, cotangent, activated, pooled, w_short
    )
    early = pair_sum(early)
    image, expand, depth = pixel_step(
        d_conv, slots16(below), right, even, odd, slopes, cells, w_expand, taps16,
        d_pooled,
    )
    image = image.reshape(2, 2, 12, 16, 256)[:, :, :, :12]
    grad_image = image.transpose(2, 0, 3, 1, 4).reshape(1, 24, 24, 256)
    return (grad_image,) + all_sums(early, expand, depth)


def solution(mesh):
    fine = Mesh(mesh.devices.reshape(4, 2, 2, 4, 8), ("ylo", "core", "yhi", "x", "z"))
    cells = P(SAMPLE, ROW, COL, None)
    rows = P(SAMPLE, None)
    return jax.shard_map(
        on_device,
        mesh=fine,
        in_specs=(cells, P(), P(), P(), rows, rows, rows, cells),
        out_specs=(cells, P(), P(), P(), rows, rows, rows),
        check_vma=False,
    )
```

```python
import math

import jax
import jax.numpy as jnp
import numpy as np
from jax import lax
from jax.experimental import pallas as pl
from jax.experimental.pallas import tpu as pltpu
from jax.sharding import Mesh
from jax.sharding import PartitionSpec as P

HEADS = 8
PARTS = 8

SAMPLE = ("ylo", "core")
ROW = ("yhi", "x")
COL = "z"
GRID_AXES = ("yhi", "x", "z")
CHIPS = ("ylo", "yhi", "x", "z")
RING = ("ylo", "yhi")

norm_epsilon = 1e-05
tanh_coeff = 0.7978845608028654
cubic_coeff = 0.044715

bf16 = jnp.bfloat16
f32 = jnp.float32


def gelu_both(values):
    square = values * values
    inner = jnp.tanh(values * (tanh_coeff * cubic_coeff * square + tanh_coeff))
    half = 0.5 * inner + 0.5
    value = values * half
    slope = half + value * (1.0 - inner) * (3.0 * tanh_coeff * cubic_coeff * square + tanh_coeff)
    return value, slope


def dot(left, right):
    return lax.dot_general(
        left, right, (((left.ndim - 1,), (0,)), ((), ())), preferred_element_type=f32
    )


def dot_t(left, right):
    return lax.dot_general(
        left, right, (((left.ndim - 1,), (1,)), ((), ())), preferred_element_type=f32
    )


def dot_tt(left, right):
    return lax.dot_general(left, right, (((0,), (0,)), ((), ())), preferred_element_type=f32)


def outer_sum(left, right):
    return lax.dot_general(
        left.reshape(-1, left.shape[-1]),
        right.reshape(-1, right.shape[-1]),
        (((0,), (0,)), ((), ())),
        preferred_element_type=f32,
    )


def step_route(count, distance):
    return [(i - distance, i) for i in range(count) if 0 <= i - distance < count]


def row_rim(edge, distance):
    return lax.ppermute(edge, ROW, step_route(PARTS, distance))


def col_rim(edge, distance):
    return lax.ppermute(edge, COL, step_route(PARTS, distance))


def diagonal_rim(edge, distance):
    route = [
        ((r - distance) * PARTS + c - distance, r * PARTS + c)
        for r in range(PARTS)
        for c in range(PARTS)
        if 0 <= r - distance < PARTS and 0 <= c - distance < PARTS
    ]
    return lax.ppermute(edge, GRID_AXES, route)


def around(distance):
    place = [y % 4 * 2 + y // 4 for y in range(8)]
    return [(place[y], place[(y + distance) % 8]) for y in range(8)]


def swap_cores(block):
    return lax.ppermute(block, "core", [(0, 1), (1, 0)])


def exchange(block, axes):
    return lax.all_to_all(block, axes, 0, 0, tiled=True)


def spread(block, axes, count):
    return exchange(jnp.broadcast_to(block[None], (count,) + block.shape), axes)


def call(body, name, out_shape, flops, scratch=(), **rest):
    return pl.pallas_call(
        body,
        out_shape=out_shape,
        scratch_shapes=scratch,
        compiler_params=pltpu.CompilerParams(vmem_limit_bytes=24 * 1024 * 1024),
        cost_estimate=pl.CostEstimate(flops=flops, bytes_accessed=8_000_000, transcendentals=0),
        name=name,
        **rest,
    )


def in_place(array):
    return pltpu.with_memory_space_constraint(array, pltpu.HBM)


def shard_kernel(proj_ref, qkv_ref, out_ref, own_ref, sems):
    moves = [
        (proj_ref, own_ref.at[0:128]),
        (qkv_ref.at[:, 0:512], own_ref.at[128:192]),
        (out_ref, own_ref.at[192:224]),
        (qkv_ref.at[0:32, 512:768], own_ref.at[224:256, 0:256]),
        (qkv_ref.at[32:64, 512:768], own_ref.at[224:256, 256:512]),
    ]
    copies = [
        pltpu.make_async_copy(source, target, sems.at[index])
        for index, (source, target) in enumerate(moves)
    ]
    for copy in copies:
        copy.start()
    for copy in copies:
        copy.wait()


def first_transfers(images, w_proj, w_qkv, w_out):
    own = call(
        shard_kernel,
        "shard",
        jax.ShapeDtypeStruct((256, 512), bf16),
        1_000_000,
        scratch=[pltpu.SemaphoreType.DMA((5,))],
        in_specs=[pl.BlockSpec(memory_space=pltpu.HBM)] * 3,
    )(in_place(w_proj), in_place(w_qkv), in_place(w_out))
    top = row_rim(images[-1:], 1)
    below = lax.ppermute(own, RING, around(1))
    above = lax.ppermute(own, RING, around(7))
    own, top = lax.optimization_barrier((own, top))
    left = col_rim(jnp.concatenate([top[:, -1:], images[:, -1:]], axis=0), 1)
    far = jnp.concatenate(
        [lax.ppermute(own[:128], RING, around(2)), lax.ppermute(own[128:], RING, around(6))]
    )
    ring = jnp.stack([own, above, far, below])
    ring, left = lax.optimization_barrier((ring, left))
    return top, left, ring, swap_cores(ring)


def slot_order():
    target = np.arange(192)
    both = []
    for odd in range(2):
        group = (target // 24 + odd * 4) % 8
        wanted = target // 2 % 12 * 16 + target % 2 * 8 + group
        both.append(target[None, :] == wanted[:, None])
    both = jnp.asarray(np.stack(both), bf16)
    return lax.dynamic_index_in_dim(both, lax.axis_index("z") % 2, 0, keepdims=False)


def row_order():
    target = np.arange(192)
    wanted = target // 2 % 8 * 24 + target // 16 * 2 + target % 2
    return jnp.asarray(target[None, :] == wanted[:, None], bf16)


def dot_kt(left, right):
    return lax.dot_general(left, right, (((1,), (1,)), ((), ())), preferred_element_type=f32)


def attention_kernel(slots_ref, order_ref, valid_ref, out_ref, sorted_ref, result_ref):
    scale = 1.0 / math.sqrt(32)
    order = order_ref[...]
    valid = valid_ref[...] > 0.0
    for part in range(8):
        sorted_ref[part * 192 : part * 192 + 192] = dot(order, slots_ref[part]).astype(bf16)
    for group in range(8):
        blocks = [row * 16 for row in range(96) if row % 8 == group]
        unit = jnp.concatenate([sorted_ref[at : at + 16] for at in blocks], axis=0)
        query, key, value, d_mix = (unit[:, 32 * i : 32 * i + 32] for i in range(4))
        raised = jnp.where(valid, jnp.exp(dot_kt(query, key) * scale), 0.0)
        weights32 = raised * (1.0 / jnp.sum(raised, axis=-1, keepdims=True))
        weights = weights32.astype(bf16)
        mixture = dot(weights, value)
        d_weights = dot_kt(d_mix, value)
        d_value = dot_tt(weights, d_mix)
        d_scores = (
            weights32 * (d_weights - jnp.sum(weights32 * d_weights, axis=-1, keepdims=True))
        ).astype(bf16)
        d_query = dot(d_scores, key) * scale
        d_key = dot_tt(d_scores, query) * scale
        result = jnp.concatenate([d_query, d_key, d_value, mixture], axis=-1).astype(bf16)
        for index, at in enumerate(blocks):
            result_ref[at : at + 16] = result[index * 16 : index * 16 + 16]
    for part in range(8):
        out_ref[part] = dot_tt(order, result_ref[part * 192 : part * 192 + 192]).astype(bf16)


def attention(slots):
    slot = lax.broadcasted_iota(jnp.int32, (1, 192), 1)
    high = (lax.axis_index("z") >= 4).astype(jnp.int32)
    valid = ((slot % 2 == 0) | (slot // 2 % 2 == high)).astype(f32)
    return pl.pallas_call(
        attention_kernel,
        out_shape=jax.ShapeDtypeStruct((8, 192, 128), bf16),
        scratch_shapes=[pltpu.VMEM((1536, 128), bf16), pltpu.VMEM((1536, 128), bf16)],
        cost_estimate=pl.CostEstimate(
            flops=7_000_000_000, bytes_accessed=1_000_000, transcendentals=300_000
        ),
        name="attention",
    )(slots, row_order(), valid)


def token_mask():
    return lax.broadcasted_iota(jnp.int32, (192, 1), 0) % 16 < 12


def normalize(section):
    wide = section.astype(f32)
    centred = wide - jnp.mean(wide, axis=-1, keepdims=True)
    inv_std = lax.rsqrt(jnp.mean(centred * centred, axis=-1, keepdims=True) + norm_epsilon)
    return centred * inv_std, inv_std


def held(shape, dtype=bf16):
    return pltpu.HBM(shape, dtype)


def expand_kernel(
    images_ref, top_ref, left_ref, w_expand_ref, taps_ref,
    even_ref, odd_ref, slopes_ref, activated_ref, conv_slope_ref, cells_ref, pooled_ref,
    wide_ref, top_wide_ref, left_wide_ref, plane_ref, rows_ref,
):
    @pl.when(pl.program_id(0) == 0)
    def _():
        slot = lax.broadcasted_iota(jnp.int32, (1, 16, 1), 1)
        for half in range(2):
            lanes = slice(128 * half, 128 * half + 128)
            wide_ref[half] = images_ref[:, :, lanes].astype(f32)
            top_wide_ref[half] = top_ref[:, :, lanes].astype(f32)
        left_wide_ref[...] = left_ref[...].astype(f32)
        pooled = 0.0
        for row in range(2):
            for col in range(2):
                plane = 2 * row + col
                plane_ref[...] = jnp.zeros((13, 16, 256), f32)
                for half in range(2):
                    lanes = slice(128 * half, 128 * half + 128)
                    plane_ref[row : row + 12, 0:12, lanes] = wide_ref[
                        half, pl.ds(row, 12, stride=2), pl.ds(col, 12, stride=2), :
                    ]
                    if row:
                        plane_ref[0:1, 0:12, lanes] = top_wide_ref[
                            half, :, pl.ds(col, 12, stride=2), :
                        ]
                if col:
                    plane_ref[row : row + 12, 15:16, :] = left_wide_ref[1:25].reshape(
                        12, 2, 1, 256
                    )[:, row]
                if row and col:
                    plane_ref[0:1, 15:16, :] = left_wide_ref[0:1]
                cells = plane_ref[...]
                rows_ref[plane] = cells.astype(bf16).reshape(208, 256)
                cells = cells[row : row + 12]
                cells_ref[plane] = cells.astype(bf16).reshape(192, 256)
                pooled = pooled + cells
        pooled = jnp.where(slot < 12, pooled * 0.25, 0.0)
        pooled_ref[...] = pooled.astype(bf16).reshape(192, 256)

    taps = [[taps_ref[3 * a + b : 3 * a + b + 1, :].astype(f32) for b in range(3)] for a in range(3)]
    expanded = {}
    for row in range(2):
        for col in range(2):
            count = 192 + 16 * row
            value, slope = gelu_both(dot(rows_ref[2 * row + col, 0:count], w_expand_ref[...]))
            value = value.astype(bf16)
            (odd_ref if row else even_ref)[col] = value
            slopes_ref[2 * row + col] = slope[16 * row :].astype(bf16)
            expanded[row, col] = value.astype(f32).reshape(12 + row, 16, 256)

    def window(row_tap, odd_col):
        plane = expanded[(row_tap + 1) % 2, odd_col]
        return plane[row_tap // 2 : row_tap // 2 + 12]

    straight = sum(
        window(a, 0) * taps[a][1] + window(a, 1) * taps[a][2] for a in range(3)
    )
    moved = sum(window(a, 1) * taps[a][0] for a in range(3))
    value, slope = gelu_both(straight + pltpu.roll(moved, 1, 1))
    activated_ref[...] = value.astype(bf16).reshape(192, 256)
    conv_slope_ref[...] = slope.astype(bf16).reshape(192, 256)


def expand_step(*inputs):
    def chunk(*lead):
        return pl.BlockSpec(lead + (256,), lambda step: (0,) * len(lead) + (step,))

    def whole(*shape):
        return pl.BlockSpec(shape, lambda step: (0,) * len(shape))

    shapes = [
        (2, 192, 1024), (2, 208, 1024), (4, 192, 1024), (192, 1024), (192, 1024), (4, 192, 256),
        (192, 256),
    ]
    return call(
        expand_kernel,
        "expand",
        [held(shape) for shape in shapes],
        6_000_000_000,
        scratch=[
            pltpu.VMEM((2, 24, 24, 128), f32),
            pltpu.VMEM((2, 1, 24, 128), f32),
            pltpu.VMEM((25, 1, 256), f32),
            pltpu.VMEM((13, 16, 256), f32),
            pltpu.VMEM((4, 208, 256), bf16),
        ],
        grid=(4,),
        in_specs=[whole(24, 24, 256), whole(1, 24, 256), whole(25, 1, 256), chunk(256), chunk(9)],
        out_specs=[
            chunk(2, 192), chunk(2, 208), chunk(4, 192), chunk(192), chunk(192),
            whole(4, 192, 256), whole(192, 256),
        ],
    )(*inputs)


def row_buffers():
    return [
        pltpu.VMEM((192, 1024), bf16),
        pltpu.VMEM((192, 256), bf16),
        pltpu.VMEM((192, 512), bf16),
        pltpu.SemaphoreType.DMA((3,)),
    ]


def section_kernel(
    spot_ref, ring_ref, other_ref, activated_in, pooled_in, short_ref, cotangent_in, slots_ref,
    pieces_ref, section_ref, normed_ref, proj_ref, qkv_ref, out_ref,
    activated_ref, pooled_ref, cotangent_ref, sems,
):
    core, y_lo = spot_ref[0], spot_ref[1]
    copies = [
        pltpu.make_async_copy(activated_in, activated_ref, sems.at[0]),
        pltpu.make_async_copy(pooled_in, pooled_ref, sems.at[1]),
        pltpu.make_async_copy(cotangent_in, cotangent_ref, sems.at[2]),
    ]
    for copy in copies:
        copy.start()

    def place(shard, source, at):
        proj_ref[shard * 128 : shard * 128 + 128] = source[at, 0:128]
        qkv_ref[shard * 64 : shard * 64 + 64, 0:512] = source[at, 128:192]
        out_ref[shard * 32 : shard * 32 + 32] = source[at, 192:224]
        qkv_ref[shard * 64 : shard * 64 + 32, 512:768] = source[at, 224:256, 0:256]
        qkv_ref[shard * 64 + 32 : shard * 64 + 64, 512:768] = source[at, 224:256, 256:512]

    for shard in range(8):
        at = lax.rem(shard // 2 - y_lo + 4, 4)
        pl.when(core == shard % 2)(lambda: place(shard, ring_ref, at))
        pl.when(core != shard % 2)(lambda: place(shard, other_ref, at))
    for copy in copies:
        copy.wait()
    section = (
        dot(activated_ref[...], proj_ref[...]) + dot(pooled_ref[...], short_ref[...])
    ).astype(bf16)
    section_ref[...] = section
    normed = jnp.where(token_mask(), normalize(section)[0], 0.0).astype(bf16)
    normed_ref[...] = normed
    packed = dot(normed, qkv_ref[...]).astype(bf16)
    d_mixture = dot_kt(cotangent_ref[...], out_ref[...]).astype(bf16)
    tokens = jnp.concatenate([packed, d_mixture], axis=1)
    tokens = dot(slots_ref[...], tokens).astype(bf16)
    for head in range(HEADS):
        at = [part * 256 + head * 32 for part in range(4)]
        pieces_ref[head] = jnp.concatenate([tokens[:, i : i + 32] for i in at], axis=1)


def section_step(spot, ring, other, activated, pooled, w_short, cotangent, slots):
    inputs = (spot, ring, other, in_place(activated), in_place(pooled), w_short, in_place(cotangent), slots)
    shapes = [(8, 192, 128), (192, 512), (192, 512), (1024, 512), (512, 768), (256, 512)]
    return call(
        section_kernel,
        "section",
        [held(shape) for shape in shapes],
        4_000_000_000,
        scratch=row_buffers(),
        in_specs=[
            pl.BlockSpec(memory_space=space)
            for space in (
                pltpu.SMEM, pltpu.VMEM, pltpu.VMEM, pltpu.HBM, pltpu.HBM, pltpu.VMEM, pltpu.HBM,
                pltpu.VMEM,
            )
        ],
    )(*inputs)[:5]


def back_kernel(
    got_ref, slots_ref, section_ref, cotangent_ref, proj_in, qkv_in, slope_in,
    results_ref, d_section_ref, d_conv_ref, proj_ref, qkv_ref, slope_ref, sems,
):
    copies = [
        pltpu.make_async_copy(qkv_in, qkv_ref, sems.at[0]),
        pltpu.make_async_copy(proj_in, proj_ref, sems.at[1]),
        pltpu.make_async_copy(slope_in, slope_ref, sems.at[2]),
    ]
    for copy in copies:
        copy.start()
    used = token_mask()
    got = [got_ref[head] for head in range(HEADS)]
    got = jnp.concatenate(
        [got[head][:, 32 * part : 32 * part + 32] for part in range(4) for head in range(HEADS)],
        axis=1,
    )
    results = dot_tt(slots_ref[...], got)
    results = jnp.where(used, results, 0.0).astype(bf16)
    results_ref[...] = results
    normalized, inv_std = normalize(section_ref[...])
    copies[0].wait()
    d_normed = dot_kt(results[:, :768], qkv_ref[...])
    d_section = cotangent_ref[...].astype(f32) + inv_std * (
        d_normed
        - jnp.mean(d_normed, axis=-1, keepdims=True)
        - normalized * jnp.mean(d_normed * normalized, axis=-1, keepdims=True)
    )
    d_section = jnp.where(used, d_section, 0.0).astype(bf16)
    d_section_ref[...] = d_section
    copies[1].wait()
    copies[2].wait()
    d_activated = dot_kt(d_section, proj_ref[...])
    d_conv_ref[...] = (d_activated * slope_ref[...].astype(f32)).astype(bf16)


def back_step(got, slots, section, cotangent, proj, qkv, slope):
    shapes = [(192, 1024), (192, 512), (192, 1024)]
    return call(
        back_kernel,
        "back",
        [jax.ShapeDtypeStruct(shape, bf16) for shape in shapes],
        1_500_000_000,
        scratch=[
            pltpu.VMEM((1024, 512), bf16),
            pltpu.VMEM((512, 768), bf16),
            pltpu.VMEM((192, 1024), bf16),
            pltpu.SemaphoreType.DMA((3,)),
        ],
        in_specs=[pl.BlockSpec(memory_space=pltpu.VMEM)] * 4
        + [pl.BlockSpec(memory_space=pltpu.HBM)] * 3,
    )(got, slots, section, cotangent, in_place(proj), in_place(qkv), in_place(slope))


def parts_kernel(
    results_ref, d_section_ref, normed_ref, cotangent_in, activated_in, pooled_in, short_ref,
    early_ref, d_pooled_ref, activated_ref, pooled_ref, cotangent_ref, sems,
):
    copies = [
        pltpu.make_async_copy(activated_in, activated_ref, sems.at[0]),
        pltpu.make_async_copy(pooled_in, pooled_ref, sems.at[1]),
        pltpu.make_async_copy(cotangent_in, cotangent_ref, sems.at[2]),
    ]
    for copy in copies:
        copy.start()
    results = results_ref[...]
    d_section = d_section_ref[...]

    def store(part, first, rows):
        lanes = part.shape[1] // 128
        for shard in range(8):
            for piece in range(rows // 16 * lanes):
                row = shard * rows + piece // lanes * 16
                lane = piece % lanes * 128
                index = first + piece
                at = shard // 2 * 32 + index % 2 * 16
                early_ref[shard % 2, index // 2, at : at + 16, :] = part[
                    row : row + 16, lane : lane + 128
                ]

    store(dot_tt(normed_ref[...], results[:, :768]).astype(bf16), 32, 64)
    for copy in copies:
        copy.wait()
    store(dot_tt(activated_ref[...], d_section).astype(bf16), 0, 128)
    store(dot_tt(results[:, 768:], cotangent_ref[...]).astype(bf16), 56, 32)
    short = dot_tt(pooled_ref[...], d_section)
    rows = [short[:, lane * 128 : lane * 128 + 128].reshape(32, 8, 128) for lane in range(4)]
    for core in range(2):
        early_ref[core, :, 128:144, :] = jnp.concatenate(
            [rows[2 * core], rows[2 * core + 1]], axis=1
        ).astype(bf16)
    d_pooled_ref[...] = dot_kt(d_section, short_ref[...]) * 0.25


def parts_step(results, d_section, normed, cotangent, activated, pooled, w_short):
    inputs = (results, d_section, normed, in_place(cotangent), in_place(activated), in_place(pooled), w_short)
    return call(
        parts_kernel,
        "parts",
        [
            jax.ShapeDtypeStruct((2, 32, 144, 128), bf16),
            jax.ShapeDtypeStruct((192, 256), f32),
        ],
        1_000_000_000,
        scratch=row_buffers(),
        in_specs=[
            pl.BlockSpec(memory_space=space)
            for space in (
                pltpu.VMEM, pltpu.VMEM, pltpu.VMEM, pltpu.HBM, pltpu.HBM, pltpu.HBM, pltpu.VMEM,
            )
        ],
    )(*inputs)


def pixel_kernel(
    d_conv_ref, below_ref, right_ref, even_ref, odd_ref, slopes_ref, cells_ref, w_expand_ref,
    taps_ref, d_pooled_ref, image_ref, expand_ref, depth_ref, total_ref,
):
    slot = lax.broadcasted_iota(jnp.int32, (1, 16, 1), 1)
    row_terms = {0: ((1, 0),), 1: ((2, 0), (0, 1))}
    for step in range(4):
        lanes = slice(step * 256, step * 256 + 256)
        here = d_conv_ref[:, lanes].astype(f32).reshape(12, 16, 256)
        rows = jnp.concatenate([here, below_ref[:, :, lanes].astype(f32)], axis=0)
        turned = pltpu.roll(rows, 15, 1)
        after = jnp.where(slot == 11, right_ref[:, :, lanes].astype(f32), turned)
        back = turned[:12]
        taps = [
            [taps_ref[3 * a + b : 3 * a + b + 1, lanes].astype(f32) for b in range(3)]
            for a in range(3)
        ]

        def window(row_tap, odd_col):
            source = even_ref if row_tap == 1 else odd_ref
            first = 16 * (row_tap // 2) if row_tap != 1 else 0
            return source[odd_col, first : first + 192, lanes].astype(f32).reshape(12, 16, 256)

        for a in range(3):
            odd = window(a, 1)
            even = window(a, 0)
            for b, product in ((0, odd * back), (1, even * here), (2, odd * here)):
                total = jnp.sum(jnp.sum(product, axis=0), axis=0, keepdims=True)
                depth_ref[3 * a + b : 3 * a + b + 1, lanes] = total
        col_terms = {0: ((1, rows),), 1: ((2, rows), (0, after))}
        part_expand = 0.0
        for row in range(2):
            for col in range(2):
                d_cells = sum(
                    source[i : i + 12] * taps[a][b]
                    for a, i in row_terms[row]
                    for b, source in col_terms[col]
                )
                d_cells = jnp.where(slot < 12, d_cells, 0.0).reshape(192, 256)
                plane = row * 2 + col
                d_pre = (d_cells * slopes_ref[plane, :, lanes].astype(f32)).astype(bf16)
                part_expand = part_expand + dot_tt(cells_ref[plane], d_pre)
                back_image = dot_kt(d_pre, w_expand_ref[:, lanes])
                so_far = d_pooled_ref[...] if step == 0 else total_ref[plane]
                if step < 3:
                    total_ref[plane] = so_far + back_image
                else:
                    image_ref[plane] = (so_far + back_image).astype(bf16)
        expand_ref[step // 2, :, step % 2 * 16 : step % 2 * 16 + 16] = jnp.concatenate(
            [part_expand[:, :128].reshape(32, 8, 128), part_expand[:, 128:].reshape(32, 8, 128)],
            axis=1,
        ).astype(bf16)


def pixel_step(*inputs):
    return call(
        pixel_kernel,
        "pixel",
        [
            jax.ShapeDtypeStruct((4, 192, 256), bf16),
            jax.ShapeDtypeStruct((2, 32, 32, 128), bf16),
            jax.ShapeDtypeStruct((16, 1024), f32),
        ],
        6_000_000_000,
        scratch=[pltpu.VMEM((4, 192, 256), f32)],
    )(*inputs)


def untiled(pieces, rows, columns):
    height = pieces.shape[1]
    cut = pieces.reshape(rows // height, columns // 128, height, 128)
    return cut.transpose(0, 2, 1, 3).reshape(rows, columns).astype(f32)


def pair_sum(halves):
    core = lax.axis_index("core")
    mine = lax.dynamic_index_in_dim(halves, core, 0, keepdims=False)
    theirs = lax.dynamic_index_in_dim(halves, 1 - core, 0, keepdims=False)
    return (mine.astype(f32) + swap_cores(theirs).astype(f32)).astype(bf16)


def all_sums(early, expand, depth):
    depth = jnp.pad(depth[:9].astype(bf16).reshape(9, 8, 128), ((0, 23), (0, 0), (0, 0)))
    core = lax.axis_index("core")

    def share(of):
        own = lax.dynamic_index_in_dim(expand, of, 0, keepdims=False)
        return jnp.concatenate([own, jnp.where(of == 0, depth, jnp.zeros((), bf16))], axis=1)

    late = (share(core).astype(f32) + swap_cores(share(1 - core)).astype(f32)).astype(bf16)
    pair = jnp.concatenate([early, late], axis=1)
    line = jnp.sum(exchange(pair, "x").reshape(4, 8, 184, 128).astype(f32), axis=0).astype(bf16)
    sheet = jnp.sum(exchange(line, "z").astype(f32), axis=0).astype(bf16)
    column = jnp.concatenate(
        [sheet[:128].reshape(4, 32, 128), jnp.broadcast_to(sheet[None, 128:], (4, 56, 128))], axis=1
    )
    column = jnp.broadcast_to(column[:, None], (4, 2, 88, 128)).reshape(8, 88, 128)
    grad_scale = 1.0 / math.sqrt(8 * 96 * 96)
    total = jnp.sum(exchange(column, RING).astype(f32), axis=0) * grad_scale
    near = spread(total.astype(bf16), ("x", "z"), 32)
    own = near[:, 32:]
    other = swap_cores(own)
    matrix = near[:, :32].reshape(64, 16, 128)
    grad_proj = untiled(matrix[:32], 128, 512)
    grad_qkv = untiled(matrix[32:56], 64, 768)
    grad_out = untiled(matrix[56:], 32, 512)
    first = lax.axis_index("core") == 0
    both = jnp.where(first, jnp.stack([own, other]), jnp.stack([other, own]))

    def joined(start, count):
        part = both[:, :, start : start + 8 * count].reshape(2, 32, count, 8, 128)
        return part.transpose(1, 3, 0, 2, 4).reshape(256, 256 * count).astype(f32)

    grad_short = joined(0, 2)
    grad_expand = joined(16, 4)
    grad_depth = both[0, :9, 48:].reshape(3, 3, 1024).astype(f32)
    return grad_expand, grad_depth, grad_short, grad_proj, grad_qkv, grad_out


def slots16(cells):
    return jnp.pad(cells, ((0, 0), (0, 4), (0, 0)))


def on_device(images, w_expand, w_depth, w_short, w_proj, w_qkv, w_out, cotangent):
    images = images[0]
    cotangent = slots16(cotangent[0])
    top, left, ring, other = first_transfers(images, w_proj, w_qkv, w_out)
    slots = slot_order()
    taps = w_depth.reshape(9, 1024)
    even, odd, slopes, activated, conv_slope, cells, pooled = expand_step(
        images, top, left, w_expand, taps
    )
    cotangent = cotangent.reshape(192, 512)
    spot = jnp.stack([lax.axis_index("core"), lax.axis_index("ylo")]).astype(jnp.int32)
    pieces, section_out, normed, proj, qkv = section_step(
        spot, ring, other, activated, pooled, w_short, cotangent, slots
    )
    got = exchange(pieces.reshape(64, 24, 128), GRID_AXES)
    mixed = attention(got.reshape(8, 192, 128))
    got = exchange(mixed.reshape(64, 24, 128), GRID_AXES).reshape(HEADS, 192, 128)
    results, d_section, d_conv = back_step(
        got, slots, section_out, cotangent, proj, qkv, conv_slope
    )
    below = row_rim(d_conv[:12].reshape(1, 12, 1024), -1)
    edge = d_conv.reshape(12, 16, 1024)[:, :1]
    right = jnp.concatenate([col_rim(edge, -1), diagonal_rim(edge[:1], -1)], axis=0)
    early, d_pooled = parts_step(
        results, d_section, normed, cotangent, activated, pooled, w_short
    )
    early = pair_sum(early)
    image, expand, depth = pixel_step(
        d_conv, slots16(below), right, even, odd, slopes, cells, w_expand, taps,
        d_pooled,
    )
    image = image.reshape(2, 2, 12, 16, 256)[:, :, :, :12]
    grad_image = image.transpose(2, 0, 3, 1, 4).reshape(1, 24, 24, 256)
    return (grad_image,) + all_sums(early, expand, depth)


def solution(mesh):
    fine = Mesh(mesh.devices.reshape(4, 2, 2, 4, 8), ("ylo", "core", "yhi", "x", "z"))
    cells = P(SAMPLE, ROW, COL, None)
    rows = P(SAMPLE, None)
    return jax.shard_map(
        on_device,
        mesh=fine,
        in_specs=(cells, P(), P(), P(), rows, rows, rows, cells),
        out_specs=(cells, P(), P(), P(), rows, rows, rows),
        check_vma=False,
    )
```

```python
import math

import jax
import jax.numpy as jnp
import numpy as np
from jax import lax
from jax.experimental import pallas as pl
from jax.experimental.pallas import tpu as pltpu
from jax.sharding import Mesh
from jax.sharding import PartitionSpec as P

HEADS = 8
PARTS = 8

SAMPLE = ("ylo", "core")
ROW = ("yhi", "x")
COL = "z"
GRID_AXES = ("yhi", "x", "z")
CHIPS = ("ylo", "yhi", "x", "z")
RING = ("ylo", "yhi")

norm_epsilon = 1e-05
tanh_coeff = 0.7978845608028654
cubic_coeff = 0.044715

bf16 = jnp.bfloat16
f32 = jnp.float32


def gelu_both(values):
    square = values * values
    inner = jnp.tanh(values * (tanh_coeff * cubic_coeff * square + tanh_coeff))
    half = 0.5 * inner + 0.5
    value = values * half
    slope = half + value * (1.0 - inner) * (3.0 * tanh_coeff * cubic_coeff * square + tanh_coeff)
    return value, slope


def dot(left, right):
    return lax.dot_general(
        left, right, (((left.ndim - 1,), (0,)), ((), ())), preferred_element_type=f32
    )


def dot_t(left, right):
    return lax.dot_general(
        left, right, (((left.ndim - 1,), (1,)), ((), ())), preferred_element_type=f32
    )


def dot_tt(left, right):
    return lax.dot_general(left, right, (((0,), (0,)), ((), ())), preferred_element_type=f32)


def outer_sum(left, right):
    return lax.dot_general(
        left.reshape(-1, left.shape[-1]),
        right.reshape(-1, right.shape[-1]),
        (((0,), (0,)), ((), ())),
        preferred_element_type=f32,
    )


def step_route(count, distance):
    return [(i - distance, i) for i in range(count) if 0 <= i - distance < count]


def row_rim(edge, distance):
    return lax.ppermute(edge, ROW, step_route(PARTS, distance))


def col_rim(edge, distance):
    return lax.ppermute(edge, COL, step_route(PARTS, distance))


def diagonal_rim(edge, distance):
    route = [
        ((r - distance) * PARTS + c - distance, r * PARTS + c)
        for r in range(PARTS)
        for c in range(PARTS)
        if 0 <= r - distance < PARTS and 0 <= c - distance < PARTS
    ]
    return lax.ppermute(edge, GRID_AXES, route)


def around(distance):
    place = [y % 4 * 2 + y // 4 for y in range(8)]
    return [(place[y], place[(y + distance) % 8]) for y in range(8)]


def swap_cores(block):
    return lax.ppermute(block, "core", [(0, 1), (1, 0)])


def exchange(block, axes):
    return lax.all_to_all(block, axes, 0, 0, tiled=True)


def spread(block, axes, count):
    return exchange(jnp.broadcast_to(block[None], (count,) + block.shape), axes)


def call(body, name, out_shape, flops, scratch=(), **rest):
    return pl.pallas_call(
        body,
        out_shape=out_shape,
        scratch_shapes=scratch,
        compiler_params=pltpu.CompilerParams(vmem_limit_bytes=24 * 1024 * 1024),
        cost_estimate=pl.CostEstimate(flops=flops, bytes_accessed=8_000_000, transcendentals=0),
        name=name,
        **rest,
    )


def in_place(array):
    return pltpu.with_memory_space_constraint(array, pltpu.HBM)


def shard_kernel(proj_ref, qkv_ref, out_ref, own_ref, sems):
    moves = [
        (proj_ref, own_ref.at[0:128]),
        (qkv_ref.at[:, 0:512], own_ref.at[128:192]),
        (out_ref, own_ref.at[192:224]),
        (qkv_ref.at[0:32, 512:768], own_ref.at[224:256, 0:256]),
        (qkv_ref.at[32:64, 512:768], own_ref.at[224:256, 256:512]),
    ]
    copies = [
        pltpu.make_async_copy(source, target, sems.at[index])
        for index, (source, target) in enumerate(moves)
    ]
    for copy in copies:
        copy.start()
    for copy in copies:
        copy.wait()


def first_transfers(images, w_proj, w_qkv, w_out):
    own = call(
        shard_kernel,
        "shard",
        jax.ShapeDtypeStruct((256, 512), bf16),
        1_000_000,
        scratch=[pltpu.SemaphoreType.DMA((5,))],
        in_specs=[pl.BlockSpec(memory_space=pltpu.HBM)] * 3,
    )(in_place(w_proj), in_place(w_qkv), in_place(w_out))
    top = row_rim(images[-1:], 1)
    below = lax.ppermute(own, RING, around(1))
    above = lax.ppermute(own, RING, around(7))
    own, top = lax.optimization_barrier((own, top))
    left = col_rim(jnp.concatenate([top[:, -1:], images[:, -1:]], axis=0), 1)
    far = jnp.concatenate(
        [lax.ppermute(own[:128], RING, around(2)), lax.ppermute(own[128:], RING, around(6))]
    )
    ring = jnp.stack([own, above, far, below])
    ring, left = lax.optimization_barrier((ring, left))
    return top, left, ring, swap_cores(ring)


def slot_order():
    order = np.zeros((144, 192), np.float32)
    for row in range(12):
        for col in range(12):
            piece = row % 4 * 2 + col % 4 // 2
            place = row // 4 * 6 + col // 4 * 2 + col % 2
            order[piece * 18 + place, row * 16 + col] = 1.0
    return jnp.asarray(order, bf16)


def unit_order():
    order = np.zeros((576, 576), np.float32)
    filled = [0] * 8
    for source in range(576):
        part_row, part_col, place = source // 144, source % 144 // 18, source % 18
        high_row = (part_row + place // 6) % 2
        high_col = (part_col + place % 6 // 2) % 2
        unit = high_row * 4 + high_col * 2 + place % 2
        order[unit * 72 + filled[unit], source] = 1.0
        filled[unit] += 1
    return jnp.asarray(order, bf16)


def dot_kt(left, right):
    return lax.dot_general(left, right, (((1,), (1,)), ((), ())), preferred_element_type=f32)


def attention_kernel(tokens_ref, order_ref, out_ref, sorted_ref, result_ref):
    scale = 1.0 / math.sqrt(32)
    order = order_ref[...]
    for half in range(2):
        tokens = tokens_ref[4 * half : 4 * half + 4].reshape(576, 128)
        sorted_ref[half] = dot(order, tokens)
    for unit in range(8):
        at = slice(unit * 72, unit * 72 + 72)
        tokens = jnp.concatenate([sorted_ref[0, at], sorted_ref[1, at]], axis=0).astype(bf16)
        query, key, value, d_mix = (tokens[:, 32 * i : 32 * i + 32] for i in range(4))
        raised = jnp.exp(dot_kt(query, key) * scale)
        weights32 = raised * (1.0 / jnp.sum(raised, axis=-1, keepdims=True))
        weights = weights32.astype(bf16)
        mixture = dot(weights, value)
        d_weights = dot_kt(d_mix, value)
        d_value = dot_tt(weights, d_mix)
        d_scores = (
            weights32 * (d_weights - jnp.sum(weights32 * d_weights, axis=-1, keepdims=True))
        ).astype(bf16)
        d_query = dot(d_scores, key) * scale
        d_key = dot_tt(d_scores, query) * scale
        result = jnp.concatenate([d_query, d_key, d_value, mixture], axis=-1)
        result_ref[0, at] = result[:72]
        result_ref[1, at] = result[72:]
    for half in range(2):
        back = dot_tt(order, result_ref[half].astype(bf16)).astype(bf16)
        out_ref[4 * half : 4 * half + 4] = back.reshape(4, 144, 128)


def attention(tokens):
    return pl.pallas_call(
        attention_kernel,
        out_shape=jax.ShapeDtypeStruct((8, 144, 128), bf16),
        scratch_shapes=[pltpu.VMEM((2, 576, 128), f32), pltpu.VMEM((2, 576, 128), f32)],
        cost_estimate=pl.CostEstimate(
            flops=6_000_000_000, bytes_accessed=1_000_000, transcendentals=300_000
        ),
        name="attention",
    )(tokens, unit_order())


def token_mask():
    return lax.broadcasted_iota(jnp.int32, (192, 1), 0) % 16 < 12


def normalize(section):
    wide = section.astype(f32)
    centred = wide - jnp.mean(wide, axis=-1, keepdims=True)
    inv_std = lax.rsqrt(jnp.mean(centred * centred, axis=-1, keepdims=True) + norm_epsilon)
    return centred * inv_std, inv_std


def held(shape, dtype=bf16):
    return pltpu.HBM(shape, dtype)


def expand_kernel(
    images_ref, top_ref, left_ref, w_expand_ref, taps_ref,
    even_ref, odd_ref, slopes_ref, activated_ref, conv_slope_ref, cells_ref, pooled_ref,
    wide_ref, top_wide_ref, left_wide_ref, plane_ref, rows_ref,
):
    @pl.when(pl.program_id(0) == 0)
    def _():
        slot = lax.broadcasted_iota(jnp.int32, (1, 16, 1), 1)
        for half in range(2):
            lanes = slice(128 * half, 128 * half + 128)
            wide_ref[half] = images_ref[:, :, lanes].astype(f32)
            top_wide_ref[half] = top_ref[:, :, lanes].astype(f32)
        left_wide_ref[...] = left_ref[...].astype(f32)
        pooled = 0.0
        for row in range(2):
            for col in range(2):
                plane = 2 * row + col
                plane_ref[...] = jnp.zeros((13, 16, 256), f32)
                for half in range(2):
                    lanes = slice(128 * half, 128 * half + 128)
                    plane_ref[row : row + 12, 0:12, lanes] = wide_ref[
                        half, pl.ds(row, 12, stride=2), pl.ds(col, 12, stride=2), :
                    ]
                    if row:
                        plane_ref[0:1, 0:12, lanes] = top_wide_ref[
                            half, :, pl.ds(col, 12, stride=2), :
                        ]
                if col:
                    plane_ref[row : row + 12, 15:16, :] = left_wide_ref[1:25].reshape(
                        12, 2, 1, 256
                    )[:, row]
                if row and col:
                    plane_ref[0:1, 15:16, :] = left_wide_ref[0:1]
                cells = plane_ref[...]
                rows_ref[plane] = cells.astype(bf16).reshape(208, 256)
                cells = cells[row : row + 12]
                cells_ref[plane] = cells.astype(bf16).reshape(192, 256)
                pooled = pooled + cells
        pooled = jnp.where(slot < 12, pooled * 0.25, 0.0)
        pooled_ref[...] = pooled.astype(bf16).reshape(192, 256)

    taps = [[taps_ref[3 * a + b : 3 * a + b + 1, :].astype(f32) for b in range(3)] for a in range(3)]
    expanded = {}
    for row in range(2):
        for col in range(2):
            count = 192 + 16 * row
            value, slope = gelu_both(dot(rows_ref[2 * row + col, 0:count], w_expand_ref[...]))
            value = value.astype(bf16)
            (odd_ref if row else even_ref)[col] = value
            slopes_ref[2 * row + col] = slope[16 * row :].astype(bf16)
            expanded[row, col] = value.astype(f32).reshape(12 + row, 16, 256)

    def window(row_tap, odd_col):
        plane = expanded[(row_tap + 1) % 2, odd_col]
        return plane[row_tap // 2 : row_tap // 2 + 12]

    straight = sum(
        window(a, 0) * taps[a][1] + window(a, 1) * taps[a][2] for a in range(3)
    )
    moved = sum(window(a, 1) * taps[a][0] for a in range(3))
    value, slope = gelu_both(straight + pltpu.roll(moved, 1, 1))
    activated_ref[...] = value.astype(bf16).reshape(192, 256)
    conv_slope_ref[...] = slope.astype(bf16).reshape(192, 256)


def expand_step(*inputs):
    def chunk(*lead):
        return pl.BlockSpec(lead + (256,), lambda step: (0,) * len(lead) + (step,))

    def whole(*shape):
        return pl.BlockSpec(shape, lambda step: (0,) * len(shape))

    shapes = [
        (2, 192, 1024), (2, 208, 1024), (4, 192, 1024), (192, 1024), (192, 1024), (4, 192, 256),
        (192, 256),
    ]
    return call(
        expand_kernel,
        "expand",
        [held(shape) for shape in shapes],
        6_000_000_000,
        scratch=[
            pltpu.VMEM((2, 24, 24, 128), f32),
            pltpu.VMEM((2, 1, 24, 128), f32),
            pltpu.VMEM((25, 1, 256), f32),
            pltpu.VMEM((13, 16, 256), f32),
            pltpu.VMEM((4, 208, 256), bf16),
        ],
        grid=(4,),
        in_specs=[whole(24, 24, 256), whole(1, 24, 256), whole(25, 1, 256), chunk(256), chunk(9)],
        out_specs=[
            chunk(2, 192), chunk(2, 208), chunk(4, 192), chunk(192), chunk(192),
            whole(4, 192, 256), whole(192, 256),
        ],
    )(*inputs)


def row_buffers():
    return [
        pltpu.VMEM((192, 1024), bf16),
        pltpu.VMEM((192, 256), bf16),
        pltpu.VMEM((192, 512), bf16),
        pltpu.SemaphoreType.DMA((3,)),
    ]


def section_kernel(
    spot_ref, ring_ref, other_ref, activated_in, pooled_in, short_ref, cotangent_in, slots_ref,
    pieces_ref, section_ref, normed_ref, proj_ref, qkv_ref, out_ref,
    activated_ref, pooled_ref, cotangent_ref, sems,
):
    core, y_lo = spot_ref[0], spot_ref[1]
    copies = [
        pltpu.make_async_copy(activated_in, activated_ref, sems.at[0]),
        pltpu.make_async_copy(pooled_in, pooled_ref, sems.at[1]),
        pltpu.make_async_copy(cotangent_in, cotangent_ref, sems.at[2]),
    ]
    for copy in copies:
        copy.start()

    def place(shard, source, at):
        proj_ref[shard * 128 : shard * 128 + 128] = source[at, 0:128]
        qkv_ref[shard * 64 : shard * 64 + 64, 0:512] = source[at, 128:192]
        out_ref[shard * 32 : shard * 32 + 32] = source[at, 192:224]
        qkv_ref[shard * 64 : shard * 64 + 32, 512:768] = source[at, 224:256, 0:256]
        qkv_ref[shard * 64 + 32 : shard * 64 + 64, 512:768] = source[at, 224:256, 256:512]

    for shard in range(8):
        at = lax.rem(shard // 2 - y_lo + 4, 4)
        pl.when(core == shard % 2)(lambda: place(shard, ring_ref, at))
        pl.when(core != shard % 2)(lambda: place(shard, other_ref, at))
    for copy in copies:
        copy.wait()
    section = (
        dot(activated_ref[...], proj_ref[...]) + dot(pooled_ref[...], short_ref[...])
    ).astype(bf16)
    section_ref[...] = section
    normed = jnp.where(token_mask(), normalize(section)[0], 0.0).astype(bf16)
    normed_ref[...] = normed
    packed = dot(normed, qkv_ref[...]).astype(bf16)
    d_mixture = dot_kt(cotangent_ref[...], out_ref[...]).astype(bf16)
    tokens = jnp.concatenate([packed, d_mixture], axis=1)
    tokens = dot(slots_ref[...], tokens).astype(bf16)
    for head in range(HEADS):
        at = [part * 256 + head * 32 for part in range(4)]
        pieces_ref[head] = jnp.concatenate([tokens[:, i : i + 32] for i in at], axis=1)


def section_step(spot, ring, other, activated, pooled, w_short, cotangent, slots):
    inputs = (spot, ring, other, in_place(activated), in_place(pooled), w_short, in_place(cotangent), slots)
    shapes = [(8, 144, 128), (192, 512), (192, 512), (1024, 512), (512, 768), (256, 512)]
    return call(
        section_kernel,
        "section",
        [held(shape) for shape in shapes],
        4_000_000_000,
        scratch=row_buffers(),
        in_specs=[
            pl.BlockSpec(memory_space=space)
            for space in (
                pltpu.SMEM, pltpu.VMEM, pltpu.VMEM, pltpu.HBM, pltpu.HBM, pltpu.VMEM, pltpu.HBM,
                pltpu.VMEM,
            )
        ],
    )(*inputs)[:5]


def back_kernel(
    got_ref, slots_ref, section_ref, cotangent_ref, proj_in, qkv_in, slope_in,
    results_ref, d_section_ref, d_conv_ref, proj_ref, qkv_ref, slope_ref, sems,
):
    copies = [
        pltpu.make_async_copy(qkv_in, qkv_ref, sems.at[0]),
        pltpu.make_async_copy(proj_in, proj_ref, sems.at[1]),
        pltpu.make_async_copy(slope_in, slope_ref, sems.at[2]),
    ]
    for copy in copies:
        copy.start()
    used = token_mask()
    got = [got_ref[head] for head in range(HEADS)]
    got = jnp.concatenate(
        [got[head][:, 32 * part : 32 * part + 32] for part in range(4) for head in range(HEADS)],
        axis=1,
    )
    results = dot_tt(slots_ref[...], got)
    results = jnp.where(used, results, 0.0).astype(bf16)
    results_ref[...] = results
    normalized, inv_std = normalize(section_ref[...])
    copies[0].wait()
    d_normed = dot_kt(results[:, :768], qkv_ref[...])
    d_section = cotangent_ref[...].astype(f32) + inv_std * (
        d_normed
        - jnp.mean(d_normed, axis=-1, keepdims=True)
        - normalized * jnp.mean(d_normed * normalized, axis=-1, keepdims=True)
    )
    d_section = jnp.where(used, d_section, 0.0).astype(bf16)
    d_section_ref[...] = d_section
    copies[1].wait()
    copies[2].wait()
    d_activated = dot_kt(d_section, proj_ref[...])
    d_conv_ref[...] = (d_activated * slope_ref[...].astype(f32)).astype(bf16)


def back_step(got, slots, section, cotangent, proj, qkv, slope):
    shapes = [(192, 1024), (192, 512), (192, 1024)]
    return call(
        back_kernel,
        "back",
        [jax.ShapeDtypeStruct(shape, bf16) for shape in shapes],
        1_500_000_000,
        scratch=[
            pltpu.VMEM((1024, 512), bf16),
            pltpu.VMEM((512, 768), bf16),
            pltpu.VMEM((192, 1024), bf16),
            pltpu.SemaphoreType.DMA((3,)),
        ],
        in_specs=[pl.BlockSpec(memory_space=pltpu.VMEM)] * 4
        + [pl.BlockSpec(memory_space=pltpu.HBM)] * 3,
    )(got, slots, section, cotangent, in_place(proj), in_place(qkv), in_place(slope))


def parts_kernel(
    results_ref, d_section_ref, normed_ref, cotangent_in, activated_in, pooled_in, short_ref,
    early_ref, d_pooled_ref, activated_ref, pooled_ref, cotangent_ref, sems,
):
    copies = [
        pltpu.make_async_copy(activated_in, activated_ref, sems.at[0]),
        pltpu.make_async_copy(pooled_in, pooled_ref, sems.at[1]),
        pltpu.make_async_copy(cotangent_in, cotangent_ref, sems.at[2]),
    ]
    for copy in copies:
        copy.start()
    results = results_ref[...]
    d_section = d_section_ref[...]

    def store(part, first, rows):
        lanes = part.shape[1] // 128
        for shard in range(8):
            for piece in range(rows // 16 * lanes):
                row = shard * rows + piece // lanes * 16
                lane = piece % lanes * 128
                index = first + piece
                at = shard // 2 * 32 + index % 2 * 16
                early_ref[shard % 2, index // 2, at : at + 16, :] = part[
                    row : row + 16, lane : lane + 128
                ]

    store(dot_tt(normed_ref[...], results[:, :768]).astype(bf16), 32, 64)
    for copy in copies:
        copy.wait()
    store(dot_tt(activated_ref[...], d_section).astype(bf16), 0, 128)
    store(dot_tt(results[:, 768:], cotangent_ref[...]).astype(bf16), 56, 32)
    short = dot_tt(pooled_ref[...], d_section)
    rows = [short[:, lane * 128 : lane * 128 + 128].reshape(32, 8, 128) for lane in range(4)]
    for core in range(2):
        early_ref[core, :, 128:144, :] = jnp.concatenate(
            [rows[2 * core], rows[2 * core + 1]], axis=1
        ).astype(bf16)
    d_pooled_ref[...] = dot_kt(d_section, short_ref[...]) * 0.25


def parts_step(results, d_section, normed, cotangent, activated, pooled, w_short):
    inputs = (results, d_section, normed, in_place(cotangent), in_place(activated), in_place(pooled), w_short)
    return call(
        parts_kernel,
        "parts",
        [
            jax.ShapeDtypeStruct((2, 32, 144, 128), bf16),
            jax.ShapeDtypeStruct((192, 256), f32),
        ],
        1_000_000_000,
        scratch=row_buffers(),
        in_specs=[
            pl.BlockSpec(memory_space=space)
            for space in (
                pltpu.VMEM, pltpu.VMEM, pltpu.VMEM, pltpu.HBM, pltpu.HBM, pltpu.HBM, pltpu.VMEM,
            )
        ],
    )(*inputs)


def pixel_kernel(
    d_conv_ref, below_ref, right_ref, even_ref, odd_ref, slopes_ref, cells_ref, w_expand_ref,
    taps_ref, d_pooled_ref, image_ref, expand_ref, depth_ref, total_ref,
):
    slot = lax.broadcasted_iota(jnp.int32, (1, 16, 1), 1)
    row_terms = {0: ((1, 0),), 1: ((2, 0), (0, 1))}
    for step in range(4):
        lanes = slice(step * 256, step * 256 + 256)
        here = d_conv_ref[:, lanes].astype(f32).reshape(12, 16, 256)
        rows = jnp.concatenate([here, below_ref[:, :, lanes].astype(f32)], axis=0)
        turned = pltpu.roll(rows, 15, 1)
        after = jnp.where(slot == 11, right_ref[:, :, lanes].astype(f32), turned)
        back = turned[:12]
        taps = [
            [taps_ref[3 * a + b : 3 * a + b + 1, lanes].astype(f32) for b in range(3)]
            for a in range(3)
        ]

        def window(row_tap, odd_col):
            source = even_ref if row_tap == 1 else odd_ref
            first = 16 * (row_tap // 2) if row_tap != 1 else 0
            return source[odd_col, first : first + 192, lanes].astype(f32).reshape(12, 16, 256)

        for a in range(3):
            odd = window(a, 1)
            even = window(a, 0)
            for b, product in ((0, odd * back), (1, even * here), (2, odd * here)):
                total = jnp.sum(jnp.sum(product, axis=0), axis=0, keepdims=True)
                depth_ref[3 * a + b : 3 * a + b + 1, lanes] = total
        col_terms = {0: ((1, rows),), 1: ((2, rows), (0, after))}
        part_expand = 0.0
        for row in range(2):
            for col in range(2):
                d_cells = sum(
                    source[i : i + 12] * taps[a][b]
                    for a, i in row_terms[row]
                    for b, source in col_terms[col]
                )
                d_cells = jnp.where(slot < 12, d_cells, 0.0).reshape(192, 256)
                plane = row * 2 + col
                d_pre = (d_cells * slopes_ref[plane, :, lanes].astype(f32)).astype(bf16)
                part_expand = part_expand + dot_tt(cells_ref[plane], d_pre)
                back_image = dot_kt(d_pre, w_expand_ref[:, lanes])
                so_far = d_pooled_ref[...] if step == 0 else total_ref[plane]
                if step < 3:
                    total_ref[plane] = so_far + back_image
                else:
                    image_ref[plane] = (so_far + back_image).astype(bf16)
        expand_ref[step // 2, :, step % 2 * 16 : step % 2 * 16 + 16] = jnp.concatenate(
            [part_expand[:, :128].reshape(32, 8, 128), part_expand[:, 128:].reshape(32, 8, 128)],
            axis=1,
        ).astype(bf16)


def pixel_step(*inputs):
    return call(
        pixel_kernel,
        "pixel",
        [
            jax.ShapeDtypeStruct((4, 192, 256), bf16),
            jax.ShapeDtypeStruct((2, 32, 32, 128), bf16),
            jax.ShapeDtypeStruct((16, 1024), f32),
        ],
        6_000_000_000,
        scratch=[pltpu.VMEM((4, 192, 256), f32)],
    )(*inputs)


def untiled(pieces, rows, columns):
    height = pieces.shape[1]
    cut = pieces.reshape(rows // height, columns // 128, height, 128)
    return cut.transpose(0, 2, 1, 3).reshape(rows, columns).astype(f32)


def pair_sum(halves):
    core = lax.axis_index("core")
    mine = lax.dynamic_index_in_dim(halves, core, 0, keepdims=False)
    theirs = lax.dynamic_index_in_dim(halves, 1 - core, 0, keepdims=False)
    return (mine.astype(f32) + swap_cores(theirs).astype(f32)).astype(bf16)


def all_sums(early, expand, depth):
    depth = jnp.pad(depth[:9].astype(bf16).reshape(9, 8, 128), ((0, 23), (0, 0), (0, 0)))
    core = lax.axis_index("core")

    def share(of):
        own = lax.dynamic_index_in_dim(expand, of, 0, keepdims=False)
        return jnp.concatenate([own, jnp.where(of == 0, depth, jnp.zeros((), bf16))], axis=1)

    late = (share(core).astype(f32) + swap_cores(share(1 - core)).astype(f32)).astype(bf16)
    pair = jnp.concatenate([early, late], axis=1)
    line = jnp.sum(exchange(pair, "x").reshape(4, 8, 184, 128).astype(f32), axis=0).astype(bf16)
    sheet = jnp.sum(exchange(line, "z").astype(f32), axis=0).astype(bf16)
    column = jnp.concatenate(
        [sheet[:128].reshape(4, 32, 128), jnp.broadcast_to(sheet[None, 128:], (4, 56, 128))], axis=1
    )
    column = jnp.broadcast_to(column[:, None], (4, 2, 88, 128)).reshape(8, 88, 128)
    grad_scale = 1.0 / math.sqrt(8 * 96 * 96)
    total = jnp.sum(exchange(column, RING).astype(f32), axis=0) * grad_scale
    near = spread(total.astype(bf16), ("x", "z"), 32)
    own = near[:, 32:]
    other = swap_cores(own)
    matrix = near[:, :32].reshape(64, 16, 128)
    grad_proj = untiled(matrix[:32], 128, 512)
    grad_qkv = untiled(matrix[32:56], 64, 768)
    grad_out = untiled(matrix[56:], 32, 512)
    first = lax.axis_index("core") == 0
    both = jnp.where(first, jnp.stack([own, other]), jnp.stack([other, own]))

    def joined(start, count):
        part = both[:, :, start : start + 8 * count].reshape(2, 32, count, 8, 128)
        return part.transpose(1, 3, 0, 2, 4).reshape(256, 256 * count).astype(f32)

    grad_short = joined(0, 2)
    grad_expand = joined(16, 4)
    grad_depth = both[0, :9, 48:].reshape(3, 3, 1024).astype(f32)
    return grad_expand, grad_depth, grad_short, grad_proj, grad_qkv, grad_out


def slots16(cells):
    return jnp.pad(cells, ((0, 0), (0, 4), (0, 0)))


def on_device(images, w_expand, w_depth, w_short, w_proj, w_qkv, w_out, cotangent):
    images = images[0]
    cotangent = slots16(cotangent[0])
    top, left, ring, other = first_transfers(images, w_proj, w_qkv, w_out)
    slots = slot_order()
    taps = w_depth.reshape(9, 1024)
    even, odd, slopes, activated, conv_slope, cells, pooled = expand_step(
        images, top, left, w_expand, taps
    )
    cotangent = cotangent.reshape(192, 512)
    spot = jnp.stack([lax.axis_index("core"), lax.axis_index("ylo")]).astype(jnp.int32)
    pieces, section_out, normed, proj, qkv = section_step(
        spot, ring, other, activated, pooled, w_short, cotangent, slots
    )
    got = exchange(pieces.reshape(64, 9, 2, 128), GRID_AXES)
    mixed = attention(got.reshape(8, 144, 128))
    got = exchange(mixed.reshape(64, 9, 2, 128), GRID_AXES).reshape(HEADS, 144, 128)
    results, d_section, d_conv = back_step(
        got, slots, section_out, cotangent, proj, qkv, conv_slope
    )
    below = row_rim(d_conv[:12].reshape(1, 12, 1024), -1)
    edge = d_conv.reshape(12, 16, 1024)[:, :1]
    right = jnp.concatenate([col_rim(edge, -1), diagonal_rim(edge[:1], -1)], axis=0)
    early, d_pooled = parts_step(
        results, d_section, normed, cotangent, activated, pooled, w_short
    )
    early = pair_sum(early)
    image, expand, depth = pixel_step(
        d_conv, slots16(below), right, even, odd, slopes, cells, w_expand, taps,
        d_pooled,
    )
    image = image.reshape(2, 2, 12, 16, 256)[:, :, :, :12]
    grad_image = image.transpose(2, 0, 3, 1, 4).reshape(1, 24, 24, 256)
    return (grad_image,) + all_sums(early, expand, depth)


def solution(mesh):
    fine = Mesh(mesh.devices.reshape(4, 2, 2, 4, 8), ("ylo", "core", "yhi", "x", "z"))
    cells = P(SAMPLE, ROW, COL, None)
    rows = P(SAMPLE, None)
    return jax.shard_map(
        on_device,
        mesh=fine,
        in_specs=(cells, P(), P(), P(), rows, rows, rows, cells),
        out_specs=(cells, P(), P(), P(), rows, rows, rows),
        check_vma=False,
    )
```

```python
import math

import jax
import jax.numpy as jnp
import numpy as np
from jax import lax
from jax.experimental import pallas as pl
from jax.experimental.pallas import tpu as pltpu
from jax.sharding import Mesh
from jax.sharding import PartitionSpec as P

HEADS = 8
PARTS = 8

SAMPLE = ("ylo", "core")
ROW = ("yhi", "x")
COL = "z"
GRID_AXES = ("yhi", "x", "z")
CHIPS = ("ylo", "yhi", "x", "z")
RING = ("ylo", "yhi")

norm_epsilon = 1e-05
tanh_coeff = 0.7978845608028654
cubic_coeff = 0.044715

bf16 = jnp.bfloat16
f32 = jnp.float32


def gelu_both(values):
    square = values * values
    inner = jnp.tanh(values * (tanh_coeff * cubic_coeff * square + tanh_coeff))
    half = 0.5 * inner + 0.5
    value = values * half
    slope = half + value * (1.0 - inner) * (3.0 * tanh_coeff * cubic_coeff * square + tanh_coeff)
    return value, slope


def dot(left, right):
    return lax.dot_general(
        left, right, (((left.ndim - 1,), (0,)), ((), ())), preferred_element_type=f32
    )


def dot_t(left, right):
    return lax.dot_general(
        left, right, (((left.ndim - 1,), (1,)), ((), ())), preferred_element_type=f32
    )


def dot_tt(left, right):
    return lax.dot_general(left, right, (((0,), (0,)), ((), ())), preferred_element_type=f32)


def outer_sum(left, right):
    return lax.dot_general(
        left.reshape(-1, left.shape[-1]),
        right.reshape(-1, right.shape[-1]),
        (((0,), (0,)), ((), ())),
        preferred_element_type=f32,
    )


def step_route(count, distance):
    return [(i - distance, i) for i in range(count) if 0 <= i - distance < count]


def row_rim(edge, distance):
    return lax.ppermute(edge, ROW, step_route(PARTS, distance))


def col_rim(edge, distance):
    return lax.ppermute(edge, COL, step_route(PARTS, distance))


def diagonal_rim(edge, distance):
    route = [
        ((r - distance) * PARTS + c - distance, r * PARTS + c)
        for r in range(PARTS)
        for c in range(PARTS)
        if 0 <= r - distance < PARTS and 0 <= c - distance < PARTS
    ]
    return lax.ppermute(edge, GRID_AXES, route)


def around(distance):
    place = [y % 4 * 2 + y // 4 for y in range(8)]
    return [(place[y], place[(y + distance) % 8]) for y in range(8)]


def swap_cores(block):
    return lax.ppermute(block, "core", [(0, 1), (1, 0)])


def exchange(block, axes):
    return lax.all_to_all(block, axes, 0, 0, tiled=True)


def spread(block, axes, count):
    return exchange(jnp.broadcast_to(block[None], (count,) + block.shape), axes)


def call(body, name, out_shape, flops, scratch=(), **rest):
    return pl.pallas_call(
        body,
        out_shape=out_shape,
        scratch_shapes=scratch,
        compiler_params=pltpu.CompilerParams(vmem_limit_bytes=24 * 1024 * 1024),
        cost_estimate=pl.CostEstimate(flops=flops, bytes_accessed=8_000_000, transcendentals=0),
        name=name,
        **rest,
    )


def in_place(array):
    return pltpu.with_memory_space_constraint(array, pltpu.HBM)


def shard_kernel(proj_ref, qkv_ref, out_ref, own_ref, sems):
    moves = [
        (proj_ref, own_ref.at[0:128]),
        (qkv_ref.at[:, 0:512], own_ref.at[128:192]),
        (out_ref, own_ref.at[192:224]),
        (qkv_ref.at[0:32, 512:768], own_ref.at[224:256, 0:256]),
        (qkv_ref.at[32:64, 512:768], own_ref.at[224:256, 256:512]),
    ]
    copies = [
        pltpu.make_async_copy(source, target, sems.at[index])
        for index, (source, target) in enumerate(moves)
    ]
    for copy in copies:
        copy.start()
    for copy in copies:
        copy.wait()


def first_transfers(images, w_proj, w_qkv, w_out, cotangent):
    own = call(
        shard_kernel,
        "shard",
        jax.ShapeDtypeStruct((256, 512), bf16),
        1_000_000,
        scratch=[pltpu.SemaphoreType.DMA((5,))],
        in_specs=[pl.BlockSpec(memory_space=pltpu.HBM)] * 3,
    )(in_place(w_proj), in_place(w_qkv), in_place(w_out))
    top = row_rim(images[-1:], 1)
    below = lax.ppermute(own, RING, around(1))
    above = lax.ppermute(own, RING, around(7))
    own, top = lax.optimization_barrier((own, top))
    left = col_rim(jnp.concatenate([top[:, -1:], images[:, -1:]], axis=0), 1)
    far = jnp.concatenate(
        [lax.ppermute(own[:128], RING, around(2)), lax.ppermute(own[128:], RING, around(6))]
    )
    ring = jnp.stack([own, above, far, below])
    ring, left, cotangent = lax.optimization_barrier((ring, left, cotangent))
    return top, left, ring, swap_cores(ring), cotangent


def slot_order():
    order = np.zeros((144, 192), np.float32)
    for row in range(12):
        for col in range(12):
            piece = row % 4 * 2 + col % 4 // 2
            place = row // 4 * 6 + col // 4 * 2 + col % 2
            order[piece * 18 + place, row * 16 + col] = 1.0
    return jnp.asarray(order, bf16)


def unit_order():
    order = np.zeros((576, 576), np.float32)
    filled = [0] * 8
    for source in range(576):
        part_row, part_col, place = source // 144, source % 144 // 18, source % 18
        high_row = (part_row + place // 6) % 2
        high_col = (part_col + place % 6 // 2) % 2
        unit = high_row * 4 + high_col * 2 + place % 2
        order[unit * 72 + filled[unit], source] = 1.0
        filled[unit] += 1
    return jnp.asarray(order, bf16), jnp.asarray(order.T, bf16)


def dot_kt(left, right):
    return lax.dot_general(left, right, (((1,), (1,)), ((), ())), preferred_element_type=f32)


def attention_kernel(tokens_ref, order_ref, home_ref, out_ref, sorted_ref, result_ref):
    scale = 1.0 / math.sqrt(32)
    order = order_ref[...]
    for half in range(2):
        tokens = tokens_ref[4 * half : 4 * half + 4].reshape(576, 128)
        sorted_ref[half] = dot(order, tokens)
    for unit in range(8):
        at = slice(unit * 72, unit * 72 + 72)
        tokens = jnp.concatenate([sorted_ref[0, at], sorted_ref[1, at]], axis=0).astype(bf16)
        query, key, value, d_mix = (tokens[:, 32 * i : 32 * i + 32] for i in range(4))
        raised = jnp.exp(dot_kt(query, key) * scale)
        weights32 = raised * (1.0 / jnp.sum(raised, axis=-1, keepdims=True))
        weights = weights32.astype(bf16)
        mixture = dot(weights, value)
        d_weights = dot_kt(d_mix, value)
        d_value = dot_tt(weights, d_mix)
        d_scores = (
            weights32 * (d_weights - jnp.sum(weights32 * d_weights, axis=-1, keepdims=True))
        ).astype(bf16)
        d_query = dot(d_scores, key) * scale
        d_key = dot_tt(d_scores, query) * scale
        result = jnp.concatenate([d_query, d_key, d_value, mixture], axis=-1)
        result_ref[0, at] = result[:72]
        result_ref[1, at] = result[72:]
    for half in range(2):
        back = dot(home_ref[...], result_ref[half].astype(bf16)).astype(bf16)
        out_ref[4 * half : 4 * half + 4] = back.reshape(4, 144, 128)


def attention(tokens):
    return pl.pallas_call(
        attention_kernel,
        out_shape=jax.ShapeDtypeStruct((8, 144, 128), bf16),
        scratch_shapes=[pltpu.VMEM((2, 576, 128), f32), pltpu.VMEM((2, 576, 128), f32)],
        cost_estimate=pl.CostEstimate(
            flops=6_000_000_000, bytes_accessed=1_000_000, transcendentals=300_000
        ),
        name="attention",
    )(tokens, *unit_order())


def token_mask():
    return lax.broadcasted_iota(jnp.int32, (192, 1), 0) % 16 < 12


def normalize(section):
    wide = section.astype(f32)
    centred = wide - jnp.mean(wide, axis=-1, keepdims=True)
    inv_std = lax.rsqrt(jnp.mean(centred * centred, axis=-1, keepdims=True) + norm_epsilon)
    return centred * inv_std, inv_std


def held(shape, dtype=bf16):
    return pltpu.HBM(shape, dtype)


def expand_kernel(
    images_ref, top_ref, left_ref, w_expand_ref, taps_ref,
    even_ref, odd_ref, slopes_ref, activated_ref, conv_slope_ref, cells_ref, pooled_ref,
    wide_ref, top_wide_ref, left_wide_ref, plane_ref, rows_ref,
):
    @pl.when(pl.program_id(0) == 0)
    def _():
        slot = lax.broadcasted_iota(jnp.int32, (1, 16, 1), 1)
        for half in range(2):
            lanes = slice(128 * half, 128 * half + 128)
            wide_ref[half] = images_ref[:, :, lanes].astype(f32)
            top_wide_ref[half] = top_ref[:, :, lanes].astype(f32)
        left_wide_ref[...] = left_ref[...].astype(f32)
        pooled = 0.0
        for row in range(2):
            for col in range(2):
                plane = 2 * row + col
                plane_ref[...] = jnp.zeros((13, 16, 256), f32)
                for half in range(2):
                    lanes = slice(128 * half, 128 * half + 128)
                    plane_ref[row : row + 12, 0:12, lanes] = wide_ref[
                        half, pl.ds(row, 12, stride=2), pl.ds(col, 12, stride=2), :
                    ]
                    if row:
                        plane_ref[0:1, 0:12, lanes] = top_wide_ref[
                            half, :, pl.ds(col, 12, stride=2), :
                        ]
                if col:
                    plane_ref[row : row + 12, 15:16, :] = left_wide_ref[1:25].reshape(
                        12, 2, 1, 256
                    )[:, row]
                if row and col:
                    plane_ref[0:1, 15:16, :] = left_wide_ref[0:1]
                cells = plane_ref[...]
                rows_ref[plane] = cells.astype(bf16).reshape(208, 256)
                cells = cells[row : row + 12]
                cells_ref[plane] = cells.astype(bf16).reshape(192, 256)
                pooled = pooled + cells
        pooled = jnp.where(slot < 12, pooled * 0.25, 0.0)
        pooled_ref[...] = pooled.astype(bf16).reshape(192, 256)

    taps = [[taps_ref[3 * a + b : 3 * a + b + 1, :].astype(f32) for b in range(3)] for a in range(3)]
    expanded = {}
    for row in range(2):
        for col in range(2):
            count = 192 + 16 * row
            value, slope = gelu_both(dot(rows_ref[2 * row + col, 0:count], w_expand_ref[...]))
            value = value.astype(bf16)
            (odd_ref if row else even_ref)[col] = value
            slopes_ref[2 * row + col] = slope[16 * row :].astype(bf16)
            expanded[row, col] = value.astype(f32).reshape(12 + row, 16, 256)

    def window(row_tap, odd_col):
        plane = expanded[(row_tap + 1) % 2, odd_col]
        return plane[row_tap // 2 : row_tap // 2 + 12]

    straight = sum(
        window(a, 0) * taps[a][1] + window(a, 1) * taps[a][2] for a in range(3)
    )
    moved = sum(window(a, 1) * taps[a][0] for a in range(3))
    value, slope = gelu_both(straight + pltpu.roll(moved, 1, 1))
    activated_ref[...] = value.astype(bf16).reshape(192, 256)
    conv_slope_ref[...] = slope.astype(bf16).reshape(192, 256)


def expand_step(*inputs):
    def chunk(*lead):
        return pl.BlockSpec(lead + (256,), lambda step: (0,) * len(lead) + (step,))

    def whole(*shape):
        return pl.BlockSpec(shape, lambda step: (0,) * len(shape))

    shapes = [
        (2, 192, 1024), (2, 208, 1024), (4, 192, 1024), (192, 1024), (192, 1024), (4, 192, 256),
        (192, 256),
    ]
    return call(
        expand_kernel,
        "expand",
        [held(shape) for shape in shapes],
        6_000_000_000,
        scratch=[
            pltpu.VMEM((2, 24, 24, 128), f32),
            pltpu.VMEM((2, 1, 24, 128), f32),
            pltpu.VMEM((25, 1, 256), f32),
            pltpu.VMEM((13, 16, 256), f32),
            pltpu.VMEM((4, 208, 256), bf16),
        ],
        grid=(4,),
        in_specs=[whole(24, 24, 256), whole(1, 24, 256), whole(25, 1, 256), chunk(256), chunk(9)],
        out_specs=[
            chunk(2, 192), chunk(2, 208), chunk(4, 192), chunk(192), chunk(192),
            whole(4, 192, 256), whole(192, 256),
        ],
    )(*inputs)


def row_buffers():
    return [
        pltpu.VMEM((192, 1024), bf16),
        pltpu.VMEM((192, 256), bf16),
        pltpu.VMEM((192, 512), bf16),
        pltpu.SemaphoreType.DMA((3,)),
    ]


def section_kernel(
    spot_ref, ring_ref, other_ref, activated_in, pooled_in, short_ref, cotangent_in, slots_ref,
    pieces_ref, section_ref, normed_ref, proj_ref, qkv_ref, out_ref,
    activated_ref, pooled_ref, cotangent_ref, sems,
):
    core, y_lo = spot_ref[0], spot_ref[1]
    copies = [
        pltpu.make_async_copy(activated_in, activated_ref, sems.at[0]),
        pltpu.make_async_copy(pooled_in, pooled_ref, sems.at[1]),
        pltpu.make_async_copy(cotangent_in, cotangent_ref, sems.at[2]),
    ]
    for copy in copies:
        copy.start()

    def place(shard, source, at):
        proj_ref[shard * 128 : shard * 128 + 128] = source[at, 0:128]
        qkv_ref[shard * 64 : shard * 64 + 64, 0:512] = source[at, 128:192]
        out_ref[shard * 32 : shard * 32 + 32] = source[at, 192:224]
        qkv_ref[shard * 64 : shard * 64 + 32, 512:768] = source[at, 224:256, 0:256]
        qkv_ref[shard * 64 + 32 : shard * 64 + 64, 512:768] = source[at, 224:256, 256:512]

    for shard in range(8):
        at = lax.rem(shard // 2 - y_lo + 4, 4)
        pl.when(core == shard % 2)(lambda: place(shard, ring_ref, at))
        pl.when(core != shard % 2)(lambda: place(shard, other_ref, at))
    for copy in copies:
        copy.wait()
    section = (
        dot(activated_ref[...], proj_ref[...]) + dot(pooled_ref[...], short_ref[...])
    ).astype(bf16)
    section_ref[...] = section
    normed = jnp.where(token_mask(), normalize(section)[0], 0.0).astype(bf16)
    normed_ref[...] = normed
    packed = dot(normed, qkv_ref[...]).astype(bf16)
    d_mixture = dot_kt(cotangent_ref[...], out_ref[...]).astype(bf16)
    tokens = jnp.concatenate([packed, d_mixture], axis=1)
    tokens = dot(slots_ref[...], tokens).astype(bf16)
    for head in range(HEADS):
        at = [part * 256 + head * 32 for part in range(4)]
        pieces_ref[head] = jnp.concatenate([tokens[:, i : i + 32] for i in at], axis=1)


def section_step(spot, ring, other, activated, pooled, w_short, cotangent, slots):
    inputs = (spot, ring, other, in_place(activated), in_place(pooled), w_short, in_place(cotangent), slots)
    shapes = [(8, 144, 128), (192, 512), (192, 512), (1024, 512), (512, 768), (256, 512)]
    return call(
        section_kernel,
        "section",
        [held(shape) for shape in shapes],
        4_000_000_000,
        scratch=row_buffers(),
        in_specs=[
            pl.BlockSpec(memory_space=space)
            for space in (
                pltpu.SMEM, pltpu.VMEM, pltpu.VMEM, pltpu.HBM, pltpu.HBM, pltpu.VMEM, pltpu.HBM,
                pltpu.VMEM,
            )
        ],
    )(*inputs)[:5]


def back_kernel(
    got_ref, slots_ref, section_ref, cotangent_ref, proj_in, qkv_in, slope_in,
    results_ref, d_section_ref, d_conv_ref, proj_ref, qkv_ref, slope_ref, sems,
):
    copies = [
        pltpu.make_async_copy(qkv_in, qkv_ref, sems.at[0]),
        pltpu.make_async_copy(proj_in, proj_ref, sems.at[1]),
        pltpu.make_async_copy(slope_in, slope_ref, sems.at[2]),
    ]
    for copy in copies:
        copy.start()
    used = token_mask()
    got = [got_ref[head] for head in range(HEADS)]
    got = jnp.concatenate(
        [got[head][:, 32 * part : 32 * part + 32] for part in range(4) for head in range(HEADS)],
        axis=1,
    )
    results = dot_tt(slots_ref[...], got)
    results = jnp.where(used, results, 0.0).astype(bf16)
    results_ref[...] = results
    normalized, inv_std = normalize(section_ref[...])
    copies[0].wait()
    d_normed = dot_kt(results[:, :768], qkv_ref[...])
    d_section = cotangent_ref[...].astype(f32) + inv_std * (
        d_normed
        - jnp.mean(d_normed, axis=-1, keepdims=True)
        - normalized * jnp.mean(d_normed * normalized, axis=-1, keepdims=True)
    )
    d_section = jnp.where(used, d_section, 0.0).astype(bf16)
    d_section_ref[...] = d_section
    copies[1].wait()
    copies[2].wait()
    d_activated = dot_kt(d_section, proj_ref[...])
    d_conv_ref[...] = (d_activated * slope_ref[...].astype(f32)).astype(bf16)


def back_step(got, slots, section, cotangent, proj, qkv, slope):
    shapes = [(192, 1024), (192, 512), (192, 1024)]
    return call(
        back_kernel,
        "back",
        [jax.ShapeDtypeStruct(shape, bf16) for shape in shapes],
        1_500_000_000,
        scratch=[
            pltpu.VMEM((1024, 512), bf16),
            pltpu.VMEM((512, 768), bf16),
            pltpu.VMEM((192, 1024), bf16),
            pltpu.SemaphoreType.DMA((3,)),
        ],
        in_specs=[pl.BlockSpec(memory_space=pltpu.VMEM)] * 4
        + [pl.BlockSpec(memory_space=pltpu.HBM)] * 3,
    )(got, slots, section, cotangent, in_place(proj), in_place(qkv), in_place(slope))


def parts_kernel(
    results_ref, d_section_ref, normed_ref, cotangent_in, activated_in, pooled_in, short_ref,
    early_ref, d_pooled_ref, activated_ref, pooled_ref, cotangent_ref, sems,
):
    copies = [
        pltpu.make_async_copy(activated_in, activated_ref, sems.at[0]),
        pltpu.make_async_copy(pooled_in, pooled_ref, sems.at[1]),
        pltpu.make_async_copy(cotangent_in, cotangent_ref, sems.at[2]),
    ]
    for copy in copies:
        copy.start()
    results = results_ref[...]
    d_section = d_section_ref[...]

    def store(part, first, rows):
        lanes = part.shape[1] // 128
        for shard in range(8):
            for piece in range(rows // 16 * lanes):
                row = shard * rows + piece // lanes * 16
                lane = piece % lanes * 128
                index = first + piece
                at = shard // 2 * 32 + index % 2 * 16
                early_ref[shard % 2, index // 2, at : at + 16, :] = part[
                    row : row + 16, lane : lane + 128
                ]

    store(dot_tt(normed_ref[...], results[:, :768]).astype(bf16), 32, 64)
    for copy in copies:
        copy.wait()
    store(dot_tt(activated_ref[...], d_section).astype(bf16), 0, 128)
    store(dot_tt(results[:, 768:], cotangent_ref[...]).astype(bf16), 56, 32)
    short = dot_tt(pooled_ref[...], d_section)
    rows = [short[:, lane * 128 : lane * 128 + 128].reshape(32, 8, 128) for lane in range(4)]
    for core in range(2):
        early_ref[core, :, 128:144, :] = jnp.concatenate(
            [rows[2 * core], rows[2 * core + 1]], axis=1
        ).astype(bf16)
    d_pooled_ref[...] = dot_kt(d_section, short_ref[...]) * 0.25


def parts_step(results, d_section, normed, cotangent, activated, pooled, w_short):
    inputs = (results, d_section, normed, in_place(cotangent), in_place(activated), in_place(pooled), w_short)
    return call(
        parts_kernel,
        "parts",
        [
            jax.ShapeDtypeStruct((2, 32, 144, 128), bf16),
            jax.ShapeDtypeStruct((192, 256), f32),
        ],
        1_000_000_000,
        scratch=row_buffers(),
        in_specs=[
            pl.BlockSpec(memory_space=space)
            for space in (
                pltpu.VMEM, pltpu.VMEM, pltpu.VMEM, pltpu.HBM, pltpu.HBM, pltpu.HBM, pltpu.VMEM,
            )
        ],
    )(*inputs)


def pixel_kernel(
    d_conv_ref, below_ref, right_ref, even_ref, odd_ref, slopes_ref, cells_ref, w_expand_ref,
    taps_ref, d_pooled_ref, image_ref, expand_ref, depth_ref, total_ref,
):
    slot = lax.broadcasted_iota(jnp.int32, (1, 16, 1), 1)
    row_terms = {0: ((1, 0),), 1: ((2, 0), (0, 1))}
    for step in range(4):
        lanes = slice(step * 256, step * 256 + 256)
        here = d_conv_ref[:, lanes].astype(f32).reshape(12, 16, 256)
        rows = jnp.concatenate([here, below_ref[:, :, lanes].astype(f32)], axis=0)
        turned = pltpu.roll(rows, 15, 1)
        after = jnp.where(slot == 11, right_ref[:, :, lanes].astype(f32), turned)
        back = turned[:12]
        taps = [
            [taps_ref[3 * a + b : 3 * a + b + 1, lanes].astype(f32) for b in range(3)]
            for a in range(3)
        ]

        def window(row_tap, odd_col):
            source = even_ref if row_tap == 1 else odd_ref
            first = 16 * (row_tap // 2) if row_tap != 1 else 0
            return source[odd_col, first : first + 192, lanes].astype(f32).reshape(12, 16, 256)

        for a in range(3):
            odd = window(a, 1)
            even = window(a, 0)
            for b, product in ((0, odd * back), (1, even * here), (2, odd * here)):
                total = jnp.sum(jnp.sum(product, axis=0), axis=0, keepdims=True)
                depth_ref[3 * a + b : 3 * a + b + 1, lanes] = total
        col_terms = {0: ((1, rows),), 1: ((2, rows), (0, after))}
        part_expand = 0.0
        for row in range(2):
            for col in range(2):
                d_cells = sum(
                    source[i : i + 12] * taps[a][b]
                    for a, i in row_terms[row]
                    for b, source in col_terms[col]
                )
                d_cells = jnp.where(slot < 12, d_cells, 0.0).reshape(192, 256)
                plane = row * 2 + col
                d_pre = (d_cells * slopes_ref[plane, :, lanes].astype(f32)).astype(bf16)
                part_expand = part_expand + dot_tt(cells_ref[plane], d_pre)
                back_image = dot_kt(d_pre, w_expand_ref[:, lanes])
                so_far = d_pooled_ref[...] if step == 0 else total_ref[plane]
                if step < 3:
                    total_ref[plane] = so_far + back_image
                else:
                    image_ref[plane] = (so_far + back_image).astype(bf16)
        expand_ref[step // 2, :, step % 2 * 16 : step % 2 * 16 + 16] = jnp.concatenate(
            [part_expand[:, :128].reshape(32, 8, 128), part_expand[:, 128:].reshape(32, 8, 128)],
            axis=1,
        ).astype(bf16)


def pixel_step(*inputs):
    return call(
        pixel_kernel,
        "pixel",
        [
            jax.ShapeDtypeStruct((4, 192, 256), bf16),
            jax.ShapeDtypeStruct((2, 32, 32, 128), bf16),
            jax.ShapeDtypeStruct((16, 1024), f32),
        ],
        6_000_000_000,
        scratch=[pltpu.VMEM((4, 192, 256), f32)],
    )(*inputs)


def untiled(pieces, rows, columns):
    height = pieces.shape[1]
    cut = pieces.reshape(rows // height, columns // 128, height, 128)
    return cut.transpose(0, 2, 1, 3).reshape(rows, columns).astype(f32)


def pair_sum(halves):
    core = lax.axis_index("core")
    mine = lax.dynamic_index_in_dim(halves, core, 0, keepdims=False)
    theirs = lax.dynamic_index_in_dim(halves, 1 - core, 0, keepdims=False)
    return (mine.astype(f32) + swap_cores(theirs).astype(f32)).astype(bf16)


def all_sums(early, expand, depth):
    depth = jnp.pad(depth[:9].astype(bf16).reshape(9, 8, 128), ((0, 23), (0, 0), (0, 0)))
    core = lax.axis_index("core")

    def share(of):
        own = lax.dynamic_index_in_dim(expand, of, 0, keepdims=False)
        return jnp.concatenate([own, jnp.where(of == 0, depth, jnp.zeros((), bf16))], axis=1)

    late = (share(core).astype(f32) + swap_cores(share(1 - core)).astype(f32)).astype(bf16)
    pair = jnp.concatenate([early, late], axis=1)
    line = jnp.sum(exchange(pair, "x").reshape(4, 8, 184, 128).astype(f32), axis=0).astype(bf16)
    sheet = jnp.sum(exchange(line, "z").astype(f32), axis=0).astype(bf16)
    column = jnp.concatenate(
        [sheet[:128].reshape(4, 32, 128), jnp.broadcast_to(sheet[None, 128:], (4, 56, 128))], axis=1
    )
    column = jnp.broadcast_to(column[:, None], (4, 2, 88, 128)).reshape(8, 88, 128)
    grad_scale = 1.0 / math.sqrt(8 * 96 * 96)
    total = jnp.sum(exchange(column, RING).astype(f32), axis=0) * grad_scale
    near = spread(total.astype(bf16), ("x", "z"), 32)
    own = near[:, 32:]
    other = swap_cores(own)
    matrix = near[:, :32].reshape(64, 16, 128)
    grad_proj = untiled(matrix[:32], 128, 512)
    grad_qkv = untiled(matrix[32:56], 64, 768)
    grad_out = untiled(matrix[56:], 32, 512)
    first = lax.axis_index("core") == 0
    both = jnp.where(first, jnp.stack([own, other]), jnp.stack([other, own]))

    def joined(start, count):
        part = both[:, :, start : start + 8 * count].reshape(2, 32, count, 8, 128)
        return part.transpose(1, 3, 0, 2, 4).reshape(256, 256 * count).astype(f32)

    grad_short = joined(0, 2)
    grad_expand = joined(16, 4)
    grad_depth = both[0, :9, 48:].reshape(3, 3, 1024).astype(f32)
    return grad_expand, grad_depth, grad_short, grad_proj, grad_qkv, grad_out


def slots16(cells):
    return jnp.pad(cells, ((0, 0), (0, 4), (0, 0)))


def on_device(images, w_expand, w_depth, w_short, w_proj, w_qkv, w_out, cotangent):
    images = images[0]
    cotangent = slots16(cotangent[0])
    top, left, ring, other, cotangent = first_transfers(images, w_proj, w_qkv, w_out, cotangent)
    slots = slot_order()
    taps = w_depth.reshape(9, 1024)
    even, odd, slopes, activated, conv_slope, cells, pooled = expand_step(
        images, top, left, w_expand, taps
    )
    cotangent = cotangent.reshape(192, 512)
    spot = jnp.stack([lax.axis_index("core"), lax.axis_index("ylo")]).astype(jnp.int32)
    pieces, section_out, normed, proj, qkv = section_step(
        spot, ring, other, activated, pooled, w_short, cotangent, slots
    )
    got = exchange(pieces.reshape(64, 9, 2, 128), GRID_AXES)
    mixed = attention(got.reshape(8, 144, 128))
    got = exchange(mixed.reshape(64, 9, 2, 128), GRID_AXES).reshape(HEADS, 144, 128)
    results, d_section, d_conv = back_step(
        got, slots, section_out, cotangent, proj, qkv, conv_slope
    )
    below = row_rim(d_conv[:12].reshape(1, 12, 1024), -1)
    edge = d_conv.reshape(12, 16, 1024)[:, :1]
    right = jnp.concatenate([col_rim(edge, -1), diagonal_rim(edge[:1], -1)], axis=0)
    early, d_pooled = parts_step(
        results, d_section, normed, cotangent, activated, pooled, w_short
    )
    early = pair_sum(early)
    image, expand, depth = pixel_step(
        d_conv, slots16(below), right, even, odd, slopes, cells, w_expand, taps,
        d_pooled,
    )
    image = image.reshape(2, 2, 12, 16, 256)[:, :, :, :12]
    grad_image = image.transpose(2, 0, 3, 1, 4).reshape(1, 24, 24, 256)
    return (grad_image,) + all_sums(early, expand, depth)


def solution(mesh):
    fine = Mesh(mesh.devices.reshape(4, 2, 2, 4, 8), ("ylo", "core", "yhi", "x", "z"))
    cells = P(SAMPLE, ROW, COL, None)
    rows = P(SAMPLE, None)
    return jax.shard_map(
        on_device,
        mesh=fine,
        in_specs=(cells, P(), P(), P(), rows, rows, rows, cells),
        out_specs=(cells, P(), P(), P(), rows, rows, rows),
        check_vma=False,
    )
```

```python
import math

import jax
import jax.numpy as jnp
import numpy as np
from jax import lax
from jax.experimental import pallas as pl
from jax.experimental.pallas import tpu as pltpu
from jax.sharding import Mesh
from jax.sharding import PartitionSpec as P

HEADS = 8
PARTS = 8

SAMPLE = ("ylo", "core")
ROW = ("yhi", "x")
COL = "z"
GRID_AXES = ("yhi", "x", "z")
CHIPS = ("ylo", "yhi", "x", "z")
RING = ("ylo", "yhi")

norm_epsilon = 1e-05
tanh_coeff = 0.7978845608028654
cubic_coeff = 0.044715

bf16 = jnp.bfloat16
f32 = jnp.float32


def gelu_both(values):
    square = values * values
    inner = jnp.tanh(values * (tanh_coeff * cubic_coeff * square + tanh_coeff))
    half = 0.5 * inner + 0.5
    value = values * half
    slope = half + value * (1.0 - inner) * (3.0 * tanh_coeff * cubic_coeff * square + tanh_coeff)
    return value, slope


def dot(left, right):
    return lax.dot_general(
        left, right, (((left.ndim - 1,), (0,)), ((), ())), preferred_element_type=f32
    )


def dot_t(left, right):
    return lax.dot_general(
        left, right, (((left.ndim - 1,), (1,)), ((), ())), preferred_element_type=f32
    )


def dot_tt(left, right):
    return lax.dot_general(left, right, (((0,), (0,)), ((), ())), preferred_element_type=f32)


def outer_sum(left, right):
    return lax.dot_general(
        left.reshape(-1, left.shape[-1]),
        right.reshape(-1, right.shape[-1]),
        (((0,), (0,)), ((), ())),
        preferred_element_type=f32,
    )


def step_route(count, distance):
    return [(i - distance, i) for i in range(count) if 0 <= i - distance < count]


def row_rim(edge, distance):
    return lax.ppermute(edge, ROW, step_route(PARTS, distance))


def col_rim(edge, distance):
    return lax.ppermute(edge, COL, step_route(PARTS, distance))


def diagonal_rim(edge, distance):
    route = [
        ((r - distance) * PARTS + c - distance, r * PARTS + c)
        for r in range(PARTS)
        for c in range(PARTS)
        if 0 <= r - distance < PARTS and 0 <= c - distance < PARTS
    ]
    return lax.ppermute(edge, GRID_AXES, route)


def around(distance):
    place = [y % 4 * 2 + y // 4 for y in range(8)]
    return [(place[y], place[(y + distance) % 8]) for y in range(8)]


def swap_cores(block):
    return lax.ppermute(block, "core", [(0, 1), (1, 0)])


def exchange(block, axes):
    return lax.all_to_all(block, axes, 0, 0, tiled=True)


def spread(block, axes, count):
    return exchange(jnp.broadcast_to(block[None], (count,) + block.shape), axes)


def call(body, name, out_shape, flops, scratch=(), **rest):
    return pl.pallas_call(
        body,
        out_shape=out_shape,
        scratch_shapes=scratch,
        compiler_params=pltpu.CompilerParams(vmem_limit_bytes=24 * 1024 * 1024),
        cost_estimate=pl.CostEstimate(flops=flops, bytes_accessed=8_000_000, transcendentals=0),
        name=name,
        **rest,
    )


def in_place(array):
    return pltpu.with_memory_space_constraint(array, pltpu.HBM)


def shard_kernel(proj_ref, qkv_ref, out_ref, own_ref, sems):
    moves = [
        (proj_ref, own_ref.at[0:128]),
        (qkv_ref.at[:, 0:512], own_ref.at[128:192]),
        (out_ref, own_ref.at[192:224]),
        (qkv_ref.at[0:32, 512:768], own_ref.at[224:256, 0:256]),
        (qkv_ref.at[32:64, 512:768], own_ref.at[224:256, 256:512]),
    ]
    copies = [
        pltpu.make_async_copy(source, target, sems.at[index])
        for index, (source, target) in enumerate(moves)
    ]
    for copy in copies:
        copy.start()
    for copy in copies:
        copy.wait()


def first_transfers(images, w_proj, w_qkv, w_out):
    own = call(
        shard_kernel,
        "shard",
        jax.ShapeDtypeStruct((256, 512), bf16),
        1_000_000,
        scratch=[pltpu.SemaphoreType.DMA((5,))],
        in_specs=[pl.BlockSpec(memory_space=pltpu.HBM)] * 3,
    )(in_place(w_proj), in_place(w_qkv), in_place(w_out))
    top = row_rim(images[-1:], 1)
    below = lax.ppermute(own, RING, around(1))
    above = lax.ppermute(own, RING, around(7))
    own, top = lax.optimization_barrier((own, top))
    left = col_rim(jnp.concatenate([top[:, -1:], images[:, -1:]], axis=0), 1)
    far = jnp.concatenate(
        [lax.ppermute(own[:128], RING, around(2)), lax.ppermute(own[128:], RING, around(6))]
    )
    ring = jnp.stack([own, above, far, below])
    ring, left = lax.optimization_barrier((ring, left))
    return top, left, ring, swap_cores(ring)


def slot_order():
    order = np.zeros((144, 192), np.float32)
    for row in range(12):
        for col in range(12):
            piece = row % 4 * 2 + col % 4 // 2
            place = row // 4 * 6 + col // 4 * 2 + col % 2
            order[piece * 18 + place, row * 16 + col] = 1.0
    return jnp.asarray(order, bf16)


def unit_order():
    order = np.zeros((576, 576), np.float32)
    filled = [0] * 8
    for source in range(576):
        part_row, part_col, place = source // 144, source % 144 // 18, source % 18
        high_row = (part_row + place // 6) % 2
        high_col = (part_col + place % 6 // 2) % 2
        unit = high_row * 4 + high_col * 2 + place % 2
        order[unit * 72 + filled[unit], source] = 1.0
        filled[unit] += 1
    return jnp.asarray(order, bf16)


def dot_kt(left, right):
    return lax.dot_general(left, right, (((1,), (1,)), ((), ())), preferred_element_type=f32)


def attention_kernel(tokens_ref, order_ref, out_ref, sorted_ref, result_ref):
    scale = 1.0 / math.sqrt(32)
    order = order_ref[...]
    for half in range(2):
        tokens = tokens_ref[4 * half : 4 * half + 4].reshape(576, 128)
        sorted_ref[half] = dot(order, tokens)
    for first in (0, 4):
        spots = [slice(unit * 72, unit * 72 + 72) for unit in range(first, first + 4)]
        units = [
            jnp.concatenate([sorted_ref[0, at], sorted_ref[1, at]], axis=0).astype(bf16)
            for at in spots
        ]
        cut = [[unit[:, 32 * i : 32 * i + 32] for i in range(4)] for unit in units]
        scores = [dot_kt(query, key) for query, key, _, _ in cut]
        d_weights = [dot_kt(d_mix, value) for _, _, value, d_mix in cut]
        raised = [jnp.exp(score * scale) for score in scores]
        totals = [1.0 / jnp.sum(part, axis=-1, keepdims=True) for part in raised]
        weights32 = [part * total for part, total in zip(raised, totals)]
        weights = [part.astype(bf16) for part in weights32]
        mixture = [dot(part, heads[2]) for part, heads in zip(weights, cut)]
        d_value = [dot_tt(part, heads[3]) for part, heads in zip(weights, cut)]
        inner = [
            jnp.sum(part * back, axis=-1, keepdims=True)
            for part, back in zip(weights32, d_weights)
        ]
        d_scores = [
            (part * (back - total)).astype(bf16)
            for part, back, total in zip(weights32, d_weights, inner)
        ]
        d_query = [dot(part, heads[1]) * scale for part, heads in zip(d_scores, cut)]
        d_key = [dot_tt(part, heads[0]) * scale for part, heads in zip(d_scores, cut)]
        for index, at in enumerate(spots):
            result = jnp.concatenate(
                [d_query[index], d_key[index], d_value[index], mixture[index]], axis=-1
            )
            result_ref[0, at] = result[:72]
            result_ref[1, at] = result[72:]
    for half in range(2):
        back = dot_tt(order, result_ref[half].astype(bf16)).astype(bf16)
        out_ref[4 * half : 4 * half + 4] = back.reshape(4, 144, 128)


def attention(tokens):
    return pl.pallas_call(
        attention_kernel,
        out_shape=jax.ShapeDtypeStruct((8, 144, 128), bf16),
        scratch_shapes=[pltpu.VMEM((2, 576, 128), f32), pltpu.VMEM((2, 576, 128), f32)],
        cost_estimate=pl.CostEstimate(
            flops=6_000_000_000, bytes_accessed=1_000_000, transcendentals=300_000
        ),
        name="attention",
    )(tokens, unit_order())


def token_mask():
    return lax.broadcasted_iota(jnp.int32, (192, 1), 0) % 16 < 12


def normalize(section):
    wide = section.astype(f32)
    centred = wide - jnp.mean(wide, axis=-1, keepdims=True)
    inv_std = lax.rsqrt(jnp.mean(centred * centred, axis=-1, keepdims=True) + norm_epsilon)
    return centred * inv_std, inv_std


def held(shape, dtype=bf16):
    return pltpu.HBM(shape, dtype)


def expand_kernel(
    images_ref, top_ref, left_ref, w_expand_ref, taps_ref,
    even_ref, odd_ref, slopes_ref, activated_ref, conv_slope_ref, cells_ref, pooled_ref,
    wide_ref, top_wide_ref, left_wide_ref, plane_ref, rows_ref,
):
    @pl.when(pl.program_id(0) == 0)
    def _():
        slot = lax.broadcasted_iota(jnp.int32, (1, 16, 1), 1)
        for half in range(2):
            lanes = slice(128 * half, 128 * half + 128)
            wide_ref[half] = images_ref[:, :, lanes].astype(f32)
            top_wide_ref[half] = top_ref[:, :, lanes].astype(f32)
        left_wide_ref[...] = left_ref[...].astype(f32)
        pooled = 0.0
        for row in range(2):
            for col in range(2):
                plane = 2 * row + col
                plane_ref[...] = jnp.zeros((13, 16, 256), f32)
                for half in range(2):
                    lanes = slice(128 * half, 128 * half + 128)
                    plane_ref[row : row + 12, 0:12, lanes] = wide_ref[
                        half, pl.ds(row, 12, stride=2), pl.ds(col, 12, stride=2), :
                    ]
                    if row:
                        plane_ref[0:1, 0:12, lanes] = top_wide_ref[
                            half, :, pl.ds(col, 12, stride=2), :
                        ]
                if col:
                    plane_ref[row : row + 12, 15:16, :] = left_wide_ref[1:25].reshape(
                        12, 2, 1, 256
                    )[:, row]
                if row and col:
                    plane_ref[0:1, 15:16, :] = left_wide_ref[0:1]
                cells = plane_ref[...]
                rows_ref[plane] = cells.astype(bf16).reshape(208, 256)
                cells = cells[row : row + 12]
                cells_ref[plane] = cells.astype(bf16).reshape(192, 256)
                pooled = pooled + cells
        pooled = jnp.where(slot < 12, pooled * 0.25, 0.0)
        pooled_ref[...] = pooled.astype(bf16).reshape(192, 256)

    taps = [[taps_ref[3 * a + b : 3 * a + b + 1, :].astype(f32) for b in range(3)] for a in range(3)]
    expanded = {}
    for row in range(2):
        for col in range(2):
            count = 192 + 16 * row
            value, slope = gelu_both(dot(rows_ref[2 * row + col, 0:count], w_expand_ref[...]))
            value = value.astype(bf16)
            (odd_ref if row else even_ref)[col] = value
            slopes_ref[2 * row + col] = slope[16 * row :].astype(bf16)
            expanded[row, col] = value.astype(f32).reshape(12 + row, 16, 256)

    def window(row_tap, odd_col):
        plane = expanded[(row_tap + 1) % 2, odd_col]
        return plane[row_tap // 2 : row_tap // 2 + 12]

    straight = sum(
        window(a, 0) * taps[a][1] + window(a, 1) * taps[a][2] for a in range(3)
    )
    moved = sum(window(a, 1) * taps[a][0] for a in range(3))
    value, slope = gelu_both(straight + pltpu.roll(moved, 1, 1))
    activated_ref[...] = value.astype(bf16).reshape(192, 256)
    conv_slope_ref[...] = slope.astype(bf16).reshape(192, 256)


def expand_step(*inputs):
    def chunk(*lead):
        return pl.BlockSpec(lead + (256,), lambda step: (0,) * len(lead) + (step,))

    def whole(*shape):
        return pl.BlockSpec(shape, lambda step: (0,) * len(shape))

    shapes = [
        (2, 192, 1024), (2, 208, 1024), (4, 192, 1024), (192, 1024), (192, 1024), (4, 192, 256),
        (192, 256),
    ]
    return call(
        expand_kernel,
        "expand",
        [held(shape) for shape in shapes],
        6_000_000_000,
        scratch=[
            pltpu.VMEM((2, 24, 24, 128), f32),
            pltpu.VMEM((2, 1, 24, 128), f32),
            pltpu.VMEM((25, 1, 256), f32),
            pltpu.VMEM((13, 16, 256), f32),
            pltpu.VMEM((4, 208, 256), bf16),
        ],
        grid=(4,),
        in_specs=[whole(24, 24, 256), whole(1, 24, 256), whole(25, 1, 256), chunk(256), chunk(9)],
        out_specs=[
            chunk(2, 192), chunk(2, 208), chunk(4, 192), chunk(192), chunk(192),
            whole(4, 192, 256), whole(192, 256),
        ],
    )(*inputs)


def row_buffers():
    return [
        pltpu.VMEM((192, 1024), bf16),
        pltpu.VMEM((192, 256), bf16),
        pltpu.VMEM((192, 512), bf16),
        pltpu.SemaphoreType.DMA((3,)),
    ]


def section_kernel(
    spot_ref, ring_ref, other_ref, activated_in, pooled_in, short_ref, cotangent_in, slots_ref,
    pieces_ref, section_ref, normed_ref, proj_ref, qkv_ref, out_ref,
    activated_ref, pooled_ref, cotangent_ref, sems,
):
    core, y_lo = spot_ref[0], spot_ref[1]
    copies = [
        pltpu.make_async_copy(activated_in, activated_ref, sems.at[0]),
        pltpu.make_async_copy(pooled_in, pooled_ref, sems.at[1]),
        pltpu.make_async_copy(cotangent_in, cotangent_ref, sems.at[2]),
    ]
    for copy in copies:
        copy.start()

    def place(shard, source, at):
        proj_ref[shard * 128 : shard * 128 + 128] = source[at, 0:128]
        qkv_ref[shard * 64 : shard * 64 + 64, 0:512] = source[at, 128:192]
        out_ref[shard * 32 : shard * 32 + 32] = source[at, 192:224]
        qkv_ref[shard * 64 : shard * 64 + 32, 512:768] = source[at, 224:256, 0:256]
        qkv_ref[shard * 64 + 32 : shard * 64 + 64, 512:768] = source[at, 224:256, 256:512]

    for shard in range(8):
        at = lax.rem(shard // 2 - y_lo + 4, 4)
        pl.when(core == shard % 2)(lambda: place(shard, ring_ref, at))
        pl.when(core != shard % 2)(lambda: place(shard, other_ref, at))
    for copy in copies:
        copy.wait()
    section = (
        dot(activated_ref[...], proj_ref[...]) + dot(pooled_ref[...], short_ref[...])
    ).astype(bf16)
    section_ref[...] = section
    normed = jnp.where(token_mask(), normalize(section)[0], 0.0).astype(bf16)
    normed_ref[...] = normed
    packed = dot(normed, qkv_ref[...]).astype(bf16)
    d_mixture = dot_kt(cotangent_ref[...], out_ref[...]).astype(bf16)
    tokens = jnp.concatenate([packed, d_mixture], axis=1)
    tokens = dot(slots_ref[...], tokens).astype(bf16)
    for head in range(HEADS):
        at = [part * 256 + head * 32 for part in range(4)]
        pieces_ref[head] = jnp.concatenate([tokens[:, i : i + 32] for i in at], axis=1)


def section_step(spot, ring, other, activated, pooled, w_short, cotangent, slots):
    inputs = (spot, ring, other, in_place(activated), in_place(pooled), w_short, in_place(cotangent), slots)
    shapes = [(8, 144, 128), (192, 512), (192, 512), (1024, 512), (512, 768), (256, 512)]
    return call(
        section_kernel,
        "section",
        [held(shape) for shape in shapes],
        4_000_000_000,
        scratch=row_buffers(),
        in_specs=[
            pl.BlockSpec(memory_space=space)
            for space in (
                pltpu.SMEM, pltpu.VMEM, pltpu.VMEM, pltpu.HBM, pltpu.HBM, pltpu.VMEM, pltpu.HBM,
                pltpu.VMEM,
            )
        ],
    )(*inputs)[:5]


def back_kernel(
    got_ref, slots_ref, section_ref, cotangent_ref, proj_in, qkv_in, slope_in,
    results_ref, d_section_ref, d_conv_ref, proj_ref, qkv_ref, slope_ref, sems,
):
    copies = [
        pltpu.make_async_copy(qkv_in, qkv_ref, sems.at[0]),
        pltpu.make_async_copy(proj_in, proj_ref, sems.at[1]),
        pltpu.make_async_copy(slope_in, slope_ref, sems.at[2]),
    ]
    for copy in copies:
        copy.start()
    used = token_mask()
    got = [got_ref[head] for head in range(HEADS)]
    got = jnp.concatenate(
        [got[head][:, 32 * part : 32 * part + 32] for part in range(4) for head in range(HEADS)],
        axis=1,
    )
    results = dot_tt(slots_ref[...], got)
    results = jnp.where(used, results, 0.0).astype(bf16)
    results_ref[...] = results
    normalized, inv_std = normalize(section_ref[...])
    copies[0].wait()
    d_normed = dot_kt(results[:, :768], qkv_ref[...])
    d_section = cotangent_ref[...].astype(f32) + inv_std * (
        d_normed
        - jnp.mean(d_normed, axis=-1, keepdims=True)
        - normalized * jnp.mean(d_normed * normalized, axis=-1, keepdims=True)
    )
    d_section = jnp.where(used, d_section, 0.0).astype(bf16)
    d_section_ref[...] = d_section
    copies[1].wait()
    copies[2].wait()
    d_activated = dot_kt(d_section, proj_ref[...])
    d_conv_ref[...] = (d_activated * slope_ref[...].astype(f32)).astype(bf16)


def back_step(got, slots, section, cotangent, proj, qkv, slope):
    shapes = [(192, 1024), (192, 512), (192, 1024)]
    return call(
        back_kernel,
        "back",
        [jax.ShapeDtypeStruct(shape, bf16) for shape in shapes],
        1_500_000_000,
        scratch=[
            pltpu.VMEM((1024, 512), bf16),
            pltpu.VMEM((512, 768), bf16),
            pltpu.VMEM((192, 1024), bf16),
            pltpu.SemaphoreType.DMA((3,)),
        ],
        in_specs=[pl.BlockSpec(memory_space=pltpu.VMEM)] * 4
        + [pl.BlockSpec(memory_space=pltpu.HBM)] * 3,
    )(got, slots, section, cotangent, in_place(proj), in_place(qkv), in_place(slope))


def parts_kernel(
    results_ref, d_section_ref, normed_ref, cotangent_in, activated_in, pooled_in, short_ref,
    early_ref, d_pooled_ref, activated_ref, pooled_ref, cotangent_ref, sems,
):
    copies = [
        pltpu.make_async_copy(activated_in, activated_ref, sems.at[0]),
        pltpu.make_async_copy(pooled_in, pooled_ref, sems.at[1]),
        pltpu.make_async_copy(cotangent_in, cotangent_ref, sems.at[2]),
    ]
    for copy in copies:
        copy.start()
    results = results_ref[...]
    d_section = d_section_ref[...]

    def store(part, first, rows):
        lanes = part.shape[1] // 128
        for shard in range(8):
            for piece in range(rows // 16 * lanes):
                row = shard * rows + piece // lanes * 16
                lane = piece % lanes * 128
                index = first + piece
                at = shard // 2 * 32 + index % 2 * 16
                early_ref[shard % 2, index // 2, at : at + 16, :] = part[
                    row : row + 16, lane : lane + 128
                ]

    store(dot_tt(normed_ref[...], results[:, :768]).astype(bf16), 32, 64)
    for copy in copies:
        copy.wait()
    store(dot_tt(activated_ref[...], d_section).astype(bf16), 0, 128)
    store(dot_tt(results[:, 768:], cotangent_ref[...]).astype(bf16), 56, 32)
    short = dot_tt(pooled_ref[...], d_section)
    rows = [short[:, lane * 128 : lane * 128 + 128].reshape(32, 8, 128) for lane in range(4)]
    for core in range(2):
        early_ref[core, :, 128:144, :] = jnp.concatenate(
            [rows[2 * core], rows[2 * core + 1]], axis=1
        ).astype(bf16)
    d_pooled_ref[...] = dot_kt(d_section, short_ref[...]) * 0.25


def parts_step(results, d_section, normed, cotangent, activated, pooled, w_short):
    inputs = (results, d_section, normed, in_place(cotangent), in_place(activated), in_place(pooled), w_short)
    return call(
        parts_kernel,
        "parts",
        [
            jax.ShapeDtypeStruct((2, 32, 144, 128), bf16),
            jax.ShapeDtypeStruct((192, 256), f32),
        ],
        1_000_000_000,
        scratch=row_buffers(),
        in_specs=[
            pl.BlockSpec(memory_space=space)
            for space in (
                pltpu.VMEM, pltpu.VMEM, pltpu.VMEM, pltpu.HBM, pltpu.HBM, pltpu.HBM, pltpu.VMEM,
            )
        ],
    )(*inputs)


def pixel_kernel(
    d_conv_ref, below_ref, right_ref, even_ref, odd_ref, slopes_ref, cells_ref, w_expand_ref,
    taps_ref, d_pooled_ref, image_ref, expand_ref, depth_ref, total_ref,
):
    slot = lax.broadcasted_iota(jnp.int32, (1, 16, 1), 1)
    row_terms = {0: ((1, 0),), 1: ((2, 0), (0, 1))}
    for step in range(4):
        lanes = slice(step * 256, step * 256 + 256)
        here = d_conv_ref[:, lanes].astype(f32).reshape(12, 16, 256)
        rows = jnp.concatenate([here, below_ref[:, :, lanes].astype(f32)], axis=0)
        turned = pltpu.roll(rows, 15, 1)
        after = jnp.where(slot == 11, right_ref[:, :, lanes].astype(f32), turned)
        back = turned[:12]
        taps = [
            [taps_ref[3 * a + b : 3 * a + b + 1, lanes].astype(f32) for b in range(3)]
            for a in range(3)
        ]

        def window(row_tap, odd_col):
            source = even_ref if row_tap == 1 else odd_ref
            first = 16 * (row_tap // 2) if row_tap != 1 else 0
            return source[odd_col, first : first + 192, lanes].astype(f32).reshape(12, 16, 256)

        for a in range(3):
            odd = window(a, 1)
            even = window(a, 0)
            for b, product in ((0, odd * back), (1, even * here), (2, odd * here)):
                total = jnp.sum(jnp.sum(product, axis=0), axis=0, keepdims=True)
                depth_ref[3 * a + b : 3 * a + b + 1, lanes] = total
        col_terms = {0: ((1, rows),), 1: ((2, rows), (0, after))}
        part_expand = 0.0
        for row in range(2):
            for col in range(2):
                d_cells = sum(
                    source[i : i + 12] * taps[a][b]
                    for a, i in row_terms[row]
                    for b, source in col_terms[col]
                )
                d_cells = jnp.where(slot < 12, d_cells, 0.0).reshape(192, 256)
                plane = row * 2 + col
                d_pre = (d_cells * slopes_ref[plane, :, lanes].astype(f32)).astype(bf16)
                part_expand = part_expand + dot_tt(cells_ref[plane], d_pre)
                back_image = dot_kt(d_pre, w_expand_ref[:, lanes])
                so_far = d_pooled_ref[...] if step == 0 else total_ref[plane]
                if step < 3:
                    total_ref[plane] = so_far + back_image
                else:
                    image_ref[plane] = (so_far + back_image).astype(bf16)
        expand_ref[step // 2, :, step % 2 * 16 : step % 2 * 16 + 16] = jnp.concatenate(
            [part_expand[:, :128].reshape(32, 8, 128), part_expand[:, 128:].reshape(32, 8, 128)],
            axis=1,
        ).astype(bf16)


def pixel_step(*inputs):
    return call(
        pixel_kernel,
        "pixel",
        [
            jax.ShapeDtypeStruct((4, 192, 256), bf16),
            jax.ShapeDtypeStruct((2, 32, 32, 128), bf16),
            jax.ShapeDtypeStruct((16, 1024), f32),
        ],
        6_000_000_000,
        scratch=[pltpu.VMEM((4, 192, 256), f32)],
    )(*inputs)


def untiled(pieces, rows, columns):
    height = pieces.shape[1]
    cut = pieces.reshape(rows // height, columns // 128, height, 128)
    return cut.transpose(0, 2, 1, 3).reshape(rows, columns).astype(f32)


def pair_sum(halves):
    core = lax.axis_index("core")
    mine = lax.dynamic_index_in_dim(halves, core, 0, keepdims=False)
    theirs = lax.dynamic_index_in_dim(halves, 1 - core, 0, keepdims=False)
    return (mine.astype(f32) + swap_cores(theirs).astype(f32)).astype(bf16)


def all_sums(early, expand, depth):
    depth = jnp.pad(depth[:9].astype(bf16).reshape(9, 8, 128), ((0, 23), (0, 0), (0, 0)))
    core = lax.axis_index("core")

    def share(of):
        own = lax.dynamic_index_in_dim(expand, of, 0, keepdims=False)
        return jnp.concatenate([own, jnp.where(of == 0, depth, jnp.zeros((), bf16))], axis=1)

    late = (share(core).astype(f32) + swap_cores(share(1 - core)).astype(f32)).astype(bf16)
    pair = jnp.concatenate([early, late], axis=1)
    line = jnp.sum(exchange(pair, "x").reshape(4, 8, 184, 128).astype(f32), axis=0).astype(bf16)
    sheet = jnp.sum(exchange(line, "z").astype(f32), axis=0).astype(bf16)
    column = jnp.concatenate(
        [sheet[:128].reshape(4, 32, 128), jnp.broadcast_to(sheet[None, 128:], (4, 56, 128))], axis=1
    )
    column = jnp.broadcast_to(column[:, None], (4, 2, 88, 128)).reshape(8, 88, 128)
    grad_scale = 1.0 / math.sqrt(8 * 96 * 96)
    total = jnp.sum(exchange(column, RING).astype(f32), axis=0) * grad_scale
    near = spread(total.astype(bf16), ("x", "z"), 32)
    own = near[:, 32:]
    other = swap_cores(own)
    matrix = near[:, :32].reshape(64, 16, 128)
    grad_proj = untiled(matrix[:32], 128, 512)
    grad_qkv = untiled(matrix[32:56], 64, 768)
    grad_out = untiled(matrix[56:], 32, 512)
    first = lax.axis_index("core") == 0
    both = jnp.where(first, jnp.stack([own, other]), jnp.stack([other, own]))

    def joined(start, count):
        part = both[:, :, start : start + 8 * count].reshape(2, 32, count, 8, 128)
        return part.transpose(1, 3, 0, 2, 4).reshape(256, 256 * count).astype(f32)

    grad_short = joined(0, 2)
    grad_expand = joined(16, 4)
    grad_depth = both[0, :9, 48:].reshape(3, 3, 1024).astype(f32)
    return grad_expand, grad_depth, grad_short, grad_proj, grad_qkv, grad_out


def slots16(cells):
    return jnp.pad(cells, ((0, 0), (0, 4), (0, 0)))


def on_device(images, w_expand, w_depth, w_short, w_proj, w_qkv, w_out, cotangent):
    images = images[0]
    cotangent = slots16(cotangent[0])
    top, left, ring, other = first_transfers(images, w_proj, w_qkv, w_out)
    slots = slot_order()
    taps = w_depth.reshape(9, 1024)
    even, odd, slopes, activated, conv_slope, cells, pooled = expand_step(
        images, top, left, w_expand, taps
    )
    cotangent = cotangent.reshape(192, 512)
    spot = jnp.stack([lax.axis_index("core"), lax.axis_index("ylo")]).astype(jnp.int32)
    pieces, section_out, normed, proj, qkv = section_step(
        spot, ring, other, activated, pooled, w_short, cotangent, slots
    )
    got = exchange(pieces.reshape(64, 9, 2, 128), GRID_AXES)
    mixed = attention(got.reshape(8, 144, 128))
    got = exchange(mixed.reshape(64, 9, 2, 128), GRID_AXES).reshape(HEADS, 144, 128)
    results, d_section, d_conv = back_step(
        got, slots, section_out, cotangent, proj, qkv, conv_slope
    )
    below = row_rim(d_conv[:12].reshape(1, 12, 1024), -1)
    edge = d_conv.reshape(12, 16, 1024)[:, :1]
    right = jnp.concatenate([col_rim(edge, -1), diagonal_rim(edge[:1], -1)], axis=0)
    early, d_pooled = parts_step(
        results, d_section, normed, cotangent, activated, pooled, w_short
    )
    early = pair_sum(early)
    image, expand, depth = pixel_step(
        d_conv, slots16(below), right, even, odd, slopes, cells, w_expand, taps,
        d_pooled,
    )
    image = image.reshape(2, 2, 12, 16, 256)[:, :, :, :12]
    grad_image = image.transpose(2, 0, 3, 1, 4).reshape(1, 24, 24, 256)
    return (grad_image,) + all_sums(early, expand, depth)


def solution(mesh):
    fine = Mesh(mesh.devices.reshape(4, 2, 2, 4, 8), ("ylo", "core", "yhi", "x", "z"))
    cells = P(SAMPLE, ROW, COL, None)
    rows = P(SAMPLE, None)
    return jax.shard_map(
        on_device,
        mesh=fine,
        in_specs=(cells, P(), P(), P(), rows, rows, rows, cells),
        out_specs=(cells, P(), P(), P(), rows, rows, rows),
        check_vma=False,
    )
```
